32 devices in a mesh: comp: 4 (over y, core), space: 8 (over z, x).
Axes of the slice: x: 2, y: 2, z: 4, core: 2. Of those that a mesh axis runs over, the one named last changes fastest.
Arguments:
- adjoint_forcing: float32 [384, 256, 1024], P('comp', 'space'), may hold values from -6 to 6
- forward_state: bfloat16 [384, 256, 1024], P(None, ('space', 'comp')), may hold values from -6 to 6
- wind_speed: float32 [256, 1024], P(('space', 'comp')), may hold values from 0.5 to 2
- cg_index: int32 [16, 256, 1024], P('comp', 'space'), may hold values from 0 to 7
- turn_index: int32 [16, 256, 1024], P('comp', 'space'), may hold values from 0 to 7
- sea_mask: int32 [256, 1024], P('space'), may hold values 0 or 1
- dir_sign: int32 [2, 24], replicated, may hold values from -1 to 1, as said below
- w_in: bfloat16 [1536, 384], replicated, may hold values from -0.3125 to 0.3125
- w_out: bfloat16 [384, 1536], replicated, may hold values from -0.15625 to 0.15625
- wind_weight: float32 [1536], replicated, may hold values from -6 to 6
Outputs:
- adjoint_start: float32 [384, 256, 1024], P('comp', 'space')
- wind_gradient: float32 [256, 1024], P(('space', 'comp'))
The draws below stay inside these ranges and needn't reach their ends.
Inputs may be any that keep to these rules, and one draw needn't show every extreme that they name: `dir_sign`: every entry is -1 or 1.
All inputs are finite; a program needn't handle non-finite values. No bound on the sum of `sea_mask` on one device may be relied on, other than what follows from the above.
Results may differ from the reference program's by a relative error of at most 0.0035.
Values may be sent and summed in bfloat16 or wider, within the bound.
No kernel may reach another device: no remote copies, remote signals or barrier semaphores. Data moves between devices by JAX's collectives and lax.ppermute only.
A program may use at most 192 MiB of HBM per device.

```python
import math
import jax
import jax.numpy as jnp
from jax import lax

DIRS = 24
FREQ = 16
HID = 1536
STEPS = 2
NLON = 1024
COMPONENTS = 384
NLAT = 256


def draw_dir_sign(key, part):
    key = jax.random.fold_in(key, 11)
    flips = jax.random.randint(key, (2, DIRS), 0, 2)
    return (flips * 2 - 1).astype(jnp.int32)


def set_ends(drawn, own_key, least, top_value):
    spot = [jax.random.randint(jax.random.fold_in(own_key, axis), (), 0, length) for axis, length in enumerate(drawn.shape)]
    main_axis = drawn.shape.index(max(drawn.shape))
    next_to = spot[:main_axis] + [(spot[main_axis] + 1) % drawn.shape[main_axis]] + spot[main_axis + 1:]
    return drawn.at[tuple(spot)].set(least).at[tuple(next_to)].set(top_value)


def block_scale(key, extent, shards, smallest, high):
    factor_of = 1.0
    for position, shards_of in shards:
        steps = jax.random.uniform(jax.random.fold_in(jax.random.fold_in(key, 6), position), (shards_of,), jnp.float32, smallest / len(shards), high / len(shards))
        factor_of = factor_of * jnp.repeat(jnp.exp(steps), extent[position] // shards_of).reshape((-1,) + (1,) * (len(extent) - 1 - position))
    return factor_of


def normal_values(own_key, extent, scale, most, split=(), kind=jnp.bfloat16):
    entries = scale * jax.random.normal(own_key, extent, jnp.float32)
    if split:
        entries = entries * block_scale(own_key, extent, split, -0.22, 0.18)
    return jnp.clip(entries, -most, most).astype(kind)


def setup_inputs(seed: int = 0) -> dict:
    keys = jax.random.split(jax.random.key(seed), 11)
    return {
        "adjoint_forcing": normal_values(keys[0], (COMPONENTS, NLAT, NLON), 1.0, 6.0, ((0, 4), (1, 8)), jnp.float32),
        "forward_state": normal_values(keys[1], (COMPONENTS, NLAT, NLON), 1.0, 6.0, ((1, 32),)),
        "wind_speed": jnp.clip(0.5 + 1.5 * jax.random.uniform(keys[2], (NLAT, NLON), jnp.float32) ** block_scale(keys[2], (NLAT, NLON), ((0, 32),), -0.2, 0.2), 0.5, 2.0),
        "cg_index": set_ends(jax.random.randint(keys[3], (FREQ, NLAT, NLON), 0, 8), jax.random.fold_in(keys[3], 1), 0, 7).astype(jnp.int32),
        "turn_index": set_ends(jax.random.randint(keys[4], (FREQ, NLAT, NLON), 0, 8), jax.random.fold_in(keys[4], 1), 0, 7).astype(jnp.int32),
        "sea_mask": set_ends((jax.random.randint(keys[5], (NLAT, NLON), 0, 8) < 7).astype(jnp.int32), jax.random.fold_in(keys[5], 1), 0, 1),
        "dir_sign": draw_dir_sign(jax.random.fold_in(keys[10], 71), 0),
        "w_in": normal_values(keys[7], (HID, COMPONENTS), COMPONENTS ** -0.5, 0.3125),
        "w_out": normal_values(keys[8], (COMPONENTS, HID), HID ** -0.5, 0.15625),
        "wind_weight": normal_values(keys[9], (HID,), 1.0, 6.0, (), jnp.float32),
    }


def direction_factors(dirs):
    angle = (jnp.arange(dirs, dtype=jnp.float32) + 0.5) * (2.0 * math.pi / dirs)
    return 0.5 * jnp.abs(jnp.cos(angle)), 0.5 * jnp.abs(jnp.sin(angle))


def adjoint_step(costate, celerity, turning, turn_up, sea_land, sign_x, sign_y, along_x, along_y):
    cour_x = along_x * celerity
    cour_y = along_y * celerity
    masked = costate * sea_land
    retained = (1.0 - cour_x - cour_y - turning) * masked
    flux_x = cour_x * masked
    flux_y = cour_y * masked
    flux_t = turning * masked
    zero_col = jnp.zeros_like(flux_x[..., :1])
    from_right = jnp.concatenate([flux_x[..., 1:], zero_col], axis=-1)
    from_left = jnp.concatenate([zero_col, flux_x[..., :-1]], axis=-1)
    term_x = jnp.where(sign_x > 0, from_right, from_left)
    padded = jnp.pad(flux_y, ((0, 0), (1, 1), (0, 0)))
    term_y = jnp.where(sign_y > 0, padded[:, 2:, :], padded[:, :-2, :])
    term_t = jnp.where(turn_up, jnp.roll(flux_t, -1, axis=-3), jnp.roll(flux_t, 1, axis=-3))
    return retained + term_x + term_y + term_t


def source_adjoint(cell_half, cell_state, cell_wind, w_in, w_out, wind_weight):
    pulled = jnp.dot(w_out.T, cell_half, preferred_element_type=jnp.float32)
    forward = jnp.dot(w_in, cell_state, preferred_element_type=jnp.float32) + wind_weight[:, None] * cell_wind[None, :]
    squash = jnp.tanh(forward)
    weighted = (1.0 - squash * squash) * pulled
    increment = jnp.dot(w_in.T, weighted.astype(jnp.bfloat16), preferred_element_type=jnp.float32).astype(jnp.bfloat16)
    wind_grad = jnp.sum(wind_weight[:, None] * weighted, axis=0)
    return increment, wind_grad


def reference(adjoint_forcing, forward_state, wind_speed, cg_index, turn_index, sea_mask, dir_sign, w_in, w_out, wind_weight):
    along_x, along_y = direction_factors(DIRS)
    along_x = along_x.reshape(DIRS, 1, 1)
    along_y = along_y.reshape(DIRS, 1, 1)
    sign_x = dir_sign[0].reshape(DIRS, 1, 1)
    sign_y = dir_sign[1].reshape(DIRS, 1, 1)
    sea_land = sea_mask.astype(jnp.float32)

    def propagate(pieces):
        costate, grid_index, turn_grid = pieces
        celerity = (0.1 + 0.8 * grid_index.astype(jnp.float32) / 7.0)[None]
        turning = (0.3 * jnp.abs(turn_grid.astype(jnp.float32) - 3.5) / 3.5)[None]
        turn_up = (turn_grid >= 4)[None]
        for sweep in range(STEPS):
            costate = adjoint_step(costate, celerity, turning, turn_up, sea_land, sign_x, sign_y, along_x, along_y)
        return costate

    costate = lax.map(propagate, (adjoint_forcing.reshape(FREQ, DIRS, NLAT, NLON), cg_index, turn_index))
    costate = costate.reshape(COMPONENTS, NLAT, NLON)
    cell_costate = jnp.moveaxis(costate, 1, 0)
    cell_state = jnp.moveaxis(forward_state, 1, 0)

    def source_row(pieces):
        row_costate, row_state, row_wind = pieces
        increment, wind_grad = source_adjoint(row_costate.astype(jnp.bfloat16), row_state, row_wind, w_in, w_out, wind_weight)
        return row_costate + increment.astype(jnp.float32), wind_grad

    start_rows, wind_gradient = lax.map(source_row, (cell_costate, cell_state, wind_speed))
    return jnp.moveaxis(start_rows, 0, 1), wind_gradient
```

```python
import math

import jax
import jax.numpy as jnp
from jax import lax
from jax.sharding import PartitionSpec as P

STEPS = 2


def extended(block, sides, width):
    for axis, dim in sides:
        count = lax.axis_size(axis)
        forward = [(i, i + 1) for i in range(count - 1)]
        backward = [(target, source) for source, target in forward]
        low = lax.ppermute(
            lax.slice_in_dim(block, block.shape[dim] - width, None, axis=dim), axis, forward
        )
        high = lax.ppermute(lax.slice_in_dim(block, 0, width, axis=dim), axis, backward)
        block = jnp.concatenate([low, block, high], axis=dim)
    return block


def direction_factors(dirs):
    angle = (jnp.arange(dirs, dtype=jnp.float32) + 0.5) * (2.0 * math.pi / dirs)
    return (0.5 * jnp.abs(jnp.cos(angle)), 0.5 * jnp.abs(jnp.sin(angle)))


def adjoint_step(costate, celerity, turning, turn_up, sea_land, sign_x, sign_y, along_x, along_y):
    cour_x = along_x * celerity
    cour_y = along_y * celerity
    masked = costate * sea_land
    retained = (1.0 - cour_x - cour_y - turning) * masked
    flux_x = cour_x * masked
    flux_y = cour_y * masked
    flux_t = turning * masked
    zero_col = jnp.zeros_like(flux_x[..., :1])
    from_right = jnp.concatenate([flux_x[..., 1:], zero_col], axis=-1)
    from_left = jnp.concatenate([zero_col, flux_x[..., :-1]], axis=-1)
    term_x = jnp.where(sign_x > 0, from_right, from_left)
    padded = extended(flux_y, (("space", 2),), 1)
    term_y = jnp.where(sign_y > 0, padded[:, :, 2:, :], padded[:, :, :-2, :])
    term_t = jnp.where(turn_up, jnp.roll(flux_t, -1, axis=-3), jnp.roll(flux_t, 1, axis=-3))
    return retained + term_x + term_y + term_t


def source_adjoint(cell_half, cell_state, cell_wind, w_in, w_out, wind_weight):
    pulled = lax.dot_general(
        w_out, cell_half, (((0,), (0,)), ((), ())), preferred_element_type=jnp.float32
    )
    forward = (
        jnp.dot(w_in, cell_state, preferred_element_type=jnp.float32)
        + wind_weight[:, None] * cell_wind[None, :]
    )
    squash = jnp.tanh(forward)
    weighted = (1.0 - squash * squash) * pulled
    increment = lax.dot_general(
        w_in,
        weighted.astype(jnp.bfloat16),
        (((0,), (0,)), ((), ())),
        preferred_element_type=jnp.float32,
    ).astype(jnp.bfloat16)
    wind_grad = jnp.sum(wind_weight[:, None] * weighted, axis=0)
    return (increment, wind_grad)


def shards(
    adjoint_forcing,
    forward_state,
    wind_speed,
    cg_index,
    turn_index,
    sea_mask,
    dir_sign,
    w_in,
    w_out,
    wind_weight,
):
    dirs = dir_sign.shape[1]
    comps, rows, cols = adjoint_forcing.shape
    freqs = comps // dirs
    total_comps = w_in.shape[1]
    along_x, along_y = direction_factors(dirs)
    along_x = along_x.reshape(1, dirs, 1, 1)
    along_y = along_y.reshape(1, dirs, 1, 1)
    sign_x = dir_sign[0].reshape(1, dirs, 1, 1)
    sign_y = dir_sign[1].reshape(1, dirs, 1, 1)
    sea_land = sea_mask.astype(jnp.float32)
    celerity = (0.1 + 0.8 * cg_index.astype(jnp.float32) / 7.0)[:, None]
    turning = (0.3 * jnp.abs(turn_index.astype(jnp.float32) - 3.5) / 3.5)[:, None]
    turn_up = (turn_index >= 4)[:, None]
    costate = adjoint_forcing.reshape(freqs, dirs, rows, cols)
    for sweep in range(STEPS):
        costate = adjoint_step(
            costate, celerity, turning, turn_up, sea_land, sign_x, sign_y, along_x, along_y
        )
    costate = costate.reshape(comps, rows, cols)
    parts = lax.axis_size("comp")
    local = rows // parts
    chunks = 2
    width = cols // chunks
    starts, grads = [], []
    for c in range(chunks):
        here = slice(c * width, (c + 1) * width)
        home = costate[:, :, here]
        half = home.astype(jnp.bfloat16).reshape(comps, parts, local, width)
        half = jnp.transpose(half, (1, 2, 0, 3))
        got = lax.all_to_all(half, "comp", split_axis=0, concat_axis=0, tiled=True)
        cell = jnp.transpose(got, (0, 2, 1, 3)).reshape(total_comps, local * width)
        increment, wind_grad = source_adjoint(
            cell,
            forward_state[:, :, here].reshape(total_comps, -1),
            wind_speed[:, here].reshape(-1),
            w_in,
            w_out,
            wind_weight,
        )
        back = increment.reshape(parts, comps, local, width)
        back = jnp.transpose(back, (0, 2, 1, 3))
        back = lax.all_to_all(back, "comp", split_axis=0, concat_axis=0, tiled=True)
        back = jnp.transpose(back, (2, 0, 1, 3)).reshape(comps, rows, width)
        starts.append(home + back.astype(jnp.float32))
        grads.append(wind_grad.reshape(local, width))
    return (jnp.concatenate(starts, axis=-1), jnp.concatenate(grads, axis=-1))


def solution(mesh):
    placed = (
        P("comp", "space", None),
        P(None, ("space", "comp"), None),
        P(("space", "comp"), None),
        P("comp", "space", None),
        P("comp", "space", None),
        P("space", None),
        P(),
        P(),
        P(),
        P(),
    )
    return jax.shard_map(
        shards,
        mesh=mesh,
        in_specs=placed,
        out_specs=(P("comp", "space", None), P(("space", "comp"), None)),
        check_vma=False,
    )
```

```python
import functools
import math

import jax
import jax.numpy as jnp
from jax import lax
from jax.experimental import pallas as pl
from jax.experimental.pallas import tpu as pltpu
from jax.sharding import PartitionSpec as P

HALO = 2
TILE = 8
LANES = 128
MIB = 1 << 20
VMEM_LIMIT = 56 * MIB


def direction_factors(dirs):
    angle = (jnp.arange(dirs, dtype=jnp.float32) + 0.5) * (2.0 * math.pi / dirs)
    return (0.5 * jnp.abs(jnp.cos(angle)), 0.5 * jnp.abs(jnp.sin(angle)))


def chunk_row(owner, j, half, late):
    return jnp.where((owner == 0) != late, half + j, j)


UNREAD = pl.BlockSpec(memory_space=pl.ANY)


def lane_tiles(cols):
    return [pl.ds(c * LANES, LANES) for c in range(cols // LANES)]


def propagate_kernel(parts, local, chunks, window, keep, *refs):
    refs = list(refs)
    own_ref, sign_ref, along_ref, _, forcing_ref, cg_ref, turn_ref, mask_ref = refs[:8]
    refs = refs[8:]
    wcg_ref = wturn_ref = wmask_ref = None
    if window:
        above_ref, below_ref, wcg_ref, wturn_ref, wmask_ref = refs[:5]
        refs = refs[5:]
    if keep:
        home_ref = refs.pop(0)
    sends = parts * len(chunks)
    send_refs = refs[:sends]
    cel_ref, base_ref, trn_ref, first_ref, swap_ref = refs[sends : sends + 5]
    dirs, rows, cols = forcing_ref.shape[1:]
    pitch = dirs + 1
    tiles = rows // TILE
    count = tiles + (1 if window else 0)
    lanes = lane_tiles(cols)

    def span(t):
        return pl.ds(t * TILE, TILE)

    def level(main, side, t, *lead):
        return main[(*lead, span(t), slice(None))] if t < tiles else side[(*lead, slice(None), slice(None))]

    for t in range(count):
        sea = level(mask_ref, wmask_ref, t).astype(jnp.float32)
        celerity = 0.1 + 0.8 * level(cg_ref, wcg_ref, t, 0).astype(jnp.float32) / 7.0
        turning = 0.3 * jnp.abs(level(turn_ref, wturn_ref, t, 0).astype(jnp.float32) - 3.5) / 3.5
        cel_ref[span(t), :] = celerity * sea
        base_ref[span(t), :] = (1.0 - turning) * sea
        trn_ref[span(t), :] = turning * sea

    if window:
        side_ref, edge_ref = refs[sends + 5 :]
        edge_ref[...] = jnp.zeros_like(edge_ref)
        for r in range(HALO):
            for c, here in enumerate(lanes):
                edge_ref[c, pl.ds(r * pitch, dirs), :] = above_ref[r, 0, :, here].astype(jnp.float32)
                low = (TILE - HALO + r) * pitch
                edge_ref[c, pl.ds(low, dirs), :] = below_ref[r, 0, :, here].astype(jnp.float32)

        def gather(d, carry):
            for c, here in enumerate(lanes):
                side_ref[d, :, here] = edge_ref[c, pl.ds(d, TILE, stride=pitch), :]
            return carry

        lax.fori_loop(0, dirs, gather, 0)

    row = lax.broadcasted_iota(jnp.int32, (TILE, LANES), 0)
    lane = lax.broadcasted_iota(jnp.int32, (TILE, LANES), 1)
    nothing = jnp.zeros((TILE, LANES), jnp.float32)

    def sweep(load, store, final):
        def one(d, carry):
            following = jnp.where(d == dirs - 1, 0, d + 1)
            previous = jnp.where(d == 0, dirs - 1, d - 1)
            ax = along_ref[0, d]
            ay = along_ref[1, d]
            both = ax + ay
            right = sign_ref[0, d] > 0
            high = sign_ref[1, d] > 0
            shift_x = jnp.where(right, LANES - 1, 1)
            shift_y = jnp.where(high, TILE - 1, 1)
            at_right = lane == jnp.where(right, LANES - 1, LANES)
            at_left = lane == jnp.where(right, LANES, 0)
            at_high = row == jnp.where(high, TILE - 1, TILE)
            at_low = row == jnp.where(high, TILE, 0)

            def column(c):
                here = [load(t, d, lanes[c]) for t in range(count)]
                flow = [cel_ref[span(t), lanes[c]] * here[t] for t in range(count)]
                return here, flow, [pltpu.roll(f, shift_x, 1) for f in flow]

            before = [nothing] * count
            here, flow, moved = column(0)
            for c in range(len(lanes)):
                beyond = [nothing] * count
                if c + 1 < len(lanes):
                    later = column(c + 1)
                    beyond = later[2]
                lifted = [pltpu.roll(f, shift_y, 0) for f in flow]
                side = None
                for t in reversed(range(count)):
                    above = lifted[t + 1] if t + 1 < tiles else nothing
                    below = lifted[t - 1] if 0 < t < tiles else nothing
                    flow_x = jnp.where(at_right, beyond[t], jnp.where(at_left, before[t], moved[t]))
                    flow_y = jnp.where(at_high, above, jnp.where(at_low, below, lifted[t]))
                    up = level(turn_ref, wturn_ref, t, 0)[:, c * LANES : (c + 1) * LANES] >= 4
                    turned = jnp.where(up, load(t, following, lanes[c]), load(t, previous, lanes[c]))
                    total = (base_ref[span(t), lanes[c]] - both * cel_ref[span(t), lanes[c]]) * here[t]
                    total = total + ax * flow_x + ay * flow_y + trn_ref[span(t), lanes[c]] * turned
                    if final and window:
                        if t == tiles:
                            side = total
                            continue
                        if t == 0:
                            total = total + jnp.where(row < HALO, pltpu.roll(side, TILE - HALO, 0), 0.0)
                        if t == tiles - 1:
                            total = total + jnp.where(row >= TILE - HALO, pltpu.roll(side, HALO, 0), 0.0)
                    store(t, d, c, total)
                if c + 1 < len(lanes):
                    before = moved
                    here, flow, moved = later
            return carry

        lax.fori_loop(0, dirs, one, 0, unroll=2)

    def load_input(t, d, lanes_here):
        return forcing_ref[0, d, span(t), lanes_here] if t < tiles else side_ref[d, :, lanes_here]

    def load_first(t, d, lanes_here):
        return first_ref[d, span(t), lanes_here]

    def store_first(t, d, c, value):
        first_ref[d, span(t), lanes[c]] = value

    def store_last(t, d, c, value):
        if keep:
            home_ref[0, d, span(t), lanes[c]] = value
        swap_ref[c, pl.ds(t * TILE * pitch + d, TILE, stride=pitch), :] = value

    sweep(load_input, store_first, False)
    sweep(load_first, store_last, True)

    own = own_ref[0]
    half = local // 2
    for i, late in enumerate(chunks):
        for k in range(parts):
            owner = own ^ k
            for j in range(half):
                start = (owner * local + chunk_row(owner, j, half, late)) * pitch
                for c, here in enumerate(lanes):
                    piece = swap_ref[c, pl.ds(start, dirs), :]
                    send_refs[i * parts + k][j, 0, :, here] = piece.astype(jnp.bfloat16)


def propagate(own, signs, along, after, forcing, cg, turn, mask, side, parts, chunks, keep, group):
    freqs, dirs, rows, cols = forcing.shape
    begin, many = group
    local = rows // parts
    half = local // 2
    window = side is not None
    smem = pl.BlockSpec(memory_space=pltpu.SMEM)
    levels = pl.BlockSpec((1, rows, cols), lambda f: (begin + f, 0, 0))
    block = pl.BlockSpec((1, dirs, rows, cols), lambda f: (begin + f, 0, 0, 0))
    in_specs = [smem, smem, smem, UNREAD, block, levels, levels, pl.BlockSpec((rows, cols), lambda f: (0, 0))]
    args = [own, signs, along, after, forcing, cg, turn, mask]
    if window:
        edge = pl.BlockSpec((HALO, 1, dirs, cols), lambda f: (0, begin + f, 0, 0))
        near = pl.BlockSpec((1, TILE, cols), lambda f: (begin + f, 0, 0))
        in_specs += [edge, edge, near, near, pl.BlockSpec((TILE, cols), lambda f: (0, 0))]
        args += list(side)
    out_specs, out_shape = [], []
    if keep:
        out_specs.append(pl.BlockSpec((1, dirs, rows, cols), lambda f: (f, 0, 0, 0)))
        out_shape.append(jax.ShapeDtypeStruct((many, dirs, rows, cols), jnp.float32))
    for _ in range(parts * len(chunks)):
        out_specs.append(pl.BlockSpec((half, 1, dirs, cols), lambda f: (0, f, 0, 0)))
        out_shape.append(jax.ShapeDtypeStruct((half, many, dirs, cols), jnp.bfloat16))
    deep = rows + (TILE if window else 0)
    coefs = pltpu.VMEM((deep, cols), jnp.float32)
    scratch = [
        coefs,
        coefs,
        coefs,
        pltpu.VMEM((dirs, deep, cols), jnp.float32),
        pltpu.VMEM((cols // LANES, rows * (dirs + 1), LANES), jnp.float32),
    ]
    if window:
        scratch.append(pltpu.VMEM((dirs, TILE, cols), jnp.float32))
        scratch.append(pltpu.VMEM((cols // LANES, TILE * (dirs + 1), LANES), jnp.float32))
    size = many * dirs * rows * cols
    outs = pl.pallas_call(
        functools.partial(propagate_kernel, parts, local, chunks, window, keep),
        grid=(many,),
        in_specs=in_specs,
        out_specs=out_specs,
        out_shape=out_shape,
        scratch_shapes=scratch,
        compiler_params=pltpu.CompilerParams(vmem_limit_bytes=VMEM_LIMIT),
        cost_estimate=pl.CostEstimate(flops=40 * size, bytes_accessed=(8 if keep else 4) * size, transcendentals=0),
    )(*args)
    outs = list(outs)
    home = outs.pop(0) if keep else None
    return home, [outs[i * parts : (i + 1) * parts] for i in range(len(chunks))]


def edges_kernel(_, top_ref, bottom_ref, first_ref, last_ref, swap_ref):
    dirs, _, cols = top_ref.shape[1:]
    pitch = dirs + 1
    lanes = lane_tiles(cols)

    for ref, out_ref, low in ((top_ref, first_ref, 0), (bottom_ref, last_ref, TILE - HALO)):

        def body(d, carry, ref=ref):
            for c, here in enumerate(lanes):
                swap_ref[c, pl.ds(d, TILE, stride=pitch), :] = ref[0, d, :, here]
            return carry

        lax.fori_loop(0, dirs, body, 0, unroll=2)
        for r in range(HALO):
            for c, here in enumerate(lanes):
                out_ref[r, 0, :, here] = swap_ref[c, pl.ds((low + r) * pitch, dirs), :].astype(jnp.bfloat16)


def edges(after, forcing):
    freqs, dirs, rows, cols = forcing.shape
    out = pl.BlockSpec((HALO, 1, dirs, cols), lambda f: (0, f, 0, 0))
    shape = jax.ShapeDtypeStruct((HALO, freqs, dirs, cols), jnp.bfloat16)
    return pl.pallas_call(
        edges_kernel,
        grid=(freqs,),
        in_specs=[
            UNREAD,
            pl.BlockSpec((1, dirs, TILE, cols), lambda f: (f, 0, 0, 0)),
            pl.BlockSpec((1, dirs, TILE, cols), lambda f: (f, 0, rows // TILE - 1, 0)),
        ],
        out_specs=[out, out],
        out_shape=[shape, shape],
        scratch_shapes=[pltpu.VMEM((cols // LANES, TILE * (dirs + 1), LANES), jnp.float32)],
        compiler_params=pltpu.CompilerParams(vmem_limit_bytes=VMEM_LIMIT),
        cost_estimate=pl.CostEstimate(
            flops=freqs * dirs * TILE * cols, bytes_accessed=8 * freqs * dirs * TILE * cols, transcendentals=0
        ),
    )(after, forcing, forcing)


def by_row_kernel(_, state_ref, out_ref, swap_ref):
    deep, local, _ = state_ref.shape
    pitch = deep + 1

    def body(d, carry):
        swap_ref[pl.ds(d, local, stride=pitch), :] = state_ref[d].astype(jnp.float32)
        return carry

    lax.fori_loop(0, deep, body, 0, unroll=8)
    for r in range(local):
        out_ref[r] = swap_ref[pl.ds(r * pitch, deep), :].astype(jnp.bfloat16)


def by_row(after, state):
    deep, local, cols = state.shape
    return pl.pallas_call(
        by_row_kernel,
        grid=(cols // LANES,),
        in_specs=[UNREAD, pl.BlockSpec((deep, local, LANES), lambda c: (0, 0, c))],
        out_specs=pl.BlockSpec((local, deep, LANES), lambda c: (0, 0, c)),
        out_shape=jax.ShapeDtypeStruct((local, deep, cols), jnp.bfloat16),
        scratch_shapes=[pltpu.VMEM((local * (deep + 1), LANES), jnp.float32)],
        compiler_params=pltpu.CompilerParams(vmem_limit_bytes=VMEM_LIMIT),
        cost_estimate=pl.CostEstimate(flops=4 * state.size, bytes_accessed=4 * state.size, transcendentals=0),
    )(after, state)


def turned_kernel(_, w_in_ref, w_out_ref, in_t_ref, out_t_ref):
    in_t_ref[...] = w_in_ref[...].T
    out_t_ref[...] = w_out_ref[...].T


def turned(after, w_in, w_out):
    hidden, total = w_in.shape
    step = 512
    tall = pl.BlockSpec((step, total), lambda h: (h, 0))
    wide = pl.BlockSpec((total, step), lambda h: (0, h))
    return pl.pallas_call(
        turned_kernel,
        grid=(hidden // step,),
        in_specs=[UNREAD, tall, wide],
        out_specs=[wide, tall],
        out_shape=[jax.ShapeDtypeStruct((total, hidden), w_in.dtype), jax.ShapeDtypeStruct((hidden, total), w_in.dtype)],
        compiler_params=pltpu.CompilerParams(vmem_limit_bytes=VMEM_LIMIT),
        cost_estimate=pl.CostEstimate(flops=4 * w_in.size, bytes_accessed=8 * w_in.size, transcendentals=0),
    )(after, w_in, w_out)


def source_kernel(parts, groups, step, own_ref, _, state_ref, wind_ref, w_in_ref, out_t_ref, in_t_ref, weight_ref, *refs):
    pieces = parts * groups
    cell_refs = refs[:pieces]
    grad_ref = refs[pieces]
    back_refs = refs[pieces + 1 : 2 * pieces + 1]
    cell_ref, weighted_ref, grown_ref = refs[2 * pieces + 1 :]
    many, dirs, width = cell_refs[0].shape[1:]
    comps = many * dirs
    hidden = w_in_ref.shape[0]
    own = own_ref[0]

    def place(k, g):
        return pl.ds(pl.multiple_of(((own ^ k) * groups + g) * comps, TILE), comps)

    for k in range(parts):
        for g in range(groups):
            cell_ref[place(k, g), :] = cell_refs[g * parts + k][0].astype(jnp.float32).reshape(comps, width)
    cell = cell_ref[...].astype(jnp.bfloat16)
    state = state_ref[0]
    wind = wind_ref[0]
    grad = jnp.zeros((TILE, width), jnp.float32)
    for h in range(0, hidden, step):
        some = pl.ds(h, step)
        weight = weight_ref[some, :]
        forward = jnp.dot(w_in_ref[some, :], state, preferred_element_type=jnp.float32) + weight * wind
        squash = jnp.tanh(forward)
        pulled = jnp.dot(out_t_ref[some, :], cell, preferred_element_type=jnp.float32)
        weighted = (1.0 - squash * squash) * pulled
        weighted_ref[some, :] = weighted.astype(jnp.bfloat16)
        grad = grad + jnp.sum((weight * weighted).reshape(step // TILE, TILE, width), axis=0)
    grad_ref[0] = jnp.sum(grad, axis=0, keepdims=True)
    grown_ref[...] = jnp.dot(in_t_ref[...], weighted_ref[...], preferred_element_type=jnp.float32)
    for k in range(parts):
        for g in range(groups):
            back_refs[g * parts + k][0] = grown_ref[place(k, g), :].reshape(many, dirs, width).astype(jnp.bfloat16)


def source_term(own, after, state, wind, w_in, out_t, in_t, weight, cells, late):
    groups, parts = len(cells), len(cells[0])
    half, many, dirs, cols = cells[0][0].shape
    hidden, total = w_in.shape
    width = min(cols, 512)

    def row_of(j, own_ref):
        return chunk_row(own_ref[0], j, half, late)

    def whole(shape):
        return pl.BlockSpec(shape, lambda j, c, own_ref: (0, 0))

    piece = pl.BlockSpec((1, many, dirs, width), lambda j, c, own_ref: (j, 0, 0, c))
    line = pl.BlockSpec((1, 1, width), lambda j, c, own_ref: (j, 0, c))
    pieces = groups * parts
    outs = pl.pallas_call(
        functools.partial(source_kernel, parts, groups, 256),
        grid_spec=pltpu.PrefetchScalarGridSpec(
            num_scalar_prefetch=1,
            grid=(half, cols // width),
            in_specs=[
                UNREAD,
                pl.BlockSpec((1, total, width), lambda j, c, own_ref: (row_of(j, own_ref), 0, c)),
                pl.BlockSpec((1, 1, width), lambda j, c, own_ref: (row_of(j, own_ref), 0, c)),
                whole((hidden, total)),
                whole((hidden, total)),
                whole((total, hidden)),
                whole((hidden, 1)),
            ]
            + [piece] * pieces,
            out_specs=[line] + [piece] * pieces,
            scratch_shapes=[
                pltpu.VMEM((total, width), jnp.float32),
                pltpu.VMEM((hidden, width), jnp.bfloat16),
                pltpu.VMEM((total, width), jnp.float32),
            ],
        ),
        out_shape=[jax.ShapeDtypeStruct((half, 1, cols), jnp.float32)]
        + [jax.ShapeDtypeStruct(cells[0][0].shape, jnp.bfloat16)] * pieces,
        compiler_params=pltpu.CompilerParams(vmem_limit_bytes=VMEM_LIMIT),
        cost_estimate=pl.CostEstimate(
            flops=6 * half * cols * hidden * total,
            bytes_accessed=6 * half * cols * total,
            transcendentals=half * cols * hidden,
        ),
    )(own, after, state, wind, w_in, out_t, in_t, weight, *[cell for group in cells for cell in group])
    return outs[0].reshape(half, cols), [outs[1 + g * parts : 1 + (g + 1) * parts] for g in range(groups)]


def join_kernel(parts, own_ref, _, home_ref, *refs):
    back_refs = refs[: 2 * parts]
    out_ref, swap_ref = refs[2 * parts :]
    dirs, rows, cols = home_ref.shape[1:]
    pitch = dirs + 1
    local = rows // parts
    half = local // 2
    own = own_ref[0]
    lanes = lane_tiles(cols)
    for late in (False, True):
        for k in range(parts):
            owner = own ^ k
            for j in range(half):
                start = (owner * local + chunk_row(owner, j, half, late)) * pitch
                for c, here in enumerate(lanes):
                    piece = back_refs[late * parts + k][j, 0, :, here]
                    swap_ref[c, pl.ds(start, dirs), :] = piece.astype(jnp.float32)

    def body(d, carry):
        for t in range(rows // TILE):
            for c, here in enumerate(lanes):
                grown = swap_ref[c, pl.ds(t * TILE * pitch + d, TILE, stride=pitch), :]
                out_ref[0, d, pl.ds(t * TILE, TILE), here] = home_ref[0, d, pl.ds(t * TILE, TILE), here] + grown
        return carry

    lax.fori_loop(0, dirs, body, 0, unroll=2)


def join(own, into, home, early, late, freqs, begin):
    parts = len(early)
    many, dirs, rows, cols = home.shape
    half = early[0].shape[0]
    block = pl.BlockSpec((1, dirs, rows, cols), lambda f: (f, 0, 0, 0))
    piece = pl.BlockSpec((half, 1, dirs, cols), lambda f: (0, f, 0, 0))
    return pl.pallas_call(
        functools.partial(join_kernel, parts),
        grid=(many,),
        in_specs=[pl.BlockSpec(memory_space=pltpu.SMEM), UNREAD, block] + [piece] * (2 * parts),
        out_specs=pl.BlockSpec((1, dirs, rows, cols), lambda f: (begin + f, 0, 0, 0)),
        out_shape=jax.ShapeDtypeStruct((freqs, dirs, rows, cols), jnp.float32),
        scratch_shapes=[pltpu.VMEM((cols // LANES, rows * (dirs + 1), LANES), jnp.float32)],
        input_output_aliases={} if begin == 0 else {1: 0},
        compiler_params=pltpu.CompilerParams(vmem_limit_bytes=VMEM_LIMIT),
        cost_estimate=pl.CostEstimate(flops=home.size, bytes_accessed=10 * home.size, transcendentals=0),
    )(own, into, home, *early, *late)


def swapped(pieces):
    parts = len(pieces)
    moved = {k: lax.ppermute(pieces[k], "comp", [(i, i ^ k) for i in range(parts)]) for k in range(parts - 1, 0, -1)}
    return [pieces[0]] + [moved[k] for k in range(1, parts)]


def across(low, high):
    count = lax.axis_size("space")
    up = [(i, i + 1) for i in range(count - 1)]
    down = [(i + 1, i) for i in range(count - 1)]
    return lax.ppermute(high, "space", up), lax.ppermute(low, "space", down)


def near_levels(cg, turn, mask):
    freqs, rows, _ = cg.shape
    levels = jnp.concatenate([cg, turn, mask[None]], axis=0)
    low, high = levels[:, :HALO], levels[:, rows - HALO :]
    above, below = across(low, high)
    near = jnp.concatenate([above, low, high, below], axis=1)
    return (near[:freqs], near[freqs : 2 * freqs], near[2 * freqs])


def shards(
    adjoint_forcing,
    forward_state,
    wind_speed,
    cg_index,
    turn_index,
    sea_mask,
    dir_sign,
    w_in,
    w_out,
    wind_weight,
):
    parts = lax.axis_size("comp")
    own_place = lax.axis_index("comp")
    own = own_place.astype(jnp.int32).reshape(1)
    dirs = dir_sign.shape[1]
    comps, rows, cols = adjoint_forcing.shape
    freqs = comps // dirs
    half = rows // parts // 2
    along = jnp.stack(direction_factors(dirs))
    forcing = adjoint_forcing.reshape(freqs, dirs, rows, cols)
    weight = wind_weight[:, None]
    wind = wind_speed[:, None]
    many = freqs // 2 if freqs % 2 == 0 else freqs
    groups = [(begin, many) for begin in range(0, freqs, many)]

    def spread(after, side, chunks, keep, group):
        fields = (forcing, cg_index, turn_index, sea_mask)
        return propagate(own, dir_sign, along, after, *fields, side, parts, chunks, keep, group)

    near = near_levels(cg_index, turn_index, sea_mask)
    early, late, homes = [], [], []
    after = wind
    if half >= HALO:
        _, [pieces] = spread(after, None, (False,), False, groups[0])
        early.append(swapped(pieces))
        after = pieces[-1]
    low, high = edges(after, forcing)
    side = (*across(low, high), *near)
    after = high
    if half >= HALO:
        for group in groups[1:]:
            _, [pieces] = spread(after, None, (False,), False, group)
            early.append(swapped(pieces))
            after = pieces[-1]
    state = by_row(after, forward_state)
    in_t, out_t = turned(state, w_in, w_out)
    after = in_t
    for group in groups:
        home, pieces = spread(after, side, (True,) if half >= HALO else (False, True), True, group)
        if half < HALO:
            early.append(swapped(pieces[0]))
        late.append(swapped(pieces[-1]))
        homes.append(home)
        after = pieces[-1][-1]
    early_grad, early_back = source_term(own, after, state, wind, w_in, out_t, in_t, weight, early, False)
    after = early_back[-1][-1]
    early_back = [swapped(pieces) for pieces in early_back]
    late_grad, late_back = source_term(own, after, state, wind, w_in, out_t, in_t, weight, late, True)
    start = late_back[-1][-1]
    late_back = [swapped(pieces) for pieces in late_back]
    for g, (begin, _) in enumerate(groups):
        start = join(own, start, homes[g], early_back[g], late_back[g], freqs, begin)
    first = jnp.where(own_place == 0, late_grad, early_grad)
    second = jnp.where(own_place == 0, early_grad, late_grad)
    return (start.reshape(comps, rows, cols), jnp.concatenate([first, second], axis=0))


def solution(mesh):
    placed = (
        P("comp", "space", None),
        P(None, ("space", "comp"), None),
        P(("space", "comp"), None),
        P("comp", "space", None),
        P("comp", "space", None),
        P("space", None),
        P(),
        P(),
        P(),
        P(),
    )
    return jax.shard_map(
        shards,
        mesh=mesh,
        in_specs=placed,
        out_specs=(P("comp", "space", None), P(("space", "comp"), None)),
        check_vma=False,
    )
```

```python
import functools
import math

import jax
import jax.numpy as jnp
from jax import lax
from jax.experimental import pallas as pl
from jax.experimental.pallas import tpu as pltpu
from jax.sharding import PartitionSpec as P

HALO = 2
TILE = 8
LANES = 128
MIB = 1 << 20
VMEM_LIMIT = 60 * MIB
COST = pl.CostEstimate(flops=1, bytes_accessed=1, transcendentals=0)


def direction_factors(dirs):
    angle = (jnp.arange(dirs, dtype=jnp.float32) + 0.5) * (2.0 * math.pi / dirs)
    return (0.5 * jnp.abs(jnp.cos(angle)), 0.5 * jnp.abs(jnp.sin(angle)))


def chunk_row(owner, j, half, late):
    return jnp.where((owner == 0) != late, half + j, j)


UNREAD = pl.BlockSpec(memory_space=pl.ANY)


def lane_tiles(cols):
    return [pl.ds(c * LANES, LANES) for c in range(cols // LANES)]


def coefficients(cel_ref, base_ref, trn_ref, here, cg, turn, sea):
    sea = sea.astype(jnp.float32)
    celerity = 0.1 + 0.8 * cg.astype(jnp.float32) / 7.0
    turning = 0.3 * jnp.abs(turn.astype(jnp.float32) - 3.5) / 3.5
    cel_ref[here, :] = celerity * sea
    base_ref[here, :] = (1.0 - turning) * sea
    trn_ref[here, :] = turning * sea


def sweep(dirs, tiles, lanes, sign_ref, along_ref, coefs, turns_up, load, store):
    cel_ref, base_ref, trn_ref = coefs
    row = lax.broadcasted_iota(jnp.int32, (TILE, LANES), 0)
    lane = lax.broadcasted_iota(jnp.int32, (TILE, LANES), 1)
    nothing = jnp.zeros((TILE, LANES), jnp.float32)

    def span(t):
        return pl.ds(t * TILE, TILE)

    def pair(i, carry):
        ds = (2 * i, 2 * i + 1)
        around = (jnp.where(i == 0, dirs - 1, 2 * i - 1), jnp.where(i == dirs // 2 - 1, 0, 2 * i + 2))
        right = [sign_ref[0, d] > 0 for d in ds]
        high = [sign_ref[1, d] > 0 for d in ds]
        ax = [along_ref[0, d] for d in ds]
        ay = [along_ref[1, d] for d in ds]
        shift_x = [jnp.where(r, LANES - 1, 1) for r in right]
        shift_y = [jnp.where(h, TILE - 1, 1) for h in high]
        at_right = [lane == jnp.where(r, LANES - 1, LANES) for r in right]
        at_left = [lane == jnp.where(r, LANES, 0) for r in right]
        at_high = [row == jnp.where(h, TILE - 1, TILE) for h in high]
        at_low = [row == jnp.where(h, TILE, 0) for h in high]

        def column(c):
            flow = [[None] * tiles, [None] * tiles]
            for t in range(tiles):
                cel = cel_ref[span(t), lanes[c]]
                for n in range(2):
                    flow[n][t] = cel * load(t, ds[n], lanes[c])
            return flow, [[pltpu.roll(f, shift_x[n], 1) for f in flow[n]] for n in range(2)]

        before = [[nothing] * tiles] * 2
        flow, moved = column(0)
        for c in range(len(lanes)):
            beyond = [[nothing] * tiles] * 2
            if c + 1 < len(lanes):
                later = column(c + 1)
                beyond = later[1]
            lifted = [[pltpu.roll(f, shift_y[n], 0) for f in flow[n]] for n in range(2)]
            for t in range(tiles):
                up = turns_up(t, c)
                base = base_ref[span(t), lanes[c]]
                trn = trn_ref[span(t), lanes[c]]
                here = [load(t, d, lanes[c]) for d in ds]
                aside = [load(t, d, lanes[c]) for d in around]
                turned = (jnp.where(up, here[1], aside[0]), jnp.where(up, aside[1], here[0]))
                for n in range(2):
                    above = lifted[n][t + 1] if t + 1 < tiles else nothing
                    below = lifted[n][t - 1] if t > 0 else nothing
                    flow_x = jnp.where(at_right[n], beyond[n][t], jnp.where(at_left[n], before[n][t], moved[n][t]))
                    flow_y = jnp.where(at_high[n], above, jnp.where(at_low[n], below, lifted[n][t]))
                    total = base * here[n] + ax[n] * (flow_x - flow[n][t])
                    total = total + ay[n] * (flow_y - flow[n][t]) + trn * turned[n]
                    store(t, ds[n], c, total)
            if c + 1 < len(lanes):
                before = moved
                flow, moved = later
        return carry

    lax.fori_loop(0, dirs // 2, pair, 0, unroll=1 if tiles > 1 else 3)


def emit(own, parts, local, chunks, dirs, lanes, swap_ref, send_refs):
    half = local // 2
    for i, late in enumerate(chunks):
        for k in range(parts):
            owner = own ^ k
            for j in range(half):
                start = (owner * local + chunk_row(owner, j, half, late)) * (dirs + 1)
                for c, here in enumerate(lanes):
                    piece = swap_ref[c, pl.ds(start, dirs), :]
                    send_refs[i * parts + k][j, 0, :, here] = piece.astype(jnp.bfloat16)


def inner_kernel(parts, local, chunks, into, own_ref, sign_ref, along_ref, _, forcing_ref, cg_ref, turn_ref, mask_ref, *refs):
    refs = refs[1:] if into else refs
    home_ref = refs[0]
    sends = parts * len(chunks)
    cel_ref, base_ref, trn_ref, first_ref, swap_ref = refs[sends + 1 :]
    dirs, rows, _ = forcing_ref.shape[1:]
    pitch = dirs + 1
    lanes = lane_tiles(forcing_ref.shape[3])
    tiles = rows // TILE

    def span(t):
        return pl.ds(t * TILE, TILE)

    for t in range(tiles):
        levels = (cg_ref[0, span(t), :], turn_ref[0, span(t), :], mask_ref[span(t), :])
        coefficients(cel_ref, base_ref, trn_ref, span(t), *levels)

    def turns_up(t, c):
        return turn_ref[0, span(t), lanes[c]] >= 4

    def store_first(t, d, c, value):
        first_ref[d, span(t), lanes[c]] = value

    def store_last(t, d, c, value):
        home_ref[0, d, span(t), lanes[c]] = value
        if chunks:
            swap_ref[c, pl.ds(t * TILE * pitch + d, TILE, stride=pitch), :] = value

    step = functools.partial(sweep, dirs, tiles, lanes, sign_ref, along_ref, (cel_ref, base_ref, trn_ref), turns_up)
    step(lambda t, d, here: forcing_ref[0, d, span(t), here], store_first)
    step(lambda t, d, here: first_ref[d, span(t), here], store_last)
    emit(own_ref[0], parts, local, chunks, dirs, lanes, swap_ref, refs[1 : sends + 1])


def inner(own, signs, along, after, forcing, cg, turn, mask, into, parts, chunks, group):
    freqs, dirs, rows, cols = forcing.shape
    begin, many = group
    local = rows // parts
    half = local // 2
    smem = pl.BlockSpec(memory_space=pltpu.SMEM)
    levels = pl.BlockSpec((1, rows, cols), lambda f: (begin + f, 0, 0))
    block = pl.BlockSpec((1, dirs, rows, cols), lambda f: (begin + f, 0, 0, 0))
    coefs = pltpu.VMEM((rows, cols), jnp.float32)
    sends = parts * len(chunks)
    outs = pl.pallas_call(
        functools.partial(inner_kernel, parts, local, chunks, into is not None),
        grid=(many,),
        in_specs=[smem, smem, smem, UNREAD, block, levels, levels, pl.BlockSpec((rows, cols), lambda f: (0, 0))]
        + ([] if into is None else [UNREAD]),
        out_specs=[block] + [pl.BlockSpec((half, 1, dirs, cols), lambda f: (0, f, 0, 0))] * sends,
        out_shape=[jax.ShapeDtypeStruct(forcing.shape, jnp.float32)]
        + [jax.ShapeDtypeStruct((half, many, dirs, cols), jnp.bfloat16)] * sends,
        scratch_shapes=[
            coefs,
            coefs,
            coefs,
            pltpu.VMEM((dirs, rows, cols), jnp.float32),
            pltpu.VMEM((cols // LANES, rows * (dirs + 1), LANES), jnp.float32),
        ],
        input_output_aliases={} if into is None else {8: 0},
        compiler_params=pltpu.CompilerParams(vmem_limit_bytes=VMEM_LIMIT),
        cost_estimate=COST,
    )(own, signs, along, after, forcing, cg, turn, mask, *([] if into is None else [into]))
    return outs[0], list(outs[1:])


def outer_kernel(parts, local, chunks, *refs):
    own_ref, sign_ref, along_ref, _, above_ref, below_ref, above_lev_ref, below_lev_ref = refs[:8]
    cg_ref, turn_ref, mask_ref, home_ref, share_ref = refs[8:13]
    sends = parts * len(chunks)
    send_refs = refs[13 : 13 + sends]
    cel_ref, base_ref, trn_ref, lev_ref, near_ref, first_ref, side_ref, edge_ref, swap_ref = refs[13 + sends :]
    dirs, rows, cols = home_ref.shape[1:]
    pitch = dirs + 1
    lanes = lane_tiles(cols)
    tiles = rows // TILE
    f, freqs = pl.program_id(0), pl.num_programs(0)

    for i, (ref, r) in enumerate(((above_lev_ref, 0), (above_lev_ref, 1), (below_lev_ref, 0), (below_lev_ref, 1))):
        lev_ref[pl.ds(i * dirs, dirs), :] = ref[r, 0].astype(jnp.float32)
    kinds = ((f, cg_ref[0]), (freqs + f, turn_ref[0]), (2 * freqs, mask_ref[...]))
    for q, (place, mine) in enumerate(kinds):
        for i in range(HALO):
            near_ref[q * TILE + i : q * TILE + i + 1, :] = lev_ref[pl.ds(i * dirs + place, 1), :]
            low = q * TILE + TILE - HALO + i
            near_ref[low : low + 1, :] = lev_ref[pl.ds((HALO + i) * dirs + place, 1), :]
        near_ref[q * TILE + HALO : q * TILE + 2 * HALO, :] = mine[:HALO].astype(jnp.float32)
        near_ref[q * TILE + 2 * HALO : q * TILE + 3 * HALO, :] = mine[rows - HALO :].astype(jnp.float32)
    near = [near_ref[pl.ds(q * TILE, TILE), :] for q in range(3)]
    coefficients(cel_ref, base_ref, trn_ref, pl.ds(0, TILE), *near)

    edge_ref[...] = jnp.zeros_like(edge_ref)
    for r in range(HALO):
        for c, here in enumerate(lanes):
            edge_ref[c, pl.ds(r * pitch, dirs), :] = above_ref[r, 0, :, here].astype(jnp.float32)
            edge_ref[c, pl.ds((TILE - HALO + r) * pitch, dirs), :] = below_ref[r, 0, :, here].astype(jnp.float32)

    def gather(d, carry):
        for c, here in enumerate(lanes):
            side_ref[d, :, here] = edge_ref[c, pl.ds(d, TILE, stride=pitch), :]
        return carry

    lax.fori_loop(0, dirs, gather, 0, unroll=4)

    def turns_up(t, c):
        return near_ref[pl.ds(TILE, TILE), lanes[c]] >= 4.0

    def store_first(t, d, c, value):
        first_ref[d, :, lanes[c]] = value

    def store_last(t, d, c, value):
        share_ref[0, d, :, lanes[c]] = value

    step = functools.partial(sweep, dirs, 1, lanes, sign_ref, along_ref, (cel_ref, base_ref, trn_ref), turns_up)
    step(lambda t, d, here: side_ref[d, :, here], store_first)
    step(lambda t, d, here: first_ref[d, :, here], store_last)

    def whole(d, carry):
        for t in range(tiles):
            for c, here in enumerate(lanes):
                value = with_share(home_ref[0, d, pl.ds(t * TILE, TILE), here], share_ref, d, here, t, tiles)
                swap_ref[c, pl.ds(t * TILE * pitch + d, TILE, stride=pitch), :] = value
        return carry

    lax.fori_loop(0, dirs, whole, 0, unroll=2)
    emit(own_ref[0], parts, local, chunks, dirs, lanes, swap_ref, send_refs)


def with_share(value, share_ref, d, here, t, tiles):
    row = lax.broadcasted_iota(jnp.int32, value.shape, 0)
    if t == 0:
        value = value + jnp.where(row < HALO, pltpu.roll(share_ref[0, d, :, here], TILE - HALO, 0), 0.0)
    if t == tiles - 1:
        value = value + jnp.where(row >= TILE - HALO, pltpu.roll(share_ref[0, d, :, here], HALO, 0), 0.0)
    return value


def outer(own, signs, along, after, above, below, cg, turn, mask, home, parts, chunks):
    freqs, dirs, rows, cols = home.shape
    local = rows // parts
    half = local // 2
    smem = pl.BlockSpec(memory_space=pltpu.SMEM)
    edge = pl.BlockSpec((HALO, 1, dirs, cols), lambda f: (0, f, 0, 0))
    last = pl.BlockSpec((HALO, 1, dirs, cols), lambda f: (0, freqs, 0, 0))
    levels = pl.BlockSpec((1, rows, cols), lambda f: (f, 0, 0))
    sends = parts * len(chunks)
    tile = pltpu.VMEM((TILE, cols), jnp.float32)
    outs = pl.pallas_call(
        functools.partial(outer_kernel, parts, local, chunks),
        grid=(freqs,),
        in_specs=[smem, smem, smem, UNREAD, edge, edge, last, last, levels, levels]
        + [pl.BlockSpec((rows, cols), lambda f: (0, 0)), pl.BlockSpec((1, dirs, rows, cols), lambda f: (f, 0, 0, 0))],
        out_specs=[pl.BlockSpec((1, dirs, TILE, cols), lambda f: (f, 0, 0, 0))]
        + [pl.BlockSpec((half, 1, dirs, cols), lambda f: (0, f, 0, 0))] * sends,
        out_shape=[jax.ShapeDtypeStruct((freqs, dirs, TILE, cols), jnp.float32)]
        + [jax.ShapeDtypeStruct((half, freqs, dirs, cols), jnp.bfloat16)] * sends,
        scratch_shapes=[
            tile,
            tile,
            tile,
            pltpu.VMEM((2 * HALO * dirs, cols), jnp.float32),
            pltpu.VMEM((3 * TILE, cols), jnp.float32),
            pltpu.VMEM((dirs, TILE, cols), jnp.float32),
            pltpu.VMEM((dirs, TILE, cols), jnp.float32),
            pltpu.VMEM((cols // LANES, TILE * (dirs + 1), LANES), jnp.float32),
            pltpu.VMEM((cols // LANES, rows * (dirs + 1), LANES), jnp.float32),
        ],
        compiler_params=pltpu.CompilerParams(vmem_limit_bytes=VMEM_LIMIT),
        cost_estimate=COST,
    )(own, signs, along, after, above, below, above, below, cg, turn, mask, home)
    return outs[0], [list(outs[1 + i * parts : 1 + (i + 1) * parts]) for i in range(len(chunks))]


def edges_kernel(freqs, _, *refs):
    swap_ref, lev_ref = refs[-2:]
    dirs, _, cols = refs[0].shape[1:]
    pitch = dirs + 1
    lanes = lane_tiles(cols)
    f = pl.program_id(0)

    for side, low in ((0, 0), (1, TILE - HALO)):
        forcing_ref, cg_ref, turn_ref, mask_ref = refs[4 * side : 4 * side + 4]
        out_ref = refs[8 + side]

        @pl.when(f < freqs)
        def _(forcing_ref=forcing_ref, out_ref=out_ref, low=low):
            def body(d, carry):
                for c, here in enumerate(lanes):
                    swap_ref[c, pl.ds(d, TILE, stride=pitch), :] = forcing_ref[0, d, :, here]
                return carry

            lax.fori_loop(0, dirs, body, 0, unroll=2)
            for r in range(HALO):
                for c, here in enumerate(lanes):
                    out_ref[r, 0, :, here] = swap_ref[c, pl.ds((low + r) * pitch, dirs), :].astype(jnp.bfloat16)

        @pl.when(f == freqs)
        def _(cg_ref=cg_ref, turn_ref=turn_ref, mask_ref=mask_ref, out_ref=out_ref, low=low):
            lev_ref[...] = jnp.zeros_like(lev_ref)
            for r in range(low, low + HALO):
                for n in range(freqs):
                    lev_ref[n : n + 1, :] = cg_ref[n, r : r + 1, :].astype(jnp.float32)
                    lev_ref[freqs + n : freqs + n + 1, :] = turn_ref[n, r : r + 1, :].astype(jnp.float32)
                lev_ref[2 * freqs : 2 * freqs + 1, :] = mask_ref[r : r + 1, :].astype(jnp.float32)
                out_ref[r - low, 0] = lev_ref[...].astype(jnp.bfloat16)


def edges(after, forcing, cg, turn, mask):
    freqs, dirs, rows, cols = forcing.shape
    assert 2 * freqs + 1 <= dirs
    out = pl.BlockSpec((HALO, 1, dirs, cols), lambda f: (0, f, 0, 0))
    shape = jax.ShapeDtypeStruct((HALO, freqs + 1, dirs, cols), jnp.bfloat16)
    in_specs = [UNREAD]
    for t in (0, rows // TILE - 1):
        in_specs += [
            pl.BlockSpec((1, dirs, TILE, cols), lambda f, t=t: (jnp.minimum(f, freqs - 1), 0, t, 0)),
            pl.BlockSpec((freqs, TILE, cols), lambda f, t=t: (0, t, 0)),
            pl.BlockSpec((freqs, TILE, cols), lambda f, t=t: (0, t, 0)),
            pl.BlockSpec((TILE, cols), lambda f, t=t: (t, 0)),
        ]
    return pl.pallas_call(
        functools.partial(edges_kernel, freqs),
        grid=(freqs + 1,),
        in_specs=in_specs,
        out_specs=[out, out],
        out_shape=[shape, shape],
        scratch_shapes=[
            pltpu.VMEM((cols // LANES, TILE * (dirs + 1), LANES), jnp.float32),
            pltpu.VMEM((dirs, cols), jnp.float32),
        ],
        compiler_params=pltpu.CompilerParams(vmem_limit_bytes=VMEM_LIMIT),
        cost_estimate=COST,
    )(after, *(2 * [forcing, cg, turn, mask]))


def by_row_kernel(_, state_ref, out_ref, swap_ref):
    deep, local, _ = state_ref.shape
    pitch = deep + 1

    def body(d, carry):
        swap_ref[pl.ds(d, local, stride=pitch), :] = state_ref[d].astype(jnp.float32)
        return carry

    lax.fori_loop(0, deep, body, 0, unroll=16)
    for r in range(local):
        out_ref[r] = swap_ref[pl.ds(r * pitch, deep), :].astype(jnp.bfloat16)


def by_row(after, state):
    deep, local, cols = state.shape
    return pl.pallas_call(
        by_row_kernel,
        grid=(cols // LANES,),
        in_specs=[UNREAD, pl.BlockSpec((deep, local, LANES), lambda c: (0, 0, c))],
        out_specs=pl.BlockSpec((local, deep, LANES), lambda c: (0, 0, c)),
        out_shape=jax.ShapeDtypeStruct((local, deep, cols), jnp.bfloat16),
        scratch_shapes=[pltpu.VMEM((local * (deep + 1), LANES), jnp.float32)],
        compiler_params=pltpu.CompilerParams(vmem_limit_bytes=VMEM_LIMIT),
        cost_estimate=COST,
    )(after, state)


def turned_kernel(_, w_in_ref, w_out_ref, in_t_ref, out_t_ref):
    in_t_ref[...] = w_in_ref[...].T
    out_t_ref[...] = w_out_ref[...].T


def turned(after, w_in, w_out):
    hidden, total = w_in.shape
    step = 512
    tall = pl.BlockSpec((step, total), lambda h: (h, 0))
    wide = pl.BlockSpec((total, step), lambda h: (0, h))
    return pl.pallas_call(
        turned_kernel,
        grid=(hidden // step,),
        in_specs=[UNREAD, tall, wide],
        out_specs=[wide, tall],
        out_shape=[jax.ShapeDtypeStruct((total, hidden), w_in.dtype), jax.ShapeDtypeStruct((hidden, total), w_in.dtype)],
        compiler_params=pltpu.CompilerParams(vmem_limit_bytes=VMEM_LIMIT),
        cost_estimate=COST,
    )(after, w_in, w_out)


def source_kernel(parts, got, sent, dirs, step, own_ref, _, state_ref, wind_ref, w_in_ref, out_t_ref, in_t_ref, weight_ref, *refs):
    cell_refs = refs[: parts * len(got)]
    grad_ref = refs[parts * len(got)]
    back_refs = refs[parts * len(got) + 1 : -3]
    cell_ref, weighted_ref, grown_ref = refs[-3:]
    freqs = sum(many for _, many in got)
    hidden, width = weighted_ref.shape
    own = own_ref[0]

    def place(k, group):
        begin, many = group
        return pl.ds(pl.multiple_of(((own ^ k) * freqs + begin) * dirs, TILE), many * dirs)

    for g, group in enumerate(got):
        for k in range(parts):
            piece = cell_refs[g * parts + k][0].astype(jnp.float32)
            cell_ref[place(k, group), :] = piece.reshape(group[1] * dirs, width)
    cell = cell_ref[...].astype(jnp.bfloat16)
    state = state_ref[0]
    wind = wind_ref[0]
    grad = jnp.zeros((TILE, width), jnp.float32)
    for h in range(0, hidden, step):
        some = pl.ds(h, step)
        weight = weight_ref[some, :]
        forward = jnp.dot(w_in_ref[some, :], state, preferred_element_type=jnp.float32) + weight * wind
        squash = jnp.tanh(forward)
        pulled = jnp.dot(out_t_ref[some, :], cell, preferred_element_type=jnp.float32)
        weighted = (1.0 - squash * squash) * pulled
        weighted_ref[some, :] = weighted.astype(jnp.bfloat16)
        grad = grad + jnp.sum((weight * weighted).reshape(step // TILE, TILE, width), axis=0)
    grad_ref[0] = jnp.sum(grad, axis=0, keepdims=True)
    grown_ref[...] = jnp.dot(in_t_ref[...], weighted_ref[...], preferred_element_type=jnp.float32)
    for g, group in enumerate(sent):
        for k in range(parts):
            grown = grown_ref[place(k, group), :].reshape(group[1], dirs, width)
            back_refs[g * parts + k][0] = grown.astype(jnp.bfloat16)


def source_term(own, after, state, wind, w_in, out_t, in_t, weight, cells, got, sent, rows, late):
    parts = len(cells[0])
    half, _, dirs, cols = cells[0][0].shape
    first, count = rows
    hidden, total = w_in.shape
    width = min(cols, 512)

    def row_of(j, own_ref):
        return chunk_row(own_ref[0], first + j, half, late)

    def whole(shape):
        return pl.BlockSpec(shape, lambda j, c, own_ref: (0, 0))

    cell_specs = [
        pl.BlockSpec((1, many, dirs, width), lambda j, c, own_ref: (first + j, 0, 0, c)) for _, many in got for _ in range(parts)
    ]
    back_specs = [pl.BlockSpec((1, many, dirs, width), lambda j, c, own_ref: (j, 0, 0, c)) for _, many in sent for _ in range(parts)]
    outs = pl.pallas_call(
        functools.partial(source_kernel, parts, got, sent, dirs, 256),
        grid_spec=pltpu.PrefetchScalarGridSpec(
            num_scalar_prefetch=1,
            grid=(count, cols // width),
            in_specs=[
                UNREAD,
                pl.BlockSpec((1, total, width), lambda j, c, own_ref: (row_of(j, own_ref), 0, c)),
                pl.BlockSpec((1, 1, width), lambda j, c, own_ref: (row_of(j, own_ref), 0, c)),
                whole((hidden, total)),
                whole((hidden, total)),
                whole((total, hidden)),
                whole((hidden, 1)),
            ]
            + cell_specs,
            out_specs=[pl.BlockSpec((1, 1, width), lambda j, c, own_ref: (j, 0, c))] + back_specs,
            scratch_shapes=[
                pltpu.VMEM((total, width), jnp.float32),
                pltpu.VMEM((hidden, width), jnp.bfloat16),
                pltpu.VMEM((total, width), jnp.float32),
            ],
        ),
        out_shape=[jax.ShapeDtypeStruct((count, 1, cols), jnp.float32)]
        + [jax.ShapeDtypeStruct((count, many, dirs, cols), jnp.bfloat16) for _, many in sent for _ in range(parts)],
        compiler_params=pltpu.CompilerParams(vmem_limit_bytes=VMEM_LIMIT),
        cost_estimate=COST,
    )(own, after, state, wind, w_in, out_t, in_t, weight, *[cell for group in cells for cell in group])
    return outs[0].reshape(count, cols), [list(outs[1 + g * parts : 1 + (g + 1) * parts]) for g in range(len(sent))]


def join_kernel(parts, spans, own_ref, _, home_ref, share_ref, *refs):
    out_ref, swap_ref = refs[-2:]
    dirs, rows, cols = home_ref.shape[1:]
    pitch = dirs + 1
    local = rows // parts
    half = local // 2
    own = own_ref[0]
    lanes = lane_tiles(cols)
    tiles = rows // TILE
    for i, (first, count, late) in enumerate(spans):
        for k in range(parts):
            owner = own ^ k
            for j in range(count):
                start = (owner * local + chunk_row(owner, first + j, half, late)) * pitch
                for c, here in enumerate(lanes):
                    swap_ref[c, pl.ds(start, dirs), :] = refs[i * parts + k][j, 0, :, here].astype(jnp.float32)

    def body(d, carry):
        for t in range(tiles):
            for c, here in enumerate(lanes):
                grown = swap_ref[c, pl.ds(t * TILE * pitch + d, TILE, stride=pitch), :]
                value = with_share(home_ref[0, d, pl.ds(t * TILE, TILE), here], share_ref, d, here, t, tiles)
                out_ref[0, d, pl.ds(t * TILE, TILE), here] = value + grown
        return carry

    lax.fori_loop(0, dirs, body, 0, unroll=2)


def join(own, into, home, share, early, late, rows_of, group):
    begin, many = group
    parts = len(late)
    _, dirs, rows, cols = home.shape
    half = late[0].shape[0]
    spans = [(*span, False) for span in rows_of] + [(0, half, True)]
    block = pl.BlockSpec((1, dirs, rows, cols), lambda f: (begin + f, 0, 0, 0))
    specs = [
        pl.BlockSpec((count, 1, dirs, cols), lambda f: (0, begin + f, 0, 0)) for _, count in rows_of for _ in range(parts)
    ] + [pl.BlockSpec((half, 1, dirs, cols), lambda f: (0, f, 0, 0))] * parts
    return pl.pallas_call(
        functools.partial(join_kernel, parts, spans),
        grid=(many,),
        in_specs=[pl.BlockSpec(memory_space=pltpu.SMEM), UNREAD, block]
        + [pl.BlockSpec((1, dirs, TILE, cols), lambda f: (begin + f, 0, 0, 0))]
        + specs,
        out_specs=block,
        out_shape=jax.ShapeDtypeStruct(home.shape, jnp.float32),
        scratch_shapes=[pltpu.VMEM((cols // LANES, rows * (dirs + 1), LANES), jnp.float32)],
        input_output_aliases={} if begin == 0 else {1: 0},
        compiler_params=pltpu.CompilerParams(vmem_limit_bytes=VMEM_LIMIT),
        cost_estimate=COST,
    )(own, into, home, share, *[piece for pieces in early for piece in pieces], *late)


def swapped(pieces):
    parts = len(pieces)
    moved = {k: lax.ppermute(pieces[k], "comp", [(i, i ^ k) for i in range(parts)]) for k in range(parts - 1, 0, -1)}
    return [pieces[0]] + [moved[k] for k in range(1, parts)]


def across(low, high):
    count = lax.axis_size("space")
    up = [(i, i + 1) for i in range(count - 1)]
    down = [(i + 1, i) for i in range(count - 1)]
    return lax.ppermute(high, "space", up), lax.ppermute(low, "space", down)


def halves(count):
    spans, begin = [], 0
    while begin < count:
        many = max(1, (count - begin) // 2)
        spans.append((begin, many))
        begin += many
    return spans


def shards(
    adjoint_forcing,
    forward_state,
    wind_speed,
    cg_index,
    turn_index,
    sea_mask,
    dir_sign,
    w_in,
    w_out,
    wind_weight,
):
    parts = lax.axis_size("comp")
    own_place = lax.axis_index("comp")
    own = own_place.astype(jnp.int32).reshape(1)
    dirs = dir_sign.shape[1]
    comps, rows, cols = adjoint_forcing.shape
    freqs = comps // dirs
    half = rows // parts // 2
    along = jnp.stack(direction_factors(dirs))
    forcing = adjoint_forcing.reshape(freqs, dirs, rows, cols)
    weight = wind_weight[:, None]
    wind = wind_speed[:, None]
    everything = [(0, freqs)]
    many = freqs // 2 if freqs % 2 == 0 else freqs
    groups = [(begin, many) for begin in range(0, freqs, many)]
    sent = halves(freqs)
    rows_of = [(0, half // 2), (half // 2, half // 2)] if half % 2 == 0 else [(0, half)]
    levels = (cg_index, turn_index, sea_mask)
    clear = half >= HALO

    early, home, after = [], None, wind
    for g, group in enumerate(groups):
        into = home
        home, pieces = inner(own, dir_sign, along, after, forcing, *levels, into, parts, (False,) if clear else (), group)
        after = home
        if clear:
            early.append(swapped(pieces))
            after = pieces[-1]
        if g == 0:
            low, high = edges(after, forcing, *levels)
            above, below = across(low, high)
            after = high
    share, pieces = outer(own, dir_sign, along, after, above, below, *levels, home, parts, (True,) if clear else (False, True))
    if not clear:
        early.append(swapped(pieces[0]))
    late = swapped(pieces[-1])
    state = by_row(share, forward_state)
    in_t, out_t = turned(state, w_in, w_out)
    term = functools.partial(source_term, own)
    fixed = (state, wind, w_in, out_t, in_t, weight)
    after, early_grads, early_back = in_t, [], []
    for span in rows_of:
        grad, [back] = term(after, *fixed, early, groups if clear else everything, everything, span, False)
        after = grad
        early_grads.append(grad)
        early_back.append(swapped(back))
    late_grad, late_back = term(after, *fixed, [late], everything, sent, (0, half), True)
    start = late_grad
    late_back = [swapped(pieces) for pieces in late_back]
    for group, back in zip(sent, late_back, strict=True):
        start = join(own, start, home, share, early_back, back, rows_of, group)
    early_grad = jnp.concatenate(early_grads, axis=0)
    first = jnp.where(own_place == 0, late_grad, early_grad)
    second = jnp.where(own_place == 0, early_grad, late_grad)
    return (start.reshape(comps, rows, cols), jnp.concatenate([first, second], axis=0))


def solution(mesh):
    placed = (
        P("comp", "space", None),
        P(None, ("space", "comp"), None),
        P(("space", "comp"), None),
        P("comp", "space", None),
        P("comp", "space", None),
        P("space", None),
        P(),
        P(),
        P(),
        P(),
    )
    return jax.shard_map(
        shards,
        mesh=mesh,
        in_specs=placed,
        out_specs=(P("comp", "space", None), P(("space", "comp"), None)),
        check_vma=False,
    )
```

```python
import functools
import math

import jax
import jax.numpy as jnp
import numpy as np
from jax import lax
from jax.experimental import pallas as pl
from jax.experimental.pallas import tpu as pltpu
from jax.sharding import PartitionSpec as P

HALO = 2
TILE = 8
LANES = 128
MIB = 1 << 20
VMEM_LIMIT = 60 * MIB
COST = pl.CostEstimate(flops=1, bytes_accessed=1, transcendentals=0)
LONG = pl.CostEstimate(flops=10**11, bytes_accessed=100 * MIB, transcendentals=0)


def direction_factors(dirs):
    angle = (np.arange(dirs, dtype=np.float32) + np.float32(0.5)) * np.float32(2.0 * math.pi / dirs)
    return np.stack([np.float32(0.5) * np.abs(np.cos(angle)), np.float32(0.5) * np.abs(np.sin(angle))])


def chunk_row(owner, j, chunk):
    return jnp.where(owner == 0, chunk[0], chunk[1]) + j


UNREAD = pl.BlockSpec(memory_space=pl.ANY)


def lane_tiles(cols):
    return [pl.ds(c * LANES, LANES) for c in range(cols // LANES)]


def coefficients(cel_ref, base_ref, trn_ref, here, cg, turn, sea):
    sea = sea.astype(jnp.float32)
    celerity = 0.1 + 0.8 * cg.astype(jnp.float32) / 7.0
    turning = 0.3 * jnp.abs(turn.astype(jnp.float32) - 3.5) / 3.5
    cel_ref[here, :] = celerity * sea
    base_ref[here, :] = (1.0 - turning) * sea
    trn_ref[here, :] = turning * sea


def sweep(dirs, tiles, alone, lanes, sign_ref, along_ref, coefs, turns_up, load, store):
    cel_ref, base_ref, trn_ref = coefs
    row = lax.broadcasted_iota(jnp.int32, (TILE, LANES), 0)
    lane = lax.broadcasted_iota(jnp.int32, (TILE, LANES), 1)
    nothing = jnp.zeros((TILE, LANES), jnp.float32)

    def span(t):
        return pl.ds(t * TILE, TILE)

    def one(d, carry):
        following = jnp.where(d == dirs - 1, 0, d + 1)
        previous = jnp.where(d == 0, dirs - 1, d - 1)
        ax = along_ref[0, d]
        ay = along_ref[1, d]
        right = sign_ref[0, d] > 0
        high = sign_ref[1, d] > 0
        shift_x = jnp.where(right, LANES - 1, 1)
        shift_y = jnp.where(high, TILE - 1, 1)
        at_right = lane == jnp.where(right, LANES - 1, LANES)
        at_left = lane == jnp.where(right, LANES, 0)
        at_high = row == jnp.where(high, TILE - 1, TILE)
        at_low = row == jnp.where(high, TILE, 0)
        at_edge = row == jnp.where(high, TILE - 1, 0)

        def column(c):
            here = [load(t, d, lanes[c]) for t in range(tiles)]
            flow = [cel_ref[span(t), lanes[c]] * here[t] for t in range(tiles)]
            return here, flow, [pltpu.roll(f, shift_x, 1) for f in flow]

        before = [nothing] * tiles
        here, flow, moved = column(0)
        for c in range(len(lanes)):
            beyond = [nothing] * tiles
            if c + 1 < len(lanes):
                later = column(c + 1)
                beyond = later[2]
            lifted = [pltpu.roll(f, shift_y, 0) for f in flow]
            for t in range(tiles):
                flow_x = jnp.where(at_right, beyond[t], jnp.where(at_left, before[t], moved[t]))
                if alone:
                    flow_y = jnp.where(at_edge, nothing, lifted[t])
                else:
                    above = lifted[t + 1] if t + 1 < tiles else nothing
                    below = lifted[t - 1] if t > 0 else nothing
                    flow_y = jnp.where(at_high, above, jnp.where(at_low, below, lifted[t]))
                turned = jnp.where(turns_up(t, c), load(t, following, lanes[c]), load(t, previous, lanes[c]))
                total = base_ref[span(t), lanes[c]] * here[t] + ax * (flow_x - flow[t])
                total = total + ay * (flow_y - flow[t]) + trn_ref[span(t), lanes[c]] * turned
                store(t, d, c, total)
            if c + 1 < len(lanes):
                before = moved
                here, flow, moved = later
        return carry

    lax.fori_loop(0, dirs, one, 0, unroll=6)


def emit(own, parts, local, chunk, dirs, lanes, swap_ref, send_refs):
    for k in range(parts):
        owner = own ^ k
        for j in range(chunk[2]):
            start = (owner * local + chunk_row(owner, j, chunk)) * (dirs + 1)
            for c, here in enumerate(lanes):
                send_refs[k][j, 0, :, here] = swap_ref[c, pl.ds(start, dirs), :].astype(jnp.bfloat16)


def inner_kernel(parts, local, chunk, into, own_ref, sign_ref, along_ref, _, forcing_ref, cg_ref, turn_ref, mask_ref, *refs):
    refs = refs[3:] if into else refs
    home_ref, first_out, last_out = refs[:3]
    sends = parts if chunk else 0
    cel_ref, base_ref, trn_ref, first_ref, swap_ref, edge_ref = refs[sends + 3 :]
    dirs, rows, cols = forcing_ref.shape[1:]
    pitch = dirs + 1
    lanes = lane_tiles(cols)
    tiles = rows // TILE

    def span(t):
        return pl.ds(t * TILE, TILE)

    for t in range(tiles):
        levels = (cg_ref[0, span(t), :], turn_ref[0, span(t), :], mask_ref[span(t), :])
        coefficients(cel_ref, base_ref, trn_ref, span(t), *levels)

    def outermost(d, carry):
        for side, t in enumerate((0, tiles - 1)):
            for c, here in enumerate(lanes):
                swap_ref[c, pl.ds(side * TILE * pitch + d, TILE, stride=pitch), :] = forcing_ref[0, d, span(t), here]
        return carry

    lax.fori_loop(0, dirs, outermost, 0, unroll=8)
    edge_ref[...] = jnp.zeros_like(edge_ref)
    for out_ref, low, at in ((first_out, 0, 0), (last_out, rows - HALO, 2 * TILE - HALO)):
        for r in range(HALO):
            for c, here in enumerate(lanes):
                edge_ref[:dirs, here] = swap_ref[c, pl.ds((at + r) * pitch, dirs), :]
            for n, level in enumerate((cg_ref[0], turn_ref[0], mask_ref[...])):
                edge_ref[dirs + n : dirs + n + 1, :] = level[low + r : low + r + 1].astype(jnp.float32)
            out_ref[r, 0] = edge_ref[...].astype(jnp.bfloat16)

    def turns_up(t, c):
        return turn_ref[0, span(t), lanes[c]] >= 4

    def store_first(t, d, c, value):
        first_ref[d, span(t), lanes[c]] = value

    def store_last(t, d, c, value):
        home_ref[0, d, span(t), lanes[c]] = value
        if chunk:
            swap_ref[c, pl.ds(t * TILE * pitch + d, TILE, stride=pitch), :] = value

    step = functools.partial(sweep, dirs, tiles, False, lanes, sign_ref, along_ref, (cel_ref, base_ref, trn_ref), turns_up)
    step(lambda t, d, here: forcing_ref[0, d, span(t), here], store_first)
    step(lambda t, d, here: first_ref[d, span(t), here], store_last)
    if chunk:
        emit(own_ref[0], parts, local, chunk, dirs, lanes, swap_ref, refs[3 : sends + 3])


def inner(own, signs, along, after, forcing, cg, turn, mask, into, parts, chunk, group):
    freqs, dirs, rows, cols = forcing.shape
    begin, many = group
    local = rows // parts
    smem = pl.BlockSpec(memory_space=pltpu.SMEM)
    levels = pl.BlockSpec((1, rows, cols), lambda f: (begin + f, 0, 0))
    block = pl.BlockSpec((1, dirs, rows, cols), lambda f: (begin + f, 0, 0, 0))
    edge = pl.BlockSpec((HALO, 1, dirs + TILE, cols), lambda f: (0, begin + f, 0, 0))
    edge_shape = jax.ShapeDtypeStruct((HALO, freqs, dirs + TILE, cols), jnp.bfloat16)
    coefs = pltpu.VMEM((rows, cols), jnp.float32)
    sends = parts if chunk else 0
    count = chunk[2] if chunk else 0
    outs = pl.pallas_call(
        functools.partial(inner_kernel, parts, local, chunk, into is not None),
        grid=(many,),
        in_specs=[smem, smem, smem, UNREAD, block, levels, levels, pl.BlockSpec((rows, cols), lambda f: (0, 0))]
        + ([] if into is None else [UNREAD] * 3),
        out_specs=[block, edge, edge] + [pl.BlockSpec((count, 1, dirs, cols), lambda f: (0, f, 0, 0))] * sends,
        out_shape=[jax.ShapeDtypeStruct(forcing.shape, jnp.float32), edge_shape, edge_shape]
        + [jax.ShapeDtypeStruct((count, many, dirs, cols), jnp.bfloat16)] * sends,
        scratch_shapes=[
            coefs,
            coefs,
            coefs,
            pltpu.VMEM((dirs, rows, cols), jnp.float32),
            pltpu.VMEM((cols // LANES, rows * (dirs + 1), LANES), jnp.float32),
            pltpu.VMEM((dirs + TILE, cols), jnp.float32),
        ],
        input_output_aliases={} if into is None else {8: 0, 9: 1, 10: 2},
        compiler_params=pltpu.CompilerParams(vmem_limit_bytes=VMEM_LIMIT),
        cost_estimate=COST,
    )(own, signs, along, after, forcing, cg, turn, mask, *([] if into is None else into))
    return outs[:3], list(outs[3:])


def outer_kernel(parts, local, chunk, *refs):
    own_ref, sign_ref, along_ref, _, above_ref, below_ref, cg_ref, turn_ref, mask_ref, home_ref, share_ref = refs[:11]
    send_refs = refs[11 : 11 + parts]
    cel_ref, base_ref, trn_ref, up_ref, lev_ref, near_ref, first_ref, side_ref, edge_ref, swap_ref = refs[11 + parts :]
    dirs, rows, cols = home_ref.shape[1:]
    freqs = share_ref.shape[0]
    pitch = dirs + 1
    lanes = lane_tiles(cols)
    tiles = rows // TILE
    f = pl.program_id(0)

    def span(t):
        return pl.ds(t * TILE, TILE)

    @pl.when(f == 0)
    def _():
        edge_ref[...] = jnp.zeros_like(edge_ref)
        beyond = ((above_ref, 0, 0), (above_ref, 1, 1), (below_ref, 0, TILE - HALO), (below_ref, 1, TILE - 1))
        for n in range(freqs):
            for i, (ref, r, low) in enumerate(beyond):
                for c, here in enumerate(lanes):
                    piece = ref[r, n, :, here].astype(jnp.float32)
                    edge_ref[c, pl.ds(low * pitch, dirs), :] = piece[:dirs]
                    lev_ref[i * TILE : (i + 1) * TILE, here] = piece[dirs:]

            def gather(d, carry, n=n):
                for c, here in enumerate(lanes):
                    side_ref[d, span(n), here] = edge_ref[c, pl.ds(d, TILE, stride=pitch), :]
                return carry

            lax.fori_loop(0, dirs, gather, 0, unroll=12)
            for q, mine in enumerate((cg_ref[n], turn_ref[n], mask_ref[...])):
                for i, (_, _, low) in enumerate(beyond):
                    near_ref[q * TILE + low : q * TILE + low + 1, :] = lev_ref[i * TILE + q : i * TILE + q + 1, :]
                near_ref[q * TILE + HALO : q * TILE + 2 * HALO, :] = mine[:HALO].astype(jnp.float32)
                near_ref[q * TILE + 2 * HALO : q * TILE + 3 * HALO, :] = mine[rows - HALO :].astype(jnp.float32)
            coefficients(cel_ref, base_ref, trn_ref, span(n), *[near_ref[span(q), :] for q in range(3)])
            up_ref[span(n), :] = near_ref[span(1), :]

        def turns_up(t, c):
            return up_ref[span(t), lanes[c]] >= 4.0

        def store_first(t, d, c, value):
            first_ref[d, span(t), lanes[c]] = value

        def store_last(t, d, c, value):
            share_ref[t, d, :, lanes[c]] = value

        step = functools.partial(sweep, dirs, freqs, True, lanes, sign_ref, along_ref, (cel_ref, base_ref, trn_ref), turns_up)
        step(lambda t, d, here: side_ref[d, span(t), here], store_first)
        step(lambda t, d, here: first_ref[d, span(t), here], store_last)

    def whole(d, carry):
        for t in range(tiles):
            for c, here in enumerate(lanes):
                value = with_share(home_ref[0, d, span(t), here], share_ref, f, d, here, t, tiles)
                swap_ref[c, pl.ds(t * TILE * pitch + d, TILE, stride=pitch), :] = value
        return carry

    lax.fori_loop(0, dirs, whole, 0, unroll=4)
    emit(own_ref[0], parts, local, chunk, dirs, lanes, swap_ref, send_refs)


def with_share(value, share_ref, f, d, here, t, tiles):
    row = lax.broadcasted_iota(jnp.int32, value.shape, 0)
    if t == 0:
        value = value + jnp.where(row < HALO, pltpu.roll(share_ref[f, d, :, here], TILE - HALO, 0), 0.0)
    if t == tiles - 1:
        value = value + jnp.where(row >= TILE - HALO, pltpu.roll(share_ref[f, d, :, here], HALO, 0), 0.0)
    return value


def outer(own, signs, along, after, above, below, cg, turn, mask, home, parts, chunk):
    freqs, dirs, rows, cols = home.shape
    local = rows // parts
    smem = pl.BlockSpec(memory_space=pltpu.SMEM)
    edge = pl.BlockSpec((HALO, freqs, dirs + TILE, cols), lambda f: (0, 0, 0, 0))
    levels = pl.BlockSpec((freqs, rows, cols), lambda f: (0, 0, 0))
    tall = pltpu.VMEM((freqs * TILE, cols), jnp.float32)
    outs = pl.pallas_call(
        functools.partial(outer_kernel, parts, local, chunk),
        grid=(freqs,),
        in_specs=[smem, smem, smem, UNREAD, edge, edge, levels, levels]
        + [pl.BlockSpec((rows, cols), lambda f: (0, 0)), pl.BlockSpec((1, dirs, rows, cols), lambda f: (f, 0, 0, 0))],
        out_specs=[pl.BlockSpec((freqs, dirs, TILE, cols), lambda f: (0, 0, 0, 0))]
        + [pl.BlockSpec((chunk[2], 1, dirs, cols), lambda f: (0, f, 0, 0))] * parts,
        out_shape=[jax.ShapeDtypeStruct((freqs, dirs, TILE, cols), jnp.float32)]
        + [jax.ShapeDtypeStruct((chunk[2], freqs, dirs, cols), jnp.bfloat16)] * parts,
        scratch_shapes=[
            tall,
            tall,
            tall,
            tall,
            pltpu.VMEM((2 * HALO * TILE, cols), jnp.float32),
            pltpu.VMEM((3 * TILE, cols), jnp.float32),
            pltpu.VMEM((dirs, freqs * TILE, cols), jnp.float32),
            pltpu.VMEM((dirs, freqs * TILE, cols), jnp.float32),
            pltpu.VMEM((cols // LANES, TILE * (dirs + 1), LANES), jnp.float32),
            pltpu.VMEM((cols // LANES, rows * (dirs + 1), LANES), jnp.float32),
        ],
        compiler_params=pltpu.CompilerParams(vmem_limit_bytes=VMEM_LIMIT),
        cost_estimate=LONG,
    )(own, signs, along, after, above, below, cg, turn, mask, home)
    return outs[0], list(outs[1:])


def by_row_kernel(_, state_ref, out_ref, swap_ref):
    deep, local, _ = state_ref.shape
    pitch = deep + 1

    def body(d, carry):
        swap_ref[pl.ds(d, local, stride=pitch), :] = state_ref[d].astype(jnp.float32)
        return carry

    lax.fori_loop(0, deep, body, 0, unroll=64)
    for r in range(local):
        out_ref[r] = swap_ref[pl.ds(r * pitch, deep), :].astype(jnp.bfloat16)


def by_row(after, state):
    deep, local, cols = state.shape
    return pl.pallas_call(
        by_row_kernel,
        grid=(cols // LANES,),
        in_specs=[UNREAD, pl.BlockSpec((deep, local, LANES), lambda c: (0, 0, c))],
        out_specs=pl.BlockSpec((local, deep, LANES), lambda c: (0, 0, c)),
        out_shape=jax.ShapeDtypeStruct((local, deep, cols), jnp.bfloat16),
        scratch_shapes=[pltpu.VMEM((local * (deep + 1), LANES), jnp.float32)],
        compiler_params=pltpu.CompilerParams(vmem_limit_bytes=VMEM_LIMIT),
        cost_estimate=COST,
    )(after, state)


def turned_kernel(_, w_in_ref, w_out_ref, in_t_ref, out_t_ref):
    in_t_ref[...] = w_in_ref[...].T
    out_t_ref[...] = w_out_ref[...].T


def turned(after, w_in, w_out):
    hidden, total = w_in.shape
    step = 512
    tall = pl.BlockSpec((step, total), lambda h: (h, 0))
    wide = pl.BlockSpec((total, step), lambda h: (0, h))
    return pl.pallas_call(
        turned_kernel,
        grid=(hidden // step,),
        in_specs=[UNREAD, tall, wide],
        out_specs=[wide, tall],
        out_shape=[jax.ShapeDtypeStruct((total, hidden), w_in.dtype), jax.ShapeDtypeStruct((hidden, total), w_in.dtype)],
        compiler_params=pltpu.CompilerParams(vmem_limit_bytes=VMEM_LIMIT),
        cost_estimate=COST,
    )(after, w_in, w_out)


def source_kernel(parts, got, sent, dirs, step, own_ref, _, state_ref, wind_ref, w_in_ref, out_t_ref, in_t_ref, weight_ref, *refs):
    cell_refs = refs[: parts * len(got)]
    grad_ref = refs[parts * len(got)]
    back_refs = refs[parts * len(got) + 1 : -3]
    cell_ref, weighted_ref, grown_ref = refs[-3:]
    freqs = sum(many for _, many in got)
    hidden, width = weighted_ref.shape
    own = own_ref[0]

    def place(k, group):
        begin, many = group
        return pl.ds(pl.multiple_of(((own ^ k) * freqs + begin) * dirs, TILE), many * dirs)

    for g, group in enumerate(got):
        for k in range(parts):
            piece = cell_refs[g * parts + k][0].astype(jnp.float32)
            cell_ref[place(k, group), :] = piece.reshape(group[1] * dirs, width)
    cell = cell_ref[...].astype(jnp.bfloat16)
    state = state_ref[0]
    wind = wind_ref[0]
    grad = jnp.zeros((TILE, width), jnp.float32)
    for h in range(0, hidden, step):
        some = pl.ds(h, step)
        weight = weight_ref[some, :]
        forward = jnp.dot(w_in_ref[some, :], state, preferred_element_type=jnp.float32) + weight * wind
        squash = jnp.tanh(forward)
        pulled = jnp.dot(out_t_ref[some, :], cell, preferred_element_type=jnp.float32)
        weighted = (1.0 - squash * squash) * pulled
        weighted_ref[some, :] = weighted.astype(jnp.bfloat16)
        grad = grad + jnp.sum((weight * weighted).reshape(step // TILE, TILE, width), axis=0)
    grad_ref[0] = jnp.sum(grad, axis=0, keepdims=True)
    grown_ref[...] = jnp.dot(in_t_ref[...], weighted_ref[...], preferred_element_type=jnp.float32)
    for g, group in enumerate(sent):
        for k in range(parts):
            grown = grown_ref[place(k, group), :].reshape(group[1], dirs, width)
            back_refs[g * parts + k][0] = grown.astype(jnp.bfloat16)


def source_term(own, after, state, wind, w_in, out_t, in_t, weight, cells, got, sent, rows, chunk):
    parts = len(cells[0])
    _, _, dirs, cols = cells[0][0].shape
    first, count = rows
    hidden, total = w_in.shape
    width = min(cols, 512)

    def row_of(j, own_ref):
        return chunk_row(own_ref[0], first + j, chunk)

    def whole(shape):
        return pl.BlockSpec(shape, lambda j, c, own_ref: (0, 0))

    cell_specs = [
        pl.BlockSpec((1, many, dirs, width), lambda j, c, own_ref: (first + j, 0, 0, c)) for _, many in got for _ in range(parts)
    ]
    back_specs = [pl.BlockSpec((1, many, dirs, width), lambda j, c, own_ref: (j, 0, 0, c)) for _, many in sent for _ in range(parts)]
    outs = pl.pallas_call(
        functools.partial(source_kernel, parts, got, sent, dirs, 256),
        grid_spec=pltpu.PrefetchScalarGridSpec(
            num_scalar_prefetch=1,
            grid=(count, cols // width),
            in_specs=[
                UNREAD,
                pl.BlockSpec((1, total, width), lambda j, c, own_ref: (row_of(j, own_ref), 0, c)),
                pl.BlockSpec((1, 1, width), lambda j, c, own_ref: (row_of(j, own_ref), 0, c)),
                whole((hidden, total)),
                whole((hidden, total)),
                whole((total, hidden)),
                whole((hidden, 1)),
            ]
            + cell_specs,
            out_specs=[pl.BlockSpec((1, 1, width), lambda j, c, own_ref: (j, 0, c))] + back_specs,
            scratch_shapes=[
                pltpu.VMEM((total, width), jnp.float32),
                pltpu.VMEM((hidden, width), jnp.bfloat16),
                pltpu.VMEM((total, width), jnp.float32),
            ],
        ),
        out_shape=[jax.ShapeDtypeStruct((count, 1, cols), jnp.float32)]
        + [jax.ShapeDtypeStruct((count, many, dirs, cols), jnp.bfloat16) for _, many in sent for _ in range(parts)],
        compiler_params=pltpu.CompilerParams(vmem_limit_bytes=VMEM_LIMIT),
        cost_estimate=COST,
    )(own, after, state, wind, w_in, out_t, in_t, weight, *[cell for group in cells for cell in group])
    return outs[0], [list(outs[1 + g * parts : 1 + (g + 1) * parts]) for g in range(len(sent))]


def join_kernel(parts, spans, own_ref, _, home_ref, share_ref, *refs):
    out_ref, swap_ref = refs[-2:]
    dirs, rows, cols = home_ref.shape[1:]
    pitch = dirs + 1
    local = rows // parts
    own = own_ref[0]
    lanes = lane_tiles(cols)
    tiles = rows // TILE
    for i, (first, count, chunk) in enumerate(spans):
        for k in range(parts):
            owner = own ^ k
            for j in range(count):
                start = (owner * local + chunk_row(owner, first + j, chunk)) * pitch
                for c, here in enumerate(lanes):
                    swap_ref[c, pl.ds(start, dirs), :] = refs[i * parts + k][j, 0, :, here].astype(jnp.float32)

    def body(d, carry):
        for t in range(tiles):
            for c, here in enumerate(lanes):
                grown = swap_ref[c, pl.ds(t * TILE * pitch + d, TILE, stride=pitch), :]
                value = with_share(home_ref[0, d, pl.ds(t * TILE, TILE), here], share_ref, 0, d, here, t, tiles)
                out_ref[0, d, pl.ds(t * TILE, TILE), here] = value + grown
        return carry

    lax.fori_loop(0, dirs, body, 0, unroll=12)


def join(own, into, home, share, early, late, rows_of, chunks, group):
    begin, many = group
    parts = len(late)
    _, dirs, rows, cols = home.shape
    last = late[0].shape[0]
    spans = [(*span, chunks[0]) for span in rows_of] + [(0, last, chunks[-1])]
    width = min(cols, 256)
    block = pl.BlockSpec((1, dirs, rows, width), lambda f, c: (begin + f, 0, 0, c))
    specs = [
        pl.BlockSpec((count, 1, dirs, width), lambda f, c: (0, begin + f, 0, c)) for _, count in rows_of for _ in range(parts)
    ] + [pl.BlockSpec((last, 1, dirs, width), lambda f, c: (0, f, 0, c))] * parts
    return pl.pallas_call(
        functools.partial(join_kernel, parts, spans),
        grid=(many, cols // width),
        in_specs=[pl.BlockSpec(memory_space=pltpu.SMEM), UNREAD, block]
        + [pl.BlockSpec((1, dirs, TILE, width), lambda f, c: (begin + f, 0, 0, c))]
        + specs,
        out_specs=block,
        out_shape=jax.ShapeDtypeStruct(home.shape, jnp.float32),
        scratch_shapes=[pltpu.VMEM((width // LANES, rows * (dirs + 1), LANES), jnp.float32)],
        input_output_aliases={} if begin == 0 else {1: 0},
        compiler_params=pltpu.CompilerParams(vmem_limit_bytes=VMEM_LIMIT),
        cost_estimate=COST,
    )(own, into, home, share, *[piece for pieces in early for piece in pieces], *late)


def arrived_kernel(held, *refs):
    refs[-1][...] = jnp.zeros_like(refs[-1])


def arrived(after, pieces, held=()):
    outs = pl.pallas_call(
        functools.partial(arrived_kernel, len(held)),
        in_specs=[UNREAD] * (1 + len(pieces) + len(held)),
        out_specs=[UNREAD] * len(held) + [pl.BlockSpec(memory_space=pltpu.VMEM)],
        out_shape=[jax.ShapeDtypeStruct(h.shape, h.dtype) for h in held] + [jax.ShapeDtypeStruct((TILE, LANES), jnp.float32)],
        input_output_aliases={1 + len(pieces) + i: i for i in range(len(held))},
        cost_estimate=COST,
    )(after, *pieces, *held)
    return outs[-1], list(outs[:-1])


def swapped(pieces):
    parts = len(pieces)
    moved = {k: lax.ppermute(pieces[k], "comp", [(i, i ^ k) for i in range(parts)]) for k in range(parts - 1, 0, -1)}
    return [pieces[0]] + [moved[k] for k in range(1, parts)]


def across(low, high):
    count = lax.axis_size("space")
    up = [(i, i + 1) for i in range(count - 1)]
    down = [(i + 1, i) for i in range(count - 1)]
    return lax.ppermute(high, "space", up), lax.ppermute(low, "space", down)


def halves(count):
    spans, begin = [], 0
    while begin < count:
        many = max(1, (count - begin) // 2)
        spans.append((begin, many))
        begin += many
    return spans


def shards(
    adjoint_forcing,
    forward_state,
    wind_speed,
    cg_index,
    turn_index,
    sea_mask,
    dir_sign,
    w_in,
    w_out,
    wind_weight,
):
    parts = lax.axis_size("comp")
    own_place = lax.axis_index("comp")
    own = own_place.astype(jnp.int32).reshape(1)
    dirs = dir_sign.shape[1]
    comps, rows, cols = adjoint_forcing.shape
    freqs = comps // dirs
    local = rows // parts
    along = jnp.asarray(direction_factors(dirs))
    forcing = adjoint_forcing.reshape(freqs, dirs, rows, cols)
    weight = wind_weight[:, None]
    wind = wind_speed[:, None]
    everything = [(0, freqs)]
    many = freqs // 2 if freqs % 2 == 0 else freqs
    groups = [(begin, many) for begin in range(0, freqs, many)]
    sent = halves(freqs)
    levels = (cg_index, turn_index, sea_mask)
    if local > HALO:
        chunks = [(HALO, 0, local - HALO), (0, local - HALO, HALO)]
    else:
        chunks = [(0, 0, local)]
    ahead = chunks[0] if len(chunks) > 1 else None

    early, into, after = [], None, sea_mask
    for group in groups:
        into, pieces = inner(own, dir_sign, along, after, forcing, *levels, into, parts, ahead, group)
        if ahead:
            early.append(swapped(pieces))
    home, low, high = into
    above, below = across(low, high)
    after = arrived(home, early[0][1:])[0] if len(early) > 1 else home
    state = by_row(after, forward_state)
    in_t, out_t = turned(state, w_in, w_out)
    share, pieces = outer(own, dir_sign, along, in_t, above, below, *levels, home, parts, chunks[-1])
    late = swapped(pieces)
    term = functools.partial(source_term, own)
    fixed = (state, wind, w_in, out_t, in_t, weight)
    after, grads, early_back, rows_of = share, [], [], []
    if ahead:
        count = ahead[2]
        rows_of = [(0, count // 2), (count // 2, count - count // 2)] if count > 1 else [(0, count)]
    for span in rows_of:
        grad, [back] = term(after, *fixed, early, groups, everything, span, ahead)
        after = grad
        if not grads:
            after, rest = arrived(grad, late[1:], back[1:])
            back = [back[0], *rest]
        grads.append(grad)
        early_back.append(swapped(back))
    late_grad, late_back = term(after, *fixed, [late], everything, sent, (0, chunks[-1][2]), chunks[-1])
    start, returned = late_grad, []
    for g, pieces in enumerate(late_back):
        if g < len(early_back):
            rest = [piece for group in late_back[g:] for piece in group[1:]]
            start, rest = arrived(start, early_back[g][1:], rest)
            for n, group in enumerate(late_back[g:]):
                late_back[g + n] = [group[0], *rest[n * (parts - 1) : (n + 1) * (parts - 1)]]
        returned.append(swapped(late_back[g]))
    late_back = returned
    for group, back in zip(sent, late_back, strict=True):
        start = join(own, start, home, share, early_back, back, rows_of, chunks, group)
    gradient = jnp.where(
        own_place == 0, jnp.concatenate([late_grad, *grads], axis=0), jnp.concatenate([*grads, late_grad], axis=0)
    )
    return (start.reshape(comps, rows, cols), gradient.reshape(wind_speed.shape))


def solution(mesh):
    placed = (
        P("comp", "space", None),
        P(None, ("space", "comp"), None),
        P(("space", "comp"), None),
        P("comp", "space", None),
        P("comp", "space", None),
        P("space", None),
        P(),
        P(),
        P(),
        P(),
    )
    return jax.shard_map(
        shards,
        mesh=mesh,
        in_specs=placed,
        out_specs=(P("comp", "space", None), P(("space", "comp"), None)),
        check_vma=False,
    )
```

```python
import functools
import math

import jax
import jax.numpy as jnp
import numpy as np
from jax import lax
from jax.experimental import pallas as pl
from jax.experimental.pallas import tpu as pltpu
from jax.sharding import PartitionSpec as P

HALO = 2
TILE = 8
LANES = 128
MIB = 1 << 20
VMEM_LIMIT = 60 * MIB
COST = pl.CostEstimate(flops=1, bytes_accessed=1, transcendentals=0)
LONG = pl.CostEstimate(flops=10**11, bytes_accessed=100 * MIB, transcendentals=0)


def direction_factors(dirs):
    angle = (np.arange(dirs, dtype=np.float32) + np.float32(0.5)) * np.float32(2.0 * math.pi / dirs)
    return np.stack([np.float32(0.5) * np.abs(np.cos(angle)), np.float32(0.5) * np.abs(np.sin(angle))])


def chunk_row(owner, j, chunk):
    return jnp.where(owner == 0, chunk[0], chunk[1]) + j


UNREAD = pl.BlockSpec(memory_space=pl.ANY)


def lane_tiles(cols):
    return [pl.ds(c * LANES, LANES) for c in range(cols // LANES)]


def coefficients(cel_ref, base_ref, trn_ref, here, cg, turn, sea):
    sea = sea.astype(jnp.float32)
    celerity = 0.1 + 0.8 * cg.astype(jnp.float32) / 7.0
    turning = 0.3 * jnp.abs(turn.astype(jnp.float32) - 3.5) / 3.5
    cel_ref[here, :] = celerity * sea
    base_ref[here, :] = (1.0 - turning) * sea
    trn_ref[here, :] = turning * sea


def sweep(dirs, tiles, alone, lanes, sign_ref, along_ref, coefs, turns_up, load, store):
    cel_ref, base_ref, trn_ref = coefs
    row = lax.broadcasted_iota(jnp.int32, (TILE, LANES), 0)
    lane = lax.broadcasted_iota(jnp.int32, (TILE, LANES), 1)
    nothing = jnp.zeros((TILE, LANES), jnp.float32)

    def span(t):
        return pl.ds(t * TILE, TILE)

    def one(d, carry):
        following = jnp.where(d == dirs - 1, 0, d + 1)
        previous = jnp.where(d == 0, dirs - 1, d - 1)
        ax = along_ref[0, d]
        ay = along_ref[1, d]
        right = sign_ref[0, d] > 0
        high = sign_ref[1, d] > 0
        shift_x = jnp.where(right, LANES - 1, 1)
        shift_y = jnp.where(high, TILE - 1, 1)
        at_right = lane == jnp.where(right, LANES - 1, LANES)
        at_left = lane == jnp.where(right, LANES, 0)
        at_high = row == jnp.where(high, TILE - 1, TILE)
        at_low = row == jnp.where(high, TILE, 0)
        at_edge = row == jnp.where(high, TILE - 1, 0)

        def column(c):
            here = [load(t, d, lanes[c]) for t in range(tiles)]
            flow = [cel_ref[span(t), lanes[c]] * here[t] for t in range(tiles)]
            return here, flow, [pltpu.roll(f, shift_x, 1) for f in flow]

        before = [nothing] * tiles
        here, flow, moved = column(0)
        for c in range(len(lanes)):
            beyond = [nothing] * tiles
            if c + 1 < len(lanes):
                later = column(c + 1)
                beyond = later[2]
            lifted = [pltpu.roll(f, shift_y, 0) for f in flow]
            for t in range(tiles):
                flow_x = jnp.where(at_right, beyond[t], jnp.where(at_left, before[t], moved[t]))
                if alone:
                    flow_y = jnp.where(at_edge, nothing, lifted[t])
                else:
                    above = lifted[t + 1] if t + 1 < tiles else nothing
                    below = lifted[t - 1] if t > 0 else nothing
                    flow_y = jnp.where(at_high, above, jnp.where(at_low, below, lifted[t]))
                turned = jnp.where(turns_up(t, c), load(t, following, lanes[c]), load(t, previous, lanes[c]))
                total = base_ref[span(t), lanes[c]] * here[t] + ax * (flow_x - flow[t])
                total = total + ay * (flow_y - flow[t]) + trn_ref[span(t), lanes[c]] * turned
                store(t, d, c, total)
            if c + 1 < len(lanes):
                before = moved
                here, flow, moved = later
        return carry

    lax.fori_loop(0, dirs, one, 0, unroll=6)


def emit(own, parts, local, chunk, dirs, lanes, swap_ref, send_refs):
    for k in range(parts):
        owner = own ^ k
        for j in range(chunk[2]):
            start = (owner * local + chunk_row(owner, j, chunk)) * (dirs + 1)
            for c, here in enumerate(lanes):
                send_refs[k][j, 0, :, here] = swap_ref[c, pl.ds(start, dirs), :].astype(jnp.bfloat16)


def inner_kernel(parts, local, chunk, into, own_ref, sign_ref, along_ref, _, forcing_ref, cg_ref, turn_ref, mask_ref, *refs):
    refs = refs[3:] if into else refs
    home_ref, first_out, last_out = refs[:3]
    sends = parts if chunk else 0
    cel_ref, base_ref, trn_ref, first_ref, swap_ref, edge_ref = refs[sends + 3 :]
    dirs, rows, cols = forcing_ref.shape[1:]
    pitch = dirs + 1
    lanes = lane_tiles(cols)
    tiles = rows // TILE

    def span(t):
        return pl.ds(t * TILE, TILE)

    for t in range(tiles):
        levels = (cg_ref[0, span(t), :], turn_ref[0, span(t), :], mask_ref[span(t), :])
        coefficients(cel_ref, base_ref, trn_ref, span(t), *levels)

    def outermost(d, carry):
        for side, t in enumerate((0, tiles - 1)):
            for c, here in enumerate(lanes):
                swap_ref[c, pl.ds(side * TILE * pitch + d, TILE, stride=pitch), :] = forcing_ref[0, d, span(t), here]
        return carry

    lax.fori_loop(0, dirs, outermost, 0, unroll=8)
    edge_ref[...] = jnp.zeros_like(edge_ref)
    for out_ref, low, at in ((first_out, 0, 0), (last_out, rows - HALO, 2 * TILE - HALO)):
        for r in range(HALO):
            for c, here in enumerate(lanes):
                edge_ref[:dirs, here] = swap_ref[c, pl.ds((at + r) * pitch, dirs), :]
            for n, level in enumerate((cg_ref[0], turn_ref[0], mask_ref[...])):
                edge_ref[dirs + n : dirs + n + 1, :] = level[low + r : low + r + 1].astype(jnp.float32)
            out_ref[r, 0] = edge_ref[...].astype(jnp.bfloat16)

    def turns_up(t, c):
        return turn_ref[0, span(t), lanes[c]] >= 4

    def store_first(t, d, c, value):
        first_ref[d, span(t), lanes[c]] = value

    def store_last(t, d, c, value):
        home_ref[0, d, span(t), lanes[c]] = value
        if chunk:
            swap_ref[c, pl.ds(t * TILE * pitch + d, TILE, stride=pitch), :] = value

    step = functools.partial(sweep, dirs, tiles, False, lanes, sign_ref, along_ref, (cel_ref, base_ref, trn_ref), turns_up)
    step(lambda t, d, here: forcing_ref[0, d, span(t), here], store_first)
    step(lambda t, d, here: first_ref[d, span(t), here], store_last)
    if chunk:
        emit(own_ref[0], parts, local, chunk, dirs, lanes, swap_ref, refs[3 : sends + 3])


def inner(own, signs, along, after, forcing, cg, turn, mask, into, parts, chunk, group):
    freqs, dirs, rows, cols = forcing.shape
    begin, many = group
    local = rows // parts
    smem = pl.BlockSpec(memory_space=pltpu.SMEM)
    levels = pl.BlockSpec((1, rows, cols), lambda f: (begin + f, 0, 0))
    block = pl.BlockSpec((1, dirs, rows, cols), lambda f: (begin + f, 0, 0, 0))
    edge = pl.BlockSpec((HALO, 1, dirs + TILE, cols), lambda f: (0, begin + f, 0, 0))
    edge_shape = jax.ShapeDtypeStruct((HALO, freqs, dirs + TILE, cols), jnp.bfloat16)
    coefs = pltpu.VMEM((rows, cols), jnp.float32)
    sends = parts if chunk else 0
    count = chunk[2] if chunk else 0
    outs = pl.pallas_call(
        functools.partial(inner_kernel, parts, local, chunk, into is not None),
        grid=(many,),
        in_specs=[smem, smem, smem, UNREAD, block, levels, levels, pl.BlockSpec((rows, cols), lambda f: (0, 0))]
        + ([] if into is None else [UNREAD] * 3),
        out_specs=[block, edge, edge] + [pl.BlockSpec((count, 1, dirs, cols), lambda f: (0, f, 0, 0))] * sends,
        out_shape=[jax.ShapeDtypeStruct(forcing.shape, jnp.float32), edge_shape, edge_shape]
        + [jax.ShapeDtypeStruct((count, many, dirs, cols), jnp.bfloat16)] * sends,
        scratch_shapes=[
            coefs,
            coefs,
            coefs,
            pltpu.VMEM((dirs, rows, cols), jnp.float32),
            pltpu.VMEM((cols // LANES, rows * (dirs + 1), LANES), jnp.float32),
            pltpu.VMEM((dirs + TILE, cols), jnp.float32),
        ],
        input_output_aliases={} if into is None else {8: 0, 9: 1, 10: 2},
        compiler_params=pltpu.CompilerParams(vmem_limit_bytes=VMEM_LIMIT),
        cost_estimate=COST,
    )(own, signs, along, after, forcing, cg, turn, mask, *([] if into is None else into))
    return outs[:3], list(outs[3:])


def outer_kernel(parts, local, chunk, *refs):
    own_ref, sign_ref, along_ref, _, above_ref, below_ref, cg_ref, turn_ref, mask_ref, home_ref, share_ref = refs[:11]
    send_refs = refs[11 : 11 + parts]
    cel_ref, base_ref, trn_ref, up_ref, lev_ref, near_ref, first_ref, side_ref, edge_ref, swap_ref = refs[11 + parts :]
    dirs, rows, cols = home_ref.shape[1:]
    freqs = share_ref.shape[0]
    pitch = dirs + 1
    lanes = lane_tiles(cols)
    tiles = rows // TILE
    f = pl.program_id(0)

    def span(t):
        return pl.ds(t * TILE, TILE)

    @pl.when(f == 0)
    def _():
        edge_ref[...] = jnp.zeros_like(edge_ref)
        beyond = ((above_ref, 0, 0), (above_ref, 1, 1), (below_ref, 0, TILE - HALO), (below_ref, 1, TILE - 1))
        for n in range(freqs):
            for i, (ref, r, low) in enumerate(beyond):
                for c, here in enumerate(lanes):
                    piece = ref[r, n, :, here].astype(jnp.float32)
                    edge_ref[c, pl.ds(low * pitch, dirs), :] = piece[:dirs]
                    lev_ref[i * TILE : (i + 1) * TILE, here] = piece[dirs:]

            def gather(d, carry, n=n):
                for c, here in enumerate(lanes):
                    side_ref[d, span(n), here] = edge_ref[c, pl.ds(d, TILE, stride=pitch), :]
                return carry

            lax.fori_loop(0, dirs, gather, 0, unroll=12)
            for q, mine in enumerate((cg_ref[n], turn_ref[n], mask_ref[...])):
                for i, (_, _, low) in enumerate(beyond):
                    near_ref[q * TILE + low : q * TILE + low + 1, :] = lev_ref[i * TILE + q : i * TILE + q + 1, :]
                near_ref[q * TILE + HALO : q * TILE + 2 * HALO, :] = mine[:HALO].astype(jnp.float32)
                near_ref[q * TILE + 2 * HALO : q * TILE + 3 * HALO, :] = mine[rows - HALO :].astype(jnp.float32)
            coefficients(cel_ref, base_ref, trn_ref, span(n), *[near_ref[span(q), :] for q in range(3)])
            up_ref[span(n), :] = near_ref[span(1), :]

        def turns_up(t, c):
            return up_ref[span(t), lanes[c]] >= 4.0

        def store_first(t, d, c, value):
            first_ref[d, span(t), lanes[c]] = value

        def store_last(t, d, c, value):
            share_ref[t, d, :, lanes[c]] = value

        step = functools.partial(sweep, dirs, freqs, True, lanes, sign_ref, along_ref, (cel_ref, base_ref, trn_ref), turns_up)
        step(lambda t, d, here: side_ref[d, span(t), here], store_first)
        step(lambda t, d, here: first_ref[d, span(t), here], store_last)

    def whole(d, carry):
        for t in range(tiles):
            for c, here in enumerate(lanes):
                value = with_share(home_ref[0, d, span(t), here], share_ref, f, d, here, t, tiles)
                swap_ref[c, pl.ds(t * TILE * pitch + d, TILE, stride=pitch), :] = value
        return carry

    lax.fori_loop(0, dirs, whole, 0, unroll=4)
    emit(own_ref[0], parts, local, chunk, dirs, lanes, swap_ref, send_refs)


def with_share(value, share_ref, f, d, here, t, tiles):
    row = lax.broadcasted_iota(jnp.int32, value.shape, 0)
    if t == 0:
        value = value + jnp.where(row < HALO, pltpu.roll(share_ref[f, d, :, here], TILE - HALO, 0), 0.0)
    if t == tiles - 1:
        value = value + jnp.where(row >= TILE - HALO, pltpu.roll(share_ref[f, d, :, here], HALO, 0), 0.0)
    return value


def outer(own, signs, along, after, above, below, cg, turn, mask, home, parts, chunk):
    freqs, dirs, rows, cols = home.shape
    local = rows // parts
    smem = pl.BlockSpec(memory_space=pltpu.SMEM)
    edge = pl.BlockSpec((HALO, freqs, dirs + TILE, cols), lambda f: (0, 0, 0, 0))
    levels = pl.BlockSpec((freqs, rows, cols), lambda f: (0, 0, 0))
    tall = pltpu.VMEM((freqs * TILE, cols), jnp.float32)
    outs = pl.pallas_call(
        functools.partial(outer_kernel, parts, local, chunk),
        grid=(freqs,),
        in_specs=[smem, smem, smem, UNREAD, edge, edge, levels, levels]
        + [pl.BlockSpec((rows, cols), lambda f: (0, 0)), pl.BlockSpec((1, dirs, rows, cols), lambda f: (f, 0, 0, 0))],
        out_specs=[pl.BlockSpec((freqs, dirs, TILE, cols), lambda f: (0, 0, 0, 0))]
        + [pl.BlockSpec((chunk[2], 1, dirs, cols), lambda f: (0, f, 0, 0))] * parts,
        out_shape=[jax.ShapeDtypeStruct((freqs, dirs, TILE, cols), jnp.float32)]
        + [jax.ShapeDtypeStruct((chunk[2], freqs, dirs, cols), jnp.bfloat16)] * parts,
        scratch_shapes=[
            tall,
            tall,
            tall,
            tall,
            pltpu.VMEM((2 * HALO * TILE, cols), jnp.float32),
            pltpu.VMEM((3 * TILE, cols), jnp.float32),
            pltpu.VMEM((dirs, freqs * TILE, cols), jnp.float32),
            pltpu.VMEM((dirs, freqs * TILE, cols), jnp.float32),
            pltpu.VMEM((cols // LANES, TILE * (dirs + 1), LANES), jnp.float32),
            pltpu.VMEM((cols // LANES, rows * (dirs + 1), LANES), jnp.float32),
        ],
        compiler_params=pltpu.CompilerParams(vmem_limit_bytes=VMEM_LIMIT),
        cost_estimate=LONG,
    )(own, signs, along, after, above, below, cg, turn, mask, home)
    return outs[0], list(outs[1:])


def by_row_kernel(*refs):
    state_ref, out_ref, swap_ref = refs[-3:]
    some, local, cols = state_ref.shape
    pitch = some + 1
    lanes = lane_tiles(cols)

    def body(d, carry):
        for c, here in enumerate(lanes):
            swap_ref[c, pl.ds(d, local, stride=pitch), :] = state_ref[d, :, here].astype(jnp.float32)
        return carry

    lax.fori_loop(0, some, body, 0, unroll=8)
    for r in range(local):
        for c, here in enumerate(lanes):
            out_ref[r, :, here] = swap_ref[c, pl.ds(r * pitch, some), :].astype(jnp.bfloat16)


def by_row(after, state):
    deep, local, cols = state.shape
    some = 48
    return pl.pallas_call(
        by_row_kernel,
        grid=(deep // some,),
        in_specs=[UNREAD] * len(after) + [pl.BlockSpec((some, local, cols), lambda d: (d, 0, 0))],
        out_specs=pl.BlockSpec((local, some, cols), lambda d: (0, d, 0)),
        out_shape=jax.ShapeDtypeStruct((local, deep, cols), jnp.bfloat16),
        scratch_shapes=[pltpu.VMEM((cols // LANES, local * (some + 1), LANES), jnp.float32)],
        compiler_params=pltpu.CompilerParams(vmem_limit_bytes=VMEM_LIMIT),
        cost_estimate=COST,
    )(*after, state)


def turned_kernel(_, w_in_ref, w_out_ref, in_t_ref, out_t_ref):
    in_t_ref[...] = w_in_ref[...].T
    out_t_ref[...] = w_out_ref[...].T


def turned(after, w_in, w_out):
    hidden, total = w_in.shape
    step = 512
    tall = pl.BlockSpec((step, total), lambda h: (h, 0))
    wide = pl.BlockSpec((total, step), lambda h: (0, h))
    return pl.pallas_call(
        turned_kernel,
        grid=(hidden // step,),
        in_specs=[UNREAD, tall, wide],
        out_specs=[wide, tall],
        out_shape=[jax.ShapeDtypeStruct((total, hidden), w_in.dtype), jax.ShapeDtypeStruct((hidden, total), w_in.dtype)],
        compiler_params=pltpu.CompilerParams(vmem_limit_bytes=VMEM_LIMIT),
        cost_estimate=LONG,
    )(after, w_in, w_out)


def source_kernel(parts, got, sent, dirs, step, own_ref, _, state_ref, wind_ref, w_in_ref, out_t_ref, in_t_ref, weight_ref, *refs):
    cell_refs = refs[: parts * len(got)]
    grad_ref = refs[parts * len(got)]
    back_refs = refs[parts * len(got) + 1 : -3]
    cell_ref, weighted_ref, grown_ref = refs[-3:]
    freqs = sum(many for _, many in got)
    hidden, width = weighted_ref.shape
    own = own_ref[0]

    def place(k, group):
        begin, many = group
        return pl.ds(pl.multiple_of(((own ^ k) * freqs + begin) * dirs, TILE), many * dirs)

    for g, group in enumerate(got):
        for k in range(parts):
            piece = cell_refs[g * parts + k][0].astype(jnp.float32)
            cell_ref[place(k, group), :] = piece.reshape(group[1] * dirs, width)
    cell = cell_ref[...].astype(jnp.bfloat16)
    state = state_ref[0]
    wind = wind_ref[0]
    grad = jnp.zeros((TILE, width), jnp.float32)
    for h in range(0, hidden, step):
        some = pl.ds(h, step)
        weight = weight_ref[some, :]
        forward = jnp.dot(w_in_ref[some, :], state, preferred_element_type=jnp.float32) + weight * wind
        squash = jnp.tanh(forward)
        pulled = jnp.dot(out_t_ref[some, :], cell, preferred_element_type=jnp.float32)
        weighted = (1.0 - squash * squash) * pulled
        weighted_ref[some, :] = weighted.astype(jnp.bfloat16)
        grad = grad + jnp.sum((weight * weighted).reshape(step // TILE, TILE, width), axis=0)
    grad_ref[0] = jnp.sum(grad, axis=0, keepdims=True)
    grown_ref[...] = jnp.dot(in_t_ref[...], weighted_ref[...], preferred_element_type=jnp.float32)
    for g, group in enumerate(sent):
        for k in range(parts):
            grown = grown_ref[place(k, group), :].reshape(group[1], dirs, width)
            back_refs[g * parts + k][0] = grown.astype(jnp.bfloat16)


def source_term(own, after, state, wind, w_in, out_t, in_t, weight, cells, got, sent, rows, chunk):
    parts = len(cells[0])
    _, _, dirs, cols = cells[0][0].shape
    first, count = rows
    hidden, total = w_in.shape
    width = min(cols, 512)

    def row_of(j, own_ref):
        return chunk_row(own_ref[0], first + j, chunk)

    def whole(shape):
        return pl.BlockSpec(shape, lambda j, c, own_ref: (0, 0))

    cell_specs = [
        pl.BlockSpec((1, many, dirs, width), lambda j, c, own_ref: (first + j, 0, 0, c)) for _, many in got for _ in range(parts)
    ]
    back_specs = [pl.BlockSpec((1, many, dirs, width), lambda j, c, own_ref: (j, 0, 0, c)) for _, many in sent for _ in range(parts)]
    outs = pl.pallas_call(
        functools.partial(source_kernel, parts, got, sent, dirs, 256),
        grid_spec=pltpu.PrefetchScalarGridSpec(
            num_scalar_prefetch=1,
            grid=(count, cols // width),
            in_specs=[
                UNREAD,
                pl.BlockSpec((1, total, width), lambda j, c, own_ref: (row_of(j, own_ref), 0, c)),
                pl.BlockSpec((1, 1, width), lambda j, c, own_ref: (row_of(j, own_ref), 0, c)),
                whole((hidden, total)),
                whole((hidden, total)),
                whole((total, hidden)),
                whole((hidden, 1)),
            ]
            + cell_specs,
            out_specs=[pl.BlockSpec((1, 1, width), lambda j, c, own_ref: (j, 0, c))] + back_specs,
            scratch_shapes=[
                pltpu.VMEM((total, width), jnp.float32),
                pltpu.VMEM((hidden, width), jnp.bfloat16),
                pltpu.VMEM((total, width), jnp.float32),
            ],
        ),
        out_shape=[jax.ShapeDtypeStruct((count, 1, cols), jnp.float32)]
        + [jax.ShapeDtypeStruct((count, many, dirs, cols), jnp.bfloat16) for _, many in sent for _ in range(parts)],
        compiler_params=pltpu.CompilerParams(vmem_limit_bytes=VMEM_LIMIT),
        cost_estimate=COST,
    )(own, after, state, wind, w_in, out_t, in_t, weight, *[cell for group in cells for cell in group])
    return outs[0], [list(outs[1 + g * parts : 1 + (g + 1) * parts]) for g in range(len(sent))]


def join_kernel(parts, local, spans, own_ref, _, home_ref, share_ref, *refs):
    out_ref, swap_ref = refs[-2:]
    dirs, _, cols = home_ref.shape[1:]
    pitch = dirs + 1
    own = own_ref[0]
    lanes = lane_tiles(cols)
    t = pl.program_id(1)
    tiles = pl.num_programs(1)

    @pl.when(t == 0)
    def _():
        for i, (first, count, chunk) in enumerate(spans):
            for k in range(parts):
                owner = own ^ k
                for j in range(count):
                    start = (owner * local + chunk_row(owner, first + j, chunk)) * pitch
                    for c, here in enumerate(lanes):
                        swap_ref[c, pl.ds(start, dirs), :] = refs[i * parts + k][j, 0, :, here].astype(jnp.float32)

    row = lax.broadcasted_iota(jnp.int32, (TILE, LANES), 0)
    reached = ((t == 0) & (row < HALO)) | ((t == tiles - 1) & (row >= TILE - HALO))
    shift = jnp.where(t == 0, TILE - HALO, HALO)

    def body(d, carry):
        for c, here in enumerate(lanes):
            grown = swap_ref[c, pl.ds(t * TILE * pitch + d, TILE, stride=pitch), :]
            shared = jnp.where(reached, pltpu.roll(share_ref[0, d, :, here], shift, 0), 0.0)
            out_ref[0, d, :, here] = home_ref[0, d, :, here] + shared + grown
        return carry

    lax.fori_loop(0, dirs, body, 0, unroll=8)


def join(own, into, home, share, early, late, rows_of, chunks, group):
    begin, many = group
    parts = len(late)
    _, dirs, rows, cols = home.shape
    assert rows > TILE
    last = late[0].shape[0]
    spans = [(*span, chunks[0]) for span in rows_of] + [(0, last, chunks[-1])]
    block = pl.BlockSpec((1, dirs, TILE, cols), lambda f, t: (begin + f, 0, t, 0))
    specs = [
        pl.BlockSpec((count, 1, dirs, cols), lambda f, t: (0, begin + f, 0, 0)) for _, count in rows_of for _ in range(parts)
    ] + [pl.BlockSpec((last, 1, dirs, cols), lambda f, t: (0, f, 0, 0))] * parts
    return pl.pallas_call(
        functools.partial(join_kernel, parts, rows // parts, spans),
        grid=(many, rows // TILE),
        in_specs=[pl.BlockSpec(memory_space=pltpu.SMEM), UNREAD, block]
        + [pl.BlockSpec((1, dirs, TILE, cols), lambda f, t: (begin + f, 0, 0, 0))]
        + specs,
        out_specs=block,
        out_shape=jax.ShapeDtypeStruct(home.shape, jnp.float32),
        scratch_shapes=[pltpu.VMEM((cols // LANES, rows * (dirs + 1), LANES), jnp.float32)],
        input_output_aliases={} if begin == 0 else {1: 0},
        compiler_params=pltpu.CompilerParams(vmem_limit_bytes=VMEM_LIMIT),
        cost_estimate=COST,
    )(own, into, home, share, *[piece for pieces in early for piece in pieces], *late)


def arrived_kernel(held, *refs):
    refs[-1][...] = jnp.zeros_like(refs[-1])


def arrived(after, pieces, held=()):
    outs = pl.pallas_call(
        functools.partial(arrived_kernel, len(held)),
        in_specs=[UNREAD] * (1 + len(pieces) + len(held)),
        out_specs=[UNREAD] * len(held) + [pl.BlockSpec(memory_space=pltpu.VMEM)],
        out_shape=[jax.ShapeDtypeStruct(h.shape, h.dtype) for h in held] + [jax.ShapeDtypeStruct((TILE, LANES), jnp.float32)],
        input_output_aliases={1 + len(pieces) + i: i for i in range(len(held))},
        cost_estimate=COST,
    )(after, *pieces, *held)
    return outs[-1], list(outs[:-1])


def swapped(pieces):
    parts = len(pieces)
    moved = {k: lax.ppermute(pieces[k], "comp", [(i, i ^ k) for i in range(parts)]) for k in range(parts - 1, 0, -1)}
    return [pieces[0]] + [moved[k] for k in range(1, parts)]


def across(low, high):
    count = lax.axis_size("space")
    up = [(i, i + 1) for i in range(count - 1)]
    down = [(i + 1, i) for i in range(count - 1)]
    return lax.ppermute(high, "space", up), lax.ppermute(low, "space", down)


def halves(count):
    spans, begin = [], 0
    while begin < count:
        many = max(1, (count - begin) // 2)
        spans.append((begin, many))
        begin += many
    return spans


def shards(
    adjoint_forcing,
    forward_state,
    wind_speed,
    cg_index,
    turn_index,
    sea_mask,
    dir_sign,
    w_in,
    w_out,
    wind_weight,
):
    parts = lax.axis_size("comp")
    own_place = lax.axis_index("comp")
    own = own_place.astype(jnp.int32).reshape(1)
    dirs = dir_sign.shape[1]
    comps, rows, cols = adjoint_forcing.shape
    freqs = comps // dirs
    local = rows // parts
    along = jnp.asarray(direction_factors(dirs))
    forcing = adjoint_forcing.reshape(freqs, dirs, rows, cols)
    weight = wind_weight[:, None]
    wind = wind_speed[:, None]
    everything = [(0, freqs)]
    sent = halves(freqs)
    groups = [(freqs - begin - many, many) for begin, many in reversed(sent)]
    levels = (cg_index, turn_index, sea_mask)
    if local > HALO:
        chunks = [(HALO, 0, local - HALO), (0, local - HALO, HALO)]
    else:
        chunks = [(0, 0, local)]
    ahead = chunks[0] if len(chunks) > 1 else None

    early, into, after = [], None, sea_mask
    for group in groups:
        into, pieces = inner(own, dir_sign, along, after, forcing, *levels, into, parts, ahead, group)
        if ahead:
            early.append(swapped(pieces))
    home, low, high = into
    above, below = across(low, high)
    after = home
    for pieces in early[:-2]:
        after, _ = arrived(after, pieces[1:])
    state = by_row((after, wind, weight), forward_state)
    after = state
    for pieces in early[-2:-1]:
        after, _ = arrived(after, pieces[1:])
    in_t, out_t = turned(after, w_in, w_out)
    share, pieces = outer(own, dir_sign, along, in_t, above, below, *levels, home, parts, chunks[-1])
    late = swapped(pieces)
    term = functools.partial(source_term, own)
    fixed = (state, wind, w_in, out_t, in_t, weight)
    after, grads, early_back, rows_of = share, [], [], []
    if ahead:
        count = ahead[2]
        rows_of = [(0, count // 2), (count // 2, count - count // 2)] if count > 1 else [(0, count)]
    for span in rows_of:
        grad, [back] = term(after, *fixed, early, groups, everything, span, ahead)
        after = grad
        if not grads:
            after, rest = arrived(grad, late[1:-1], back[1:])
            back = [back[0], *rest]
        grads.append(grad)
        early_back.append(swapped(back))
    late_grad, late_back = term(after, *fixed, [late], everything, sent, (0, chunks[-1][2]), chunks[-1])
    start, returned = late_grad, []
    for g, pieces in enumerate(late_back):
        if g < len(early_back):
            rest = [piece for group in late_back[g:] for piece in group[1:]]
            awaited = early_back[g][1:] if g + 1 < len(early_back) else early_back[g][1:-1]
            start, rest = arrived(start, awaited, rest)
            for n, group in enumerate(late_back[g:]):
                late_back[g + n] = [group[0], *rest[n * (parts - 1) : (n + 1) * (parts - 1)]]
        returned.append(swapped(late_back[g]))
    late_back = returned
    for group, back in zip(sent, late_back, strict=True):
        start = join(own, start, home, share, early_back, back, rows_of, chunks, group)
    gradient = jnp.where(
        own_place == 0, jnp.concatenate([late_grad, *grads], axis=0), jnp.concatenate([*grads, late_grad], axis=0)
    )
    return (start.reshape(comps, rows, cols), gradient.reshape(wind_speed.shape))


def solution(mesh):
    placed = (
        P("comp", "space", None),
        P(None, ("space", "comp"), None),
        P(("space", "comp"), None),
        P("comp", "space", None),
        P("comp", "space", None),
        P("space", None),
        P(),
        P(),
        P(),
        P(),
    )
    return jax.shard_map(
        shards,
        mesh=mesh,
        in_specs=placed,
        out_specs=(P("comp", "space", None), P(("space", "comp"), None)),
        check_vma=False,
    )
```

```python
import functools
import math

import jax
import jax.numpy as jnp
import numpy as np
from jax import lax
from jax.experimental import pallas as pl
from jax.experimental.pallas import tpu as pltpu
from jax.sharding import PartitionSpec as P

HALO = 2
TILE = 8
LANES = 128
MIB = 1 << 20
VMEM_LIMIT = 62 * MIB
COST = pl.CostEstimate(flops=1, bytes_accessed=1, transcendentals=0)
LONG = pl.CostEstimate(flops=10**11, bytes_accessed=100 * MIB, transcendentals=0)


def direction_factors(dirs):
    angle = (np.arange(dirs, dtype=np.float32) + np.float32(0.5)) * np.float32(2.0 * math.pi / dirs)
    return np.stack([np.float32(0.5) * np.abs(np.cos(angle)), np.float32(0.5) * np.abs(np.sin(angle))])


def chunk_row(owner, j, chunk):
    return jnp.where(owner == 0, chunk[0], chunk[1]) + j


UNREAD = pl.BlockSpec(memory_space=pl.ANY)


def lane_tiles(cols):
    return [pl.ds(c * LANES, LANES) for c in range(cols // LANES)]


def spreads(dirs):
    both = direction_factors(dirs).sum(axis=0)
    values = []
    for value in both:
        if not any(abs(value - other) < 1e-5 for other in values):
            values.append(value)
    return values, np.array([[int(np.argmin([abs(b - v) for v in values])) for b in both]], np.int32)


def coefficients(dirs, cel_ref, kept_ref, trn_ref, here, cg, turn, sea):
    sea = sea.astype(jnp.float32)
    celerity = 0.1 + 0.8 * cg.astype(jnp.float32) / 7.0
    turning = 0.3 * jnp.abs(turn.astype(jnp.float32) - 3.5) / 3.5
    cel_ref[here, :] = celerity * sea
    trn_ref[here, :] = turning * sea
    for n, both in enumerate(spreads(dirs)[0]):
        kept_ref[n, here, :] = (1.0 - float(both) * celerity - turning) * sea


def sweep(dirs, tiles, alone, lanes, sign_ref, along_ref, kind_ref, coefs, turns_up, load, store):
    cel_ref, kept_ref, trn_ref = coefs
    row = lax.broadcasted_iota(jnp.int32, (TILE, LANES), 0)
    lane = lax.broadcasted_iota(jnp.int32, (TILE, LANES), 1)
    nothing = jnp.zeros((TILE, LANES), jnp.float32)

    def span(t):
        return pl.ds(t * TILE, TILE)

    def one(d, carry):
        following = jnp.where(d == dirs - 1, 0, d + 1)
        previous = jnp.where(d == 0, dirs - 1, d - 1)
        ax = along_ref[0, d]
        ay = along_ref[1, d]
        kind = kind_ref[0, d]
        right = sign_ref[0, d] > 0
        high = sign_ref[1, d] > 0
        shift_x = jnp.where(right, LANES - 1, 1)
        shift_y = jnp.where(high, TILE - 1, 1)
        at_right = lane == jnp.where(right, LANES - 1, LANES)
        at_left = lane == jnp.where(right, LANES, 0)
        at_high = row == jnp.where(high, TILE - 1, TILE)
        at_low = row == jnp.where(high, TILE, 0)
        at_edge = row == jnp.where(high, TILE - 1, 0)

        def column(c):
            here = [load(t, d, lanes[c]) for t in range(tiles)]
            flow = [cel_ref[span(t), lanes[c]] * here[t] for t in range(tiles)]
            return here, flow, [pltpu.roll(f, shift_x, 1) for f in flow]

        before = [nothing] * tiles
        here, flow, moved = column(0)
        for c in range(len(lanes)):
            beyond = [nothing] * tiles
            if c + 1 < len(lanes):
                later = column(c + 1)
                beyond = later[2]
            lifted = [pltpu.roll(f, shift_y, 0) for f in flow]
            for t in range(tiles):
                flow_x = jnp.where(at_right, beyond[t], jnp.where(at_left, before[t], moved[t]))
                if alone:
                    flow_y = jnp.where(at_edge, nothing, lifted[t])
                else:
                    above = lifted[t + 1] if t + 1 < tiles else nothing
                    below = lifted[t - 1] if t > 0 else nothing
                    flow_y = jnp.where(at_high, above, jnp.where(at_low, below, lifted[t]))
                turned = jnp.where(turns_up(t, c), load(t, following, lanes[c]), load(t, previous, lanes[c]))
                total = kept_ref[kind, span(t), lanes[c]] * here[t] + ax * flow_x
                total = total + (ay * flow_y + trn_ref[span(t), lanes[c]] * turned)
                store(t, d, c, total)
            if c + 1 < len(lanes):
                before = moved
                here, flow, moved = later
        return carry

    lax.fori_loop(0, dirs, one, 0, unroll=6)


def emit(own, parts, local, chunk, dirs, lanes, swap_ref, send_refs):
    for k in range(parts):
        owner = own ^ k
        for j in range(chunk[2]):
            start = (owner * local + chunk_row(owner, j, chunk)) * (dirs + 1)
            for c, here in enumerate(lanes):
                send_refs[k][j, 0, :, here] = swap_ref[c, pl.ds(start, dirs), :].astype(jnp.bfloat16)


def inner_kernel(parts, local, chunk, into, own_ref, sign_ref, along_ref, kind_ref, _, forcing_ref, cg_ref, turn_ref, mask_ref, *refs):
    refs = refs[1:] if into else refs
    home_ref = refs[0]
    sends = parts if chunk else 0
    cel_ref, kept_ref, trn_ref, first_ref, swap_ref = refs[sends + 1 :]
    dirs, rows, cols = forcing_ref.shape[1:]
    pitch = dirs + 1
    lanes = lane_tiles(cols)
    tiles = rows // TILE

    def span(t):
        return pl.ds(t * TILE, TILE)

    for t in range(tiles):
        levels = (cg_ref[0, span(t), :], turn_ref[0, span(t), :], mask_ref[span(t), :])
        coefficients(dirs, cel_ref, kept_ref, trn_ref, span(t), *levels)

    def turns_up(t, c):
        return turn_ref[0, span(t), lanes[c]] >= 4

    def store_first(t, d, c, value):
        first_ref[d, span(t), lanes[c]] = value

    def store_last(t, d, c, value):
        home_ref[0, d, span(t), lanes[c]] = value
        if chunk:
            swap_ref[c, pl.ds(t * TILE * pitch + d, TILE, stride=pitch), :] = value

    coefs = (cel_ref, kept_ref, trn_ref)
    step = functools.partial(sweep, dirs, tiles, False, lanes, sign_ref, along_ref, kind_ref, coefs, turns_up)
    step(lambda t, d, here: forcing_ref[0, d, span(t), here], store_first)
    step(lambda t, d, here: first_ref[d, span(t), here], store_last)
    if chunk:
        emit(own_ref[0], parts, local, chunk, dirs, lanes, swap_ref, refs[1 : sends + 1])


def inner(own, signs, along, after, forcing, cg, turn, mask, into, parts, chunk, group):
    freqs, dirs, rows, cols = forcing.shape
    begin, many = group
    local = rows // parts
    smem = pl.BlockSpec(memory_space=pltpu.SMEM)
    levels = pl.BlockSpec((1, rows, cols), lambda f: (begin + f, 0, 0))
    block = pl.BlockSpec((1, dirs, rows, cols), lambda f: (begin + f, 0, 0, 0))
    coefs = pltpu.VMEM((rows, cols), jnp.float32)
    sends = parts if chunk else 0
    count = chunk[2] if chunk else 0
    outs = pl.pallas_call(
        functools.partial(inner_kernel, parts, local, chunk, into is not None),
        grid=(many,),
        in_specs=[smem, smem, smem, smem, UNREAD, block, levels, levels, pl.BlockSpec((rows, cols), lambda f: (0, 0))]
        + ([] if into is None else [UNREAD]),
        out_specs=[block] + [pl.BlockSpec((count, 1, dirs, cols), lambda f: (0, f, 0, 0))] * sends,
        out_shape=[jax.ShapeDtypeStruct(forcing.shape, jnp.float32)]
        + [jax.ShapeDtypeStruct((count, many, dirs, cols), jnp.bfloat16)] * sends,
        scratch_shapes=[
            coefs,
            pltpu.VMEM((len(spreads(dirs)[0]), rows, cols), jnp.float32),
            coefs,
            pltpu.VMEM((dirs, rows, cols), jnp.float32),
            pltpu.VMEM((cols // LANES, rows * (dirs + 1), LANES), jnp.float32),
        ],
        input_output_aliases={} if into is None else {9: 0},
        compiler_params=pltpu.CompilerParams(vmem_limit_bytes=VMEM_LIMIT),
        cost_estimate=COST,
    )(own, signs, *along, after, forcing, cg, turn, mask, *([] if into is None else [into]))
    return outs[0], list(outs[1:])


def edges_kernel(_, *refs):
    swap_ref, edge_ref = refs[-2:]
    dirs, _, cols = refs[0].shape[1:]
    pitch = dirs + 1
    lanes = lane_tiles(cols)
    edge_ref[...] = jnp.zeros_like(edge_ref)
    for side, low in ((0, 0), (1, TILE - HALO)):
        forcing_ref, cg_ref, turn_ref, mask_ref = refs[4 * side : 4 * side + 4]
        out_ref = refs[8 + side]

        def body(d, carry, forcing_ref=forcing_ref):
            for c, here in enumerate(lanes):
                swap_ref[c, pl.ds(d, TILE, stride=pitch), :] = forcing_ref[0, d, :, here]
            return carry

        lax.fori_loop(0, dirs, body, 0, unroll=12)
        for r in range(HALO):
            for c, here in enumerate(lanes):
                edge_ref[:dirs, here] = swap_ref[c, pl.ds((low + r) * pitch, dirs), :]
            for n, level in enumerate((cg_ref[0], turn_ref[0], mask_ref[...])):
                edge_ref[dirs + n : dirs + n + 1, :] = level[low + r : low + r + 1].astype(jnp.float32)
            out_ref[r, 0] = edge_ref[...].astype(jnp.bfloat16)


def edges(after, forcing, cg, turn, mask):
    freqs, dirs, rows, cols = forcing.shape
    out = pl.BlockSpec((HALO, 1, dirs + TILE, cols), lambda f: (0, f, 0, 0))
    shape = jax.ShapeDtypeStruct((HALO, freqs, dirs + TILE, cols), jnp.bfloat16)
    in_specs = [UNREAD]
    for t in (0, rows // TILE - 1):
        in_specs += [
            pl.BlockSpec((1, dirs, TILE, cols), lambda f, t=t: (f, 0, t, 0)),
            pl.BlockSpec((1, TILE, cols), lambda f, t=t: (f, t, 0)),
            pl.BlockSpec((1, TILE, cols), lambda f, t=t: (f, t, 0)),
            pl.BlockSpec((TILE, cols), lambda f, t=t: (t, 0)),
        ]
    return pl.pallas_call(
        edges_kernel,
        grid=(freqs,),
        in_specs=in_specs,
        out_specs=[out, out],
        out_shape=[shape, shape],
        scratch_shapes=[
            pltpu.VMEM((cols // LANES, TILE * (dirs + 1), LANES), jnp.float32),
            pltpu.VMEM((dirs + TILE, cols), jnp.float32),
        ],
        compiler_params=pltpu.CompilerParams(vmem_limit_bytes=VMEM_LIMIT),
        cost_estimate=COST,
    )(after, *(2 * [forcing, cg, turn, mask]))


def outer_kernel(parts, local, chunk, *refs):
    own_ref, sign_ref, along_ref, kind_ref, _, above_ref, below_ref = refs[:7]
    cg_ref, turn_ref, mask_ref, home_ref, share_ref = refs[7:12]
    send_refs = refs[12 : 12 + parts]
    cel_ref, kept_ref, trn_ref, up_ref, lev_ref, near_ref, first_ref, side_ref, edge_ref, swap_ref = refs[12 + parts :]
    dirs, rows, cols = home_ref.shape[1:]
    freqs = share_ref.shape[0]
    pitch = dirs + 1
    lanes = lane_tiles(cols)
    tiles = rows // TILE
    f = pl.program_id(0)

    def span(t):
        return pl.ds(t * TILE, TILE)

    @pl.when(f == 0)
    def _():
        edge_ref[...] = jnp.zeros_like(edge_ref)
        beyond = ((above_ref, 0, 0), (above_ref, 1, 1), (below_ref, 0, TILE - HALO), (below_ref, 1, TILE - 1))
        for n in range(freqs):
            for i, (ref, r, low) in enumerate(beyond):
                for c, here in enumerate(lanes):
                    piece = ref[r, n, :, here].astype(jnp.float32)
                    edge_ref[c, pl.ds(low * pitch, dirs), :] = piece[:dirs]
                    lev_ref[i * TILE : (i + 1) * TILE, here] = piece[dirs:]

            def gather(d, carry, n=n):
                for c, here in enumerate(lanes):
                    side_ref[d, span(n), here] = edge_ref[c, pl.ds(d, TILE, stride=pitch), :]
                return carry

            lax.fori_loop(0, dirs, gather, 0, unroll=12)
            for q, mine in enumerate((cg_ref[n], turn_ref[n], mask_ref[...])):
                for i, (_, _, low) in enumerate(beyond):
                    near_ref[q * TILE + low : q * TILE + low + 1, :] = lev_ref[i * TILE + q : i * TILE + q + 1, :]
                near_ref[q * TILE + HALO : q * TILE + 2 * HALO, :] = mine[:HALO].astype(jnp.float32)
                near_ref[q * TILE + 2 * HALO : q * TILE + 3 * HALO, :] = mine[rows - HALO :].astype(jnp.float32)
            coefficients(dirs, cel_ref, kept_ref, trn_ref, span(n), *[near_ref[span(q), :] for q in range(3)])
            up_ref[span(n), :] = near_ref[span(1), :]

        def turns_up(t, c):
            return up_ref[span(t), lanes[c]] >= 4.0

        def store_first(t, d, c, value):
            first_ref[d, span(t), lanes[c]] = value

        def store_last(t, d, c, value):
            share_ref[t, d, :, lanes[c]] = value

        coefs = (cel_ref, kept_ref, trn_ref)
        step = functools.partial(sweep, dirs, freqs, True, lanes, sign_ref, along_ref, kind_ref, coefs, turns_up)
        step(lambda t, d, here: side_ref[d, span(t), here], store_first)
        step(lambda t, d, here: first_ref[d, span(t), here], store_last)

    def whole(d, carry):
        for t in range(tiles):
            for c, here in enumerate(lanes):
                value = with_share(home_ref[0, d, span(t), here], share_ref, f, d, here, t, tiles)
                swap_ref[c, pl.ds(t * TILE * pitch + d, TILE, stride=pitch), :] = value
        return carry

    lax.fori_loop(0, dirs, whole, 0, unroll=4)
    emit(own_ref[0], parts, local, chunk, dirs, lanes, swap_ref, send_refs)


def with_share(value, share_ref, f, d, here, t, tiles):
    row = lax.broadcasted_iota(jnp.int32, value.shape, 0)
    if t == 0:
        value = value + jnp.where(row < HALO, pltpu.roll(share_ref[f, d, :, here], TILE - HALO, 0), 0.0)
    if t == tiles - 1:
        value = value + jnp.where(row >= TILE - HALO, pltpu.roll(share_ref[f, d, :, here], HALO, 0), 0.0)
    return value


def outer(own, signs, along, after, above, below, cg, turn, mask, home, parts, chunk):
    freqs, dirs, rows, cols = home.shape
    local = rows // parts
    smem = pl.BlockSpec(memory_space=pltpu.SMEM)
    edge = pl.BlockSpec((HALO, freqs, dirs + TILE, cols), lambda f: (0, 0, 0, 0))
    levels = pl.BlockSpec((freqs, rows, cols), lambda f: (0, 0, 0))
    tall = pltpu.VMEM((freqs * TILE, cols), jnp.float32)
    outs = pl.pallas_call(
        functools.partial(outer_kernel, parts, local, chunk),
        grid=(freqs,),
        in_specs=[smem, smem, smem, smem, UNREAD, edge, edge, levels, levels]
        + [pl.BlockSpec((rows, cols), lambda f: (0, 0)), pl.BlockSpec((1, dirs, rows, cols), lambda f: (f, 0, 0, 0))],
        out_specs=[pl.BlockSpec((freqs, dirs, TILE, cols), lambda f: (0, 0, 0, 0))]
        + [pl.BlockSpec((chunk[2], 1, dirs, cols), lambda f: (0, f, 0, 0))] * parts,
        out_shape=[jax.ShapeDtypeStruct((freqs, dirs, TILE, cols), jnp.float32)]
        + [jax.ShapeDtypeStruct((chunk[2], freqs, dirs, cols), jnp.bfloat16)] * parts,
        scratch_shapes=[
            tall,
            pltpu.VMEM((len(spreads(dirs)[0]), freqs * TILE, cols), jnp.float32),
            tall,
            tall,
            pltpu.VMEM((2 * HALO * TILE, cols), jnp.float32),
            pltpu.VMEM((3 * TILE, cols), jnp.float32),
            pltpu.VMEM((dirs, freqs * TILE, cols), jnp.float32),
            pltpu.VMEM((dirs, freqs * TILE, cols), jnp.float32),
            pltpu.VMEM((cols // LANES, TILE * (dirs + 1), LANES), jnp.float32),
            pltpu.VMEM((cols // LANES, rows * (dirs + 1), LANES), jnp.float32),
        ],
        compiler_params=pltpu.CompilerParams(vmem_limit_bytes=VMEM_LIMIT),
        cost_estimate=LONG,
    )(own, signs, *along, after, above, below, cg, turn, mask, home)
    return outs[0], list(outs[1:])


def by_row_kernel(*refs):
    state_ref, out_ref, swap_ref = refs[-3:]
    some, local, cols = state_ref.shape
    pitch = some + 1
    lanes = lane_tiles(cols)

    def body(d, carry):
        for c, here in enumerate(lanes):
            swap_ref[c, pl.ds(d, local, stride=pitch), :] = state_ref[d, :, here].astype(jnp.float32)
        return carry

    lax.fori_loop(0, some, body, 0, unroll=8)
    for r in range(local):
        for c, here in enumerate(lanes):
            out_ref[r, :, here] = swap_ref[c, pl.ds(r * pitch, some), :].astype(jnp.bfloat16)


def by_row(after, state):
    deep, local, cols = state.shape
    some = 48
    return pl.pallas_call(
        by_row_kernel,
        grid=(deep // some,),
        in_specs=[UNREAD] * len(after) + [pl.BlockSpec((some, local, cols), lambda d: (d, 0, 0))],
        out_specs=pl.BlockSpec((local, some, cols), lambda d: (0, d, 0)),
        out_shape=jax.ShapeDtypeStruct((local, deep, cols), jnp.bfloat16),
        scratch_shapes=[pltpu.VMEM((cols // LANES, local * (some + 1), LANES), jnp.float32)],
        compiler_params=pltpu.CompilerParams(vmem_limit_bytes=VMEM_LIMIT),
        cost_estimate=COST,
    )(*after, state)


def turned_kernel(_, w_in_ref, w_out_ref, weight_ref, in_t_ref, out_t_ref, column_ref):
    in_t_ref[...] = w_in_ref[...].T
    out_t_ref[...] = w_out_ref[...].T
    column_ref[...] = jnp.broadcast_to(weight_ref[...], (LANES, weight_ref.shape[1])).T


def turned(after, w_in, w_out, weight):
    hidden, total = w_in.shape
    step = 512
    tall = pl.BlockSpec((step, total), lambda h: (h, 0))
    wide = pl.BlockSpec((total, step), lambda h: (0, h))
    return pl.pallas_call(
        turned_kernel,
        grid=(hidden // step,),
        in_specs=[UNREAD, tall, wide, pl.BlockSpec((1, step), lambda h: (0, h))],
        out_specs=[wide, tall, pl.BlockSpec((step, LANES), lambda h: (h, 0))],
        out_shape=[
            jax.ShapeDtypeStruct((total, hidden), w_in.dtype),
            jax.ShapeDtypeStruct((hidden, total), w_in.dtype),
            jax.ShapeDtypeStruct((hidden, LANES), jnp.float32),
        ],
        compiler_params=pltpu.CompilerParams(vmem_limit_bytes=VMEM_LIMIT),
        cost_estimate=LONG,
    )(after, w_in, w_out, weight.reshape(1, hidden))


def source_kernel(parts, got, sent, dirs, step, first, chunk, own_ref, _, state_ref, wind_ref, w_in_ref, out_t_ref, in_t_ref, weight_ref, *refs):
    cell_refs = refs[: parts * len(got)]
    grad_ref = refs[parts * len(got)]
    back_refs = refs[parts * len(got) + 1 : -3]
    cell_ref, weighted_ref, grown_ref = refs[-3:]
    freqs = sum(many for _, many in got)
    hidden, width = weighted_ref.shape
    own = own_ref[0]

    def place(k, group):
        begin, many = group
        return pl.ds(pl.multiple_of(((own ^ k) * freqs + begin) * dirs, TILE), many * dirs)

    for g, group in enumerate(got):
        for k in range(parts):
            piece = cell_refs[g * parts + k][0].astype(jnp.float32)
            cell_ref[place(k, group), :] = piece.reshape(group[1] * dirs, width)
    cell = cell_ref[...].astype(jnp.bfloat16)
    state = state_ref[0]
    wind = wind_ref[pl.ds(chunk_row(own, first + pl.program_id(0), chunk), 1), :]
    grad = jnp.zeros((TILE, width), jnp.float32)
    for h in range(0, hidden, step):
        some = pl.ds(h, step)
        weight = weight_ref[some, :1]
        forward = jnp.dot(w_in_ref[some, :], state, preferred_element_type=jnp.float32) + weight * wind
        squash = jnp.tanh(forward)
        pulled = jnp.dot(out_t_ref[some, :], cell, preferred_element_type=jnp.float32)
        weighted = (1.0 - squash * squash) * pulled
        weighted_ref[some, :] = weighted.astype(jnp.bfloat16)
        grad = grad + jnp.sum((weight * weighted).reshape(step // TILE, TILE, width), axis=0)
    grad_ref[0] = jnp.sum(grad, axis=0, keepdims=True)
    grown_ref[...] = jnp.dot(in_t_ref[...], weighted_ref[...], preferred_element_type=jnp.float32)
    for g, group in enumerate(sent):
        for k in range(parts):
            grown = grown_ref[place(k, group), :].reshape(group[1], dirs, width)
            back_refs[g * parts + k][0] = grown.astype(jnp.bfloat16)


def source_term(own, after, state, wind, w_in, out_t, in_t, weight, cells, got, sent, rows, chunk):
    parts = len(cells[0])
    _, _, dirs, cols = cells[0][0].shape
    first, count = rows
    hidden, total = w_in.shape
    width = min(cols, 512)

    def row_of(j, own_ref):
        return chunk_row(own_ref[0], first + j, chunk)

    def whole(shape):
        return pl.BlockSpec(shape, lambda j, c, own_ref: (0, 0))

    cell_specs = [
        pl.BlockSpec((1, many, dirs, width), lambda j, c, own_ref: (first + j, 0, 0, c)) for _, many in got for _ in range(parts)
    ]
    back_specs = [pl.BlockSpec((1, many, dirs, width), lambda j, c, own_ref: (j, 0, 0, c)) for _, many in sent for _ in range(parts)]
    outs = pl.pallas_call(
        functools.partial(source_kernel, parts, got, sent, dirs, 256, first, chunk),
        grid_spec=pltpu.PrefetchScalarGridSpec(
            num_scalar_prefetch=1,
            grid=(count, cols // width),
            in_specs=[
                UNREAD,
                pl.BlockSpec((1, total, width), lambda j, c, own_ref: (row_of(j, own_ref), 0, c)),
                pl.BlockSpec((wind.shape[0], width), lambda j, c, own_ref: (0, c)),
                whole((hidden, total)),
                whole((hidden, total)),
                whole((total, hidden)),
                whole((hidden, LANES)),
            ]
            + cell_specs,
            out_specs=[pl.BlockSpec((1, 1, width), lambda j, c, own_ref: (j, 0, c))] + back_specs,
            scratch_shapes=[
                pltpu.VMEM((total, width), jnp.float32),
                pltpu.VMEM((hidden, width), jnp.bfloat16),
                pltpu.VMEM((total, width), jnp.float32),
            ],
        ),
        out_shape=[jax.ShapeDtypeStruct((count, 1, cols), jnp.float32)]
        + [jax.ShapeDtypeStruct((count, many, dirs, cols), jnp.bfloat16) for _, many in sent for _ in range(parts)],
        compiler_params=pltpu.CompilerParams(vmem_limit_bytes=VMEM_LIMIT),
        cost_estimate=COST,
    )(own, after, state, wind, w_in, out_t, in_t, weight, *[cell for group in cells for cell in group])
    return outs[0], [list(outs[1 + g * parts : 1 + (g + 1) * parts]) for g in range(len(sent))]


def join_kernel(parts, spans, own_ref, _, home_ref, share_ref, *refs):
    out_ref, swap_ref = refs[-2:]
    dirs, rows, cols = home_ref.shape[1:]
    pitch = dirs + 1
    local = rows // parts
    own = own_ref[0]
    lanes = lane_tiles(cols)
    tiles = rows // TILE
    for i, (first, count, chunk) in enumerate(spans):
        for k in range(parts):
            owner = own ^ k
            for j in range(count):
                start = (owner * local + chunk_row(owner, first + j, chunk)) * pitch
                for c, here in enumerate(lanes):
                    swap_ref[c, pl.ds(start, dirs), :] = refs[i * parts + k][j, 0, :, here].astype(jnp.float32)

    def body(d, carry):
        for t in range(tiles):
            for c, here in enumerate(lanes):
                grown = swap_ref[c, pl.ds(t * TILE * pitch + d, TILE, stride=pitch), :]
                value = with_share(home_ref[0, d, pl.ds(t * TILE, TILE), here], share_ref, 0, d, here, t, tiles)
                out_ref[0, d, pl.ds(t * TILE, TILE), here] = value + grown
        return carry

    lax.fori_loop(0, dirs, body, 0, unroll=2)


def join(own, into, home, share, early, late, rows_of, chunks, group):
    begin, many = group
    parts = len(late)
    _, dirs, rows, cols = home.shape
    last = late[0].shape[0]
    spans = [(*span, chunks[0]) for span in rows_of] + [(0, last, chunks[-1])]
    block = pl.BlockSpec((1, dirs, rows, cols), lambda f: (begin + f, 0, 0, 0))
    specs = [
        pl.BlockSpec((count, 1, dirs, cols), lambda f: (0, begin + f, 0, 0)) for _, count in rows_of for _ in range(parts)
    ] + [pl.BlockSpec((last, 1, dirs, cols), lambda f: (0, f, 0, 0))] * parts
    return pl.pallas_call(
        functools.partial(join_kernel, parts, spans),
        grid=(many,),
        in_specs=[pl.BlockSpec(memory_space=pltpu.SMEM), UNREAD, block]
        + [pl.BlockSpec((1, dirs, TILE, cols), lambda f: (begin + f, 0, 0, 0))]
        + specs,
        out_specs=block,
        out_shape=jax.ShapeDtypeStruct(home.shape, jnp.float32),
        scratch_shapes=[pltpu.VMEM((cols // LANES, rows * (dirs + 1), LANES), jnp.float32)],
        input_output_aliases={} if begin == 0 else {1: 0},
        compiler_params=pltpu.CompilerParams(vmem_limit_bytes=VMEM_LIMIT),
        cost_estimate=COST,
    )(own, into, home, share, *[piece for pieces in early for piece in pieces], *late)


def arrived_kernel(held, *refs):
    refs[-1][...] = jnp.zeros_like(refs[-1])


def arrived(after, pieces, held=()):
    outs = pl.pallas_call(
        functools.partial(arrived_kernel, len(held)),
        in_specs=[UNREAD] * (1 + len(pieces) + len(held)),
        out_specs=[UNREAD] * len(held) + [pl.BlockSpec(memory_space=pltpu.VMEM)],
        out_shape=[jax.ShapeDtypeStruct(h.shape, h.dtype) for h in held] + [jax.ShapeDtypeStruct((TILE, LANES), jnp.float32)],
        input_output_aliases={1 + len(pieces) + i: i for i in range(len(held))},
        cost_estimate=COST,
    )(after, *pieces, *held)
    return outs[-1], list(outs[:-1])


def swapped(pieces):
    parts = len(pieces)
    moved = {k: lax.ppermute(pieces[k], "comp", [(i, i ^ k) for i in range(parts)]) for k in range(parts - 1, 0, -1)}
    return [pieces[0]] + [moved[k] for k in range(1, parts)]


def across(low, high):
    count = lax.axis_size("space")
    up = [(i, i + 1) for i in range(count - 1)]
    down = [(i + 1, i) for i in range(count - 1)]
    return lax.ppermute(high, "space", up), lax.ppermute(low, "space", down)


def shards(
    adjoint_forcing,
    forward_state,
    wind_speed,
    cg_index,
    turn_index,
    sea_mask,
    dir_sign,
    w_in,
    w_out,
    wind_weight,
):
    parts = lax.axis_size("comp")
    own_place = lax.axis_index("comp")
    own = own_place.astype(jnp.int32).reshape(1)
    dirs = dir_sign.shape[1]
    comps, rows, cols = adjoint_forcing.shape
    freqs = comps // dirs
    local = rows // parts
    along = (jnp.asarray(direction_factors(dirs)), jnp.asarray(spreads(dirs)[1]))
    forcing = adjoint_forcing.reshape(freqs, dirs, rows, cols)
    everything = [(0, freqs)]
    many = freqs // 2 if freqs % 2 == 0 else freqs
    groups = [(begin, many) for begin in range(0, freqs, many)]
    sent = groups
    levels = (cg_index, turn_index, sea_mask)
    if local > HALO:
        chunks = [(HALO, 0, local - HALO), (0, local - HALO, HALO)]
    else:
        chunks = [(0, 0, local)]
    ahead = chunks[0] if len(chunks) > 1 else None

    early, home, after = [], None, sea_mask
    for g, group in enumerate(groups):
        home, pieces = inner(own, dir_sign, along, after, forcing, *levels, home, parts, ahead, group)
        if ahead:
            early.append(swapped(pieces))
        if g == 0:
            low, high = edges(pieces[-1] if ahead else home, forcing, *levels)
            after = high
    above, below = across(low, high)
    after = home
    for pieces in early[:-1]:
        after, _ = arrived(after, pieces[1:])
    state = by_row((after,), forward_state)
    share, pieces = outer(own, dir_sign, along, state, above, below, *levels, home, parts, chunks[-1])
    late = swapped(pieces)
    in_t, out_t, weight = turned(share, w_in, w_out, wind_weight)
    term = functools.partial(source_term, own)
    fixed = (state, wind_speed, w_in, out_t, in_t, weight)
    after, grads, early_back, rows_of = in_t, [], [], []
    if ahead:
        count = ahead[2]
        some = 2 if count % 2 == 0 else 1
        rows_of = [(first, some) for first in range(0, count, some)]
    for span in rows_of:
        grad, [back] = term(after, *fixed, early, groups, everything, span, ahead)
        after = grad
        if not grads:
            after, rest = arrived(grad, late[1:], back[1:])
            back = [back[0], *rest]
        grads.append(grad)
        early_back.append(swapped(back))
    late_grad, late_back = term(after, *fixed, [late], everything, sent, (0, chunks[-1][2]), chunks[-1])
    start = late_grad
    if early_back:
        start, rest = arrived(start, early_back[0][1:], [piece for pieces in late_back for piece in pieces[1:]])
        step = parts - 1
        late_back = [[pieces[0], *rest[g * step : (g + 1) * step]] for g, pieces in enumerate(late_back)]
    late_back = [swapped(pieces) for pieces in late_back]
    for group, back in zip(sent, late_back, strict=True):
        start = join(own, start, home, share, early_back, back, rows_of, chunks, group)
    gradient = jnp.where(
        own_place == 0, jnp.concatenate([late_grad, *grads], axis=0), jnp.concatenate([*grads, late_grad], axis=0)
    )
    return (start.reshape(comps, rows, cols), gradient.reshape(wind_speed.shape))


def solution(mesh):
    placed = (
        P("comp", "space", None),
        P(None, ("space", "comp"), None),
        P(("space", "comp"), None),
        P("comp", "space", None),
        P("comp", "space", None),
        P("space", None),
        P(),
        P(),
        P(),
        P(),
    )
    return jax.shard_map(
        shards,
        mesh=mesh,
        in_specs=placed,
        out_specs=(P("comp", "space", None), P(("space", "comp"), None)),
        check_vma=False,
    )
```

```python
import functools
import math

import jax
import jax.numpy as jnp
import numpy as np
from jax import lax
from jax.experimental import pallas as pl
from jax.experimental.pallas import tpu as pltpu
from jax.sharding import PartitionSpec as P

HALO = 2
TILE = 8
LANES = 128
MIB = 1 << 20
VMEM_LIMIT = 62 * MIB
COST = pl.CostEstimate(flops=1, bytes_accessed=1, transcendentals=0)
LONG = pl.CostEstimate(flops=10**11, bytes_accessed=100 * MIB, transcendentals=0)


def direction_factors(dirs):
    angle = (np.arange(dirs, dtype=np.float32) + np.float32(0.5)) * np.float32(2.0 * math.pi / dirs)
    return np.stack([np.float32(0.5) * np.abs(np.cos(angle)), np.float32(0.5) * np.abs(np.sin(angle))])


def chunk_row(owner, j, chunk):
    return jnp.where(owner == 0, chunk[0], chunk[1]) + j


UNREAD = pl.BlockSpec(memory_space=pl.ANY)


def lane_tiles(cols):
    return [pl.ds(c * LANES, LANES) for c in range(cols // LANES)]


def spreads(dirs):
    both = direction_factors(dirs).sum(axis=0)
    values = []
    for value in both:
        if not any(abs(value - other) < 1e-5 for other in values):
            values.append(value)
    return values, np.array([[int(np.argmin([abs(b - v) for v in values])) for b in both]], np.int32)


def coefficients(dirs, cel_ref, kept_ref, trn_ref, here, cg, turn, sea):
    sea = sea.astype(jnp.float32)
    celerity = 0.1 + 0.8 * cg.astype(jnp.float32) / 7.0
    turning = 0.3 * jnp.abs(turn.astype(jnp.float32) - 3.5) / 3.5
    cel_ref[here, :] = celerity * sea
    trn_ref[here, :] = turning * sea
    for n, both in enumerate(spreads(dirs)[0]):
        kept_ref[n, here, :] = (1.0 - float(both) * celerity - turning) * sea


def sweep(dirs, tiles, alone, lanes, sign_ref, along_ref, kind_ref, coefs, turns_up, load, store):
    cel_ref, kept_ref, trn_ref = coefs
    row = lax.broadcasted_iota(jnp.int32, (TILE, LANES), 0)
    lane = lax.broadcasted_iota(jnp.int32, (TILE, LANES), 1)
    nothing = jnp.zeros((TILE, LANES), jnp.float32)

    def span(t):
        return pl.ds(t * TILE, TILE)

    def one(d, carry):
        following = jnp.where(d == dirs - 1, 0, d + 1)
        previous = jnp.where(d == 0, dirs - 1, d - 1)
        ax = along_ref[0, d]
        ay = along_ref[1, d]
        kind = kind_ref[0, d]
        right = sign_ref[0, d] > 0
        high = sign_ref[1, d] > 0
        shift_x = jnp.where(right, LANES - 1, 1)
        shift_y = jnp.where(high, TILE - 1, 1)
        at_right = lane == jnp.where(right, LANES - 1, LANES)
        at_left = lane == jnp.where(right, LANES, 0)
        at_high = row == jnp.where(high, TILE - 1, TILE)
        at_low = row == jnp.where(high, TILE, 0)
        at_edge = row == jnp.where(high, TILE - 1, 0)

        def column(c):
            here = [load(t, d, lanes[c]) for t in range(tiles)]
            flow = [cel_ref[span(t), lanes[c]] * here[t] for t in range(tiles)]
            return here, flow, [pltpu.roll(f, shift_x, 1) for f in flow]

        before = [nothing] * tiles
        here, flow, moved = column(0)
        for c in range(len(lanes)):
            beyond = [nothing] * tiles
            if c + 1 < len(lanes):
                later = column(c + 1)
                beyond = later[2]
            lifted = [pltpu.roll(f, shift_y, 0) for f in flow]
            for t in range(tiles):
                flow_x = jnp.where(at_right, beyond[t], jnp.where(at_left, before[t], moved[t]))
                if alone:
                    flow_y = jnp.where(at_edge, nothing, lifted[t])
                else:
                    above = lifted[t + 1] if t + 1 < tiles else nothing
                    below = lifted[t - 1] if t > 0 else nothing
                    flow_y = jnp.where(at_high, above, jnp.where(at_low, below, lifted[t]))
                turned = jnp.where(turns_up(t, c), load(t, following, lanes[c]), load(t, previous, lanes[c]))
                total = kept_ref[kind, span(t), lanes[c]] * here[t] + ax * flow_x
                total = total + (ay * flow_y + trn_ref[span(t), lanes[c]] * turned)
                store(t, d, c, total)
            if c + 1 < len(lanes):
                before = moved
                here, flow, moved = later
        return carry

    lax.fori_loop(0, dirs, one, 0, unroll=6)


def emit(own, parts, local, chunk, dirs, lanes, swap_ref, send_refs):
    for k in range(parts):
        owner = own ^ k
        for j in range(chunk[2]):
            start = (owner * local + chunk_row(owner, j, chunk)) * (dirs + 1)
            for c, here in enumerate(lanes):
                send_refs[k][j, 0, :, here] = swap_ref[c, pl.ds(start, dirs), :].astype(jnp.bfloat16)


def inner_kernel(parts, local, chunk, into, own_ref, sign_ref, along_ref, kind_ref, _, forcing_ref, cg_ref, turn_ref, mask_ref, *refs):
    refs = refs[1:] if into else refs
    home_ref = refs[0]
    sends = parts if chunk else 0
    cel_ref, kept_ref, trn_ref, first_ref, swap_ref = refs[sends + 1 :]
    dirs, rows, cols = forcing_ref.shape[1:]
    pitch = dirs + 1
    lanes = lane_tiles(cols)
    tiles = rows // TILE

    def span(t):
        return pl.ds(t * TILE, TILE)

    for t in range(tiles):
        levels = (cg_ref[0, span(t), :], turn_ref[0, span(t), :], mask_ref[span(t), :])
        coefficients(dirs, cel_ref, kept_ref, trn_ref, span(t), *levels)

    def turns_up(t, c):
        return turn_ref[0, span(t), lanes[c]] >= 4

    def store_first(t, d, c, value):
        first_ref[d, span(t), lanes[c]] = value

    def store_last(t, d, c, value):
        home_ref[0, d, span(t), lanes[c]] = value
        if chunk:
            swap_ref[c, pl.ds(t * TILE * pitch + d, TILE, stride=pitch), :] = value

    coefs = (cel_ref, kept_ref, trn_ref)
    step = functools.partial(sweep, dirs, tiles, False, lanes, sign_ref, along_ref, kind_ref, coefs, turns_up)
    step(lambda t, d, here: forcing_ref[0, d, span(t), here], store_first)
    step(lambda t, d, here: first_ref[d, span(t), here], store_last)
    if chunk:
        emit(own_ref[0], parts, local, chunk, dirs, lanes, swap_ref, refs[1 : sends + 1])


def inner(own, signs, along, after, forcing, cg, turn, mask, into, parts, chunk, group):
    freqs, dirs, rows, cols = forcing.shape
    begin, many = group
    local = rows // parts
    smem = pl.BlockSpec(memory_space=pltpu.SMEM)
    levels = pl.BlockSpec((1, rows, cols), lambda f: (begin + f, 0, 0))
    block = pl.BlockSpec((1, dirs, rows, cols), lambda f: (begin + f, 0, 0, 0))
    coefs = pltpu.VMEM((rows, cols), jnp.float32)
    sends = parts if chunk else 0
    count = chunk[2] if chunk else 0
    outs = pl.pallas_call(
        functools.partial(inner_kernel, parts, local, chunk, into is not None),
        grid=(many,),
        in_specs=[smem, smem, smem, smem, UNREAD, block, levels, levels, pl.BlockSpec((rows, cols), lambda f: (0, 0))]
        + ([] if into is None else [UNREAD]),
        out_specs=[block] + [pl.BlockSpec((count, 1, dirs, cols), lambda f: (0, f, 0, 0))] * sends,
        out_shape=[jax.ShapeDtypeStruct(forcing.shape, jnp.float32)]
        + [jax.ShapeDtypeStruct((count, many, dirs, cols), jnp.bfloat16)] * sends,
        scratch_shapes=[
            coefs,
            pltpu.VMEM((len(spreads(dirs)[0]), rows, cols), jnp.float32),
            coefs,
            pltpu.VMEM((dirs, rows, cols), jnp.float32),
            pltpu.VMEM((cols // LANES, rows * (dirs + 1), LANES), jnp.float32),
        ],
        input_output_aliases={} if into is None else {9: 0},
        compiler_params=pltpu.CompilerParams(vmem_limit_bytes=VMEM_LIMIT),
        cost_estimate=COST,
    )(own, signs, *along, after, forcing, cg, turn, mask, *([] if into is None else [into]))
    return outs[0], list(outs[1:])


def edges_kernel(_, *refs):
    swap_ref, edge_ref = refs[-2:]
    dirs, _, cols = refs[0].shape[1:]
    pitch = dirs + 1
    lanes = lane_tiles(cols)
    edge_ref[...] = jnp.zeros_like(edge_ref)
    for side, low in ((0, 0), (1, TILE - HALO)):
        forcing_ref, cg_ref, turn_ref, mask_ref = refs[4 * side : 4 * side + 4]
        out_ref = refs[8 + side]

        def body(d, carry, forcing_ref=forcing_ref):
            for c, here in enumerate(lanes):
                swap_ref[c, pl.ds(d, TILE, stride=pitch), :] = forcing_ref[0, d, :, here]
            return carry

        lax.fori_loop(0, dirs, body, 0, unroll=12)
        for r in range(HALO):
            for c, here in enumerate(lanes):
                edge_ref[:dirs, here] = swap_ref[c, pl.ds((low + r) * pitch, dirs), :]
            for n, level in enumerate((cg_ref[0], turn_ref[0], mask_ref[...])):
                edge_ref[dirs + n : dirs + n + 1, :] = level[low + r : low + r + 1].astype(jnp.float32)
            out_ref[r, 0] = edge_ref[...].astype(jnp.bfloat16)


def edges(after, forcing, cg, turn, mask):
    freqs, dirs, rows, cols = forcing.shape
    out = pl.BlockSpec((HALO, 1, dirs + TILE, cols), lambda f: (0, f, 0, 0))
    shape = jax.ShapeDtypeStruct((HALO, freqs, dirs + TILE, cols), jnp.bfloat16)
    in_specs = [UNREAD]
    for t in (0, rows // TILE - 1):
        in_specs += [
            pl.BlockSpec((1, dirs, TILE, cols), lambda f, t=t: (f, 0, t, 0)),
            pl.BlockSpec((1, TILE, cols), lambda f, t=t: (f, t, 0)),
            pl.BlockSpec((1, TILE, cols), lambda f, t=t: (f, t, 0)),
            pl.BlockSpec((TILE, cols), lambda f, t=t: (t, 0)),
        ]
    return pl.pallas_call(
        edges_kernel,
        grid=(freqs,),
        in_specs=in_specs,
        out_specs=[out, out],
        out_shape=[shape, shape],
        scratch_shapes=[
            pltpu.VMEM((cols // LANES, TILE * (dirs + 1), LANES), jnp.float32),
            pltpu.VMEM((dirs + TILE, cols), jnp.float32),
        ],
        compiler_params=pltpu.CompilerParams(vmem_limit_bytes=VMEM_LIMIT),
        cost_estimate=COST,
    )(after, *(2 * [forcing, cg, turn, mask]))


def outer_kernel(parts, local, chunk, *refs):
    own_ref, sign_ref, along_ref, kind_ref, _, above_ref, below_ref = refs[:7]
    cg_ref, turn_ref, mask_ref, home_ref, share_ref = refs[7:12]
    send_refs = refs[12 : 12 + parts]
    cel_ref, kept_ref, trn_ref, up_ref, lev_ref, near_ref, first_ref, side_ref, edge_ref, swap_ref = refs[12 + parts :]
    dirs, rows, cols = home_ref.shape[1:]
    freqs = share_ref.shape[0]
    pitch = dirs + 1
    lanes = lane_tiles(cols)
    tiles = rows // TILE
    f = pl.program_id(0)

    def span(t):
        return pl.ds(t * TILE, TILE)

    @pl.when(f == 0)
    def _():
        edge_ref[...] = jnp.zeros_like(edge_ref)
        beyond = ((above_ref, 0, 0), (above_ref, 1, 1), (below_ref, 0, TILE - HALO), (below_ref, 1, TILE - 1))
        for n in range(freqs):
            for i, (ref, r, low) in enumerate(beyond):
                for c, here in enumerate(lanes):
                    piece = ref[r, n, :, here].astype(jnp.float32)
                    edge_ref[c, pl.ds(low * pitch, dirs), :] = piece[:dirs]
                    lev_ref[i * TILE : (i + 1) * TILE, here] = piece[dirs:]

            def gather(d, carry, n=n):
                for c, here in enumerate(lanes):
                    side_ref[d, span(n), here] = edge_ref[c, pl.ds(d, TILE, stride=pitch), :]
                return carry

            lax.fori_loop(0, dirs, gather, 0, unroll=12)
            for q, mine in enumerate((cg_ref[n], turn_ref[n], mask_ref[...])):
                for i, (_, _, low) in enumerate(beyond):
                    near_ref[q * TILE + low : q * TILE + low + 1, :] = lev_ref[i * TILE + q : i * TILE + q + 1, :]
                near_ref[q * TILE + HALO : q * TILE + 2 * HALO, :] = mine[:HALO].astype(jnp.float32)
                near_ref[q * TILE + 2 * HALO : q * TILE + 3 * HALO, :] = mine[rows - HALO :].astype(jnp.float32)
            coefficients(dirs, cel_ref, kept_ref, trn_ref, span(n), *[near_ref[span(q), :] for q in range(3)])
            up_ref[span(n), :] = near_ref[span(1), :]

        def turns_up(t, c):
            return up_ref[span(t), lanes[c]] >= 4.0

        def store_first(t, d, c, value):
            first_ref[d, span(t), lanes[c]] = value

        def store_last(t, d, c, value):
            share_ref[t, d, :, lanes[c]] = value

        coefs = (cel_ref, kept_ref, trn_ref)
        step = functools.partial(sweep, dirs, freqs, True, lanes, sign_ref, along_ref, kind_ref, coefs, turns_up)
        step(lambda t, d, here: side_ref[d, span(t), here], store_first)
        step(lambda t, d, here: first_ref[d, span(t), here], store_last)

    def whole(d, carry):
        for t in range(tiles):
            for c, here in enumerate(lanes):
                value = with_share(home_ref[0, d, span(t), here], share_ref, f, d, here, t, tiles)
                swap_ref[c, pl.ds(t * TILE * pitch + d, TILE, stride=pitch), :] = value
        return carry

    lax.fori_loop(0, dirs, whole, 0, unroll=4)
    emit(own_ref[0], parts, local, chunk, dirs, lanes, swap_ref, send_refs)


def with_share(value, share_ref, f, d, here, t, tiles):
    row = lax.broadcasted_iota(jnp.int32, value.shape, 0)
    if t == 0:
        value = value + jnp.where(row < HALO, pltpu.roll(share_ref[f, d, :, here], TILE - HALO, 0), 0.0)
    if t == tiles - 1:
        value = value + jnp.where(row >= TILE - HALO, pltpu.roll(share_ref[f, d, :, here], HALO, 0), 0.0)
    return value


def outer(own, signs, along, after, above, below, cg, turn, mask, home, parts, chunk):
    freqs, dirs, rows, cols = home.shape
    local = rows // parts
    smem = pl.BlockSpec(memory_space=pltpu.SMEM)
    edge = pl.BlockSpec((HALO, freqs, dirs + TILE, cols), lambda f: (0, 0, 0, 0))
    levels = pl.BlockSpec((freqs, rows, cols), lambda f: (0, 0, 0))
    tall = pltpu.VMEM((freqs * TILE, cols), jnp.float32)
    outs = pl.pallas_call(
        functools.partial(outer_kernel, parts, local, chunk),
        grid=(freqs,),
        in_specs=[smem, smem, smem, smem, UNREAD, edge, edge, levels, levels]
        + [pl.BlockSpec((rows, cols), lambda f: (0, 0)), pl.BlockSpec((1, dirs, rows, cols), lambda f: (f, 0, 0, 0))],
        out_specs=[pl.BlockSpec((freqs, dirs, TILE, cols), lambda f: (0, 0, 0, 0))]
        + [pl.BlockSpec((chunk[2], 1, dirs, cols), lambda f: (0, f, 0, 0))] * parts,
        out_shape=[jax.ShapeDtypeStruct((freqs, dirs, TILE, cols), jnp.float32)]
        + [jax.ShapeDtypeStruct((chunk[2], freqs, dirs, cols), jnp.bfloat16)] * parts,
        scratch_shapes=[
            tall,
            pltpu.VMEM((len(spreads(dirs)[0]), freqs * TILE, cols), jnp.float32),
            tall,
            tall,
            pltpu.VMEM((2 * HALO * TILE, cols), jnp.float32),
            pltpu.VMEM((3 * TILE, cols), jnp.float32),
            pltpu.VMEM((dirs, freqs * TILE, cols), jnp.float32),
            pltpu.VMEM((dirs, freqs * TILE, cols), jnp.float32),
            pltpu.VMEM((cols // LANES, TILE * (dirs + 1), LANES), jnp.float32),
            pltpu.VMEM((cols // LANES, rows * (dirs + 1), LANES), jnp.float32),
        ],
        compiler_params=pltpu.CompilerParams(vmem_limit_bytes=VMEM_LIMIT),
        cost_estimate=LONG,
    )(own, signs, *along, after, above, below, cg, turn, mask, home)
    return outs[0], list(outs[1:])


def by_row_kernel(*refs):
    state_ref, out_ref, swap_ref = refs[-3:]
    some, local, cols = state_ref.shape
    pitch = some + 1
    lanes = lane_tiles(cols)

    def body(d, carry):
        for c, here in enumerate(lanes):
            swap_ref[c, pl.ds(d, local, stride=pitch), :] = state_ref[d, :, here].astype(jnp.float32)
        return carry

    lax.fori_loop(0, some, body, 0, unroll=8)
    for r in range(local):
        for c, here in enumerate(lanes):
            out_ref[r, :, here] = swap_ref[c, pl.ds(r * pitch, some), :].astype(jnp.bfloat16)


def by_row(after, state):
    deep, local, cols = state.shape
    some = 48
    return pl.pallas_call(
        by_row_kernel,
        grid=(deep // some,),
        in_specs=[UNREAD] * len(after) + [pl.BlockSpec((some, local, cols), lambda d: (d, 0, 0))],
        out_specs=pl.BlockSpec((local, some, cols), lambda d: (0, d, 0)),
        out_shape=jax.ShapeDtypeStruct((local, deep, cols), jnp.bfloat16),
        scratch_shapes=[pltpu.VMEM((cols // LANES, local * (some + 1), LANES), jnp.float32)],
        compiler_params=pltpu.CompilerParams(vmem_limit_bytes=VMEM_LIMIT),
        cost_estimate=COST,
    )(*after, state)


def turned_kernel(_, w_in_ref, w_out_ref, weight_ref, in_t_ref, out_t_ref, column_ref):
    in_t_ref[...] = w_in_ref[...].T
    out_t_ref[...] = w_out_ref[...].T
    column_ref[...] = jnp.broadcast_to(weight_ref[...], (LANES, weight_ref.shape[1])).T


def turned(after, w_in, w_out, weight):
    hidden, total = w_in.shape
    step = 512
    tall = pl.BlockSpec((step, total), lambda h: (h, 0))
    wide = pl.BlockSpec((total, step), lambda h: (0, h))
    return pl.pallas_call(
        turned_kernel,
        grid=(hidden // step,),
        in_specs=[UNREAD, tall, wide, pl.BlockSpec((1, step), lambda h: (0, h))],
        out_specs=[wide, tall, pl.BlockSpec((step, LANES), lambda h: (h, 0))],
        out_shape=[
            jax.ShapeDtypeStruct((total, hidden), w_in.dtype),
            jax.ShapeDtypeStruct((hidden, total), w_in.dtype),
            jax.ShapeDtypeStruct((hidden, LANES), jnp.float32),
        ],
        compiler_params=pltpu.CompilerParams(vmem_limit_bytes=VMEM_LIMIT),
        cost_estimate=LONG,
    )(after, w_in, w_out, weight.reshape(1, hidden))


def source_kernel(parts, got, sent, dirs, step, first, chunk, own_ref, _, state_ref, wind_ref, w_in_ref, out_t_ref, in_t_ref, weight_ref, *refs):
    cell_refs = refs[: parts * len(got)]
    grad_ref = refs[parts * len(got)]
    back_refs = refs[parts * len(got) + 1 : -3]
    cell_ref, weighted_ref, grown_ref = refs[-3:]
    freqs = sum(many for _, many in got)
    hidden, width = weighted_ref.shape
    own = own_ref[0]

    def place(k, group):
        begin, many = group
        return pl.ds(pl.multiple_of(((own ^ k) * freqs + begin) * dirs, TILE), many * dirs)

    for g, group in enumerate(got):
        for k in range(parts):
            piece = cell_refs[g * parts + k][0].astype(jnp.float32)
            cell_ref[place(k, group), :] = piece.reshape(group[1] * dirs, width)
    cell = cell_ref[...].astype(jnp.bfloat16)
    state = state_ref[0]
    wind = wind_ref[pl.ds(chunk_row(own, first + pl.program_id(0), chunk), 1), :]
    grad = jnp.zeros((TILE, width), jnp.float32)
    for h in range(0, hidden, step):
        some = pl.ds(h, step)
        weight = weight_ref[some, :1]
        forward = jnp.dot(w_in_ref[some, :], state, preferred_element_type=jnp.float32) + weight * wind
        squash = jnp.tanh(forward)
        pulled = jnp.dot(out_t_ref[some, :], cell, preferred_element_type=jnp.float32)
        weighted = (1.0 - squash * squash) * pulled
        weighted_ref[some, :] = weighted.astype(jnp.bfloat16)
        grad = grad + jnp.sum((weight * weighted).reshape(step // TILE, TILE, width), axis=0)
    grad_ref[0] = jnp.sum(grad, axis=0, keepdims=True)
    grown_ref[...] = jnp.dot(in_t_ref[...], weighted_ref[...], preferred_element_type=jnp.float32)
    for g, group in enumerate(sent):
        for k in range(parts):
            grown = grown_ref[place(k, group), :].reshape(group[1], dirs, width)
            back_refs[g * parts + k][0] = grown.astype(jnp.bfloat16)


def source_term(own, after, state, wind, w_in, out_t, in_t, weight, cells, got, sent, rows, chunk):
    parts = len(cells[0])
    _, _, dirs, cols = cells[0][0].shape
    first, count = rows
    hidden, total = w_in.shape
    width = min(cols, 512)

    def row_of(j, own_ref):
        return chunk_row(own_ref[0], first + j, chunk)

    def whole(shape):
        return pl.BlockSpec(shape, lambda j, c, own_ref: (0, 0))

    cell_specs = [
        pl.BlockSpec((1, many, dirs, width), lambda j, c, own_ref: (first + j, 0, 0, c)) for _, many in got for _ in range(parts)
    ]
    back_specs = [pl.BlockSpec((1, many, dirs, width), lambda j, c, own_ref: (j, 0, 0, c)) for _, many in sent for _ in range(parts)]
    outs = pl.pallas_call(
        functools.partial(source_kernel, parts, got, sent, dirs, 256, first, chunk),
        grid_spec=pltpu.PrefetchScalarGridSpec(
            num_scalar_prefetch=1,
            grid=(count, cols // width),
            in_specs=[
                UNREAD,
                pl.BlockSpec((1, total, width), lambda j, c, own_ref: (row_of(j, own_ref), 0, c)),
                pl.BlockSpec((wind.shape[0], width), lambda j, c, own_ref: (0, c)),
                whole((hidden, total)),
                whole((hidden, total)),
                whole((total, hidden)),
                whole((hidden, LANES)),
            ]
            + cell_specs,
            out_specs=[pl.BlockSpec((1, 1, width), lambda j, c, own_ref: (j, 0, c))] + back_specs,
            scratch_shapes=[
                pltpu.VMEM((total, width), jnp.float32),
                pltpu.VMEM((hidden, width), jnp.bfloat16),
                pltpu.VMEM((total, width), jnp.float32),
            ],
        ),
        out_shape=[jax.ShapeDtypeStruct((count, 1, cols), jnp.float32)]
        + [jax.ShapeDtypeStruct((count, many, dirs, cols), jnp.bfloat16) for _, many in sent for _ in range(parts)],
        compiler_params=pltpu.CompilerParams(vmem_limit_bytes=VMEM_LIMIT),
        cost_estimate=COST,
    )(own, after, state, wind, w_in, out_t, in_t, weight, *[cell for group in cells for cell in group])
    return outs[0], [list(outs[1 + g * parts : 1 + (g + 1) * parts]) for g in range(len(sent))]


def join_kernel(parts, spans, own_ref, _, home_ref, share_ref, *refs):
    out_ref, swap_ref = refs[-2:]
    dirs, rows, cols = home_ref.shape[1:]
    pitch = dirs + 1
    local = rows // parts
    own = own_ref[0]
    lanes = lane_tiles(cols)
    tiles = rows // TILE
    for i, (first, count, chunk) in enumerate(spans):
        for k in range(parts):
            owner = own ^ k
            for j in range(count):
                start = (owner * local + chunk_row(owner, first + j, chunk)) * pitch
                for c, here in enumerate(lanes):
                    swap_ref[c, pl.ds(start, dirs), :] = refs[i * parts + k][j, 0, :, here].astype(jnp.float32)

    def body(d, carry):
        for t in range(tiles):
            for c, here in enumerate(lanes):
                grown = swap_ref[c, pl.ds(t * TILE * pitch + d, TILE, stride=pitch), :]
                value = with_share(home_ref[0, d, pl.ds(t * TILE, TILE), here], share_ref, 0, d, here, t, tiles)
                out_ref[0, d, pl.ds(t * TILE, TILE), here] = value + grown
        return carry

    lax.fori_loop(0, dirs, body, 0, unroll=2)


def join(own, into, home, share, early, late, rows_of, chunks, group):
    begin, many = group
    parts = len(late)
    _, dirs, rows, cols = home.shape
    last = late[0].shape[0]
    spans = [(*span, chunks[0]) for span in rows_of] + [(0, last, chunks[-1])]
    block = pl.BlockSpec((1, dirs, rows, cols), lambda f: (begin + f, 0, 0, 0))
    specs = [
        pl.BlockSpec((count, 1, dirs, cols), lambda f: (0, begin + f, 0, 0)) for _, count in rows_of for _ in range(parts)
    ] + [pl.BlockSpec((last, 1, dirs, cols), lambda f: (0, f, 0, 0))] * parts
    return pl.pallas_call(
        functools.partial(join_kernel, parts, spans),
        grid=(many,),
        in_specs=[pl.BlockSpec(memory_space=pltpu.SMEM), UNREAD, block]
        + [pl.BlockSpec((1, dirs, TILE, cols), lambda f: (begin + f, 0, 0, 0))]
        + specs,
        out_specs=block,
        out_shape=jax.ShapeDtypeStruct(home.shape, jnp.float32),
        scratch_shapes=[pltpu.VMEM((cols // LANES, rows * (dirs + 1), LANES), jnp.float32)],
        input_output_aliases={} if begin == 0 else {1: 0},
        compiler_params=pltpu.CompilerParams(vmem_limit_bytes=VMEM_LIMIT),
        cost_estimate=COST,
    )(own, into, home, share, *[piece for pieces in early for piece in pieces], *late)


def arrived_kernel(held, *refs):
    refs[-1][...] = jnp.zeros_like(refs[-1])


def arrived(after, pieces, held=()):
    outs = pl.pallas_call(
        functools.partial(arrived_kernel, len(held)),
        in_specs=[UNREAD] * (1 + len(pieces) + len(held)),
        out_specs=[UNREAD] * len(held) + [pl.BlockSpec(memory_space=pltpu.VMEM)],
        out_shape=[jax.ShapeDtypeStruct(h.shape, h.dtype) for h in held] + [jax.ShapeDtypeStruct((TILE, LANES), jnp.float32)],
        input_output_aliases={1 + len(pieces) + i: i for i in range(len(held))},
        cost_estimate=COST,
    )(after, *pieces, *held)
    return outs[-1], list(outs[:-1])


def swapped(pieces):
    parts = len(pieces)
    moved = {k: lax.ppermute(pieces[k], "comp", [(i, i ^ k) for i in range(parts)]) for k in range(parts - 1, 0, -1)}
    return [pieces[0]] + [moved[k] for k in range(1, parts)]


def across(low, high):
    count = lax.axis_size("space")
    up = [(i, i + 1) for i in range(count - 1)]
    down = [(i + 1, i) for i in range(count - 1)]
    return lax.ppermute(high, "space", up), lax.ppermute(low, "space", down)


def shards(
    adjoint_forcing,
    forward_state,
    wind_speed,
    cg_index,
    turn_index,
    sea_mask,
    dir_sign,
    w_in,
    w_out,
    wind_weight,
):
    parts = lax.axis_size("comp")
    own_place = lax.axis_index("comp")
    own = own_place.astype(jnp.int32).reshape(1)
    dirs = dir_sign.shape[1]
    comps, rows, cols = adjoint_forcing.shape
    freqs = comps // dirs
    local = rows // parts
    along = (jnp.asarray(direction_factors(dirs)), jnp.asarray(spreads(dirs)[1]))
    forcing = adjoint_forcing.reshape(freqs, dirs, rows, cols)
    everything = [(0, freqs)]
    many = freqs // 2 if freqs % 2 == 0 else freqs
    groups = [(begin, many) for begin in range(0, freqs, many)]
    sent = groups
    levels = (cg_index, turn_index, sea_mask)
    if local > HALO:
        chunks = [(HALO, 0, local - HALO), (0, local - HALO, HALO)]
    else:
        chunks = [(0, 0, local)]
    ahead = chunks[0] if len(chunks) > 1 else None

    early, home, after = [], None, sea_mask
    for g, group in enumerate(groups):
        home, pieces = inner(own, dir_sign, along, after, forcing, *levels, home, parts, ahead, group)
        if ahead:
            early.append(swapped(pieces))
        if g == 0:
            low, high = edges(pieces[-1] if ahead else home, forcing, *levels)
            after = high
    above, below = across(low, high)
    after = home
    for pieces in early[:-1]:
        after, _ = arrived(after, pieces[1:])
    state = by_row((after,), forward_state)
    share, pieces = outer(own, dir_sign, along, state, above, below, *levels, home, parts, chunks[-1])
    late = swapped(pieces)
    in_t, out_t, weight = turned(share, w_in, w_out, wind_weight)
    term = functools.partial(source_term, own)
    fixed = (state, wind_speed, w_in, out_t, in_t, weight)
    after, grads, early_back, rows_of = in_t, [], [], []
    if ahead:
        count = ahead[2]
        some = 2 if count % 2 == 0 else 1
        rows_of = [(first, some) for first in range(0, count, some)]
    for n, span in enumerate(rows_of):
        if n == 1:
            after, _ = arrived(after, late[-1:])
        if n > 1:
            after, _ = arrived(after, early_back[n - 2][1:2])
        grad, [back] = term(after, *fixed, early, groups, everything, span, ahead)
        after = grad
        if not grads:
            after, rest = arrived(grad, late[1:-1] if len(rows_of) > 1 else late[1:], back[1:])
            back = [back[0], *rest]
        grads.append(grad)
        early_back.append(swapped(back))
    late_grad, late_back = term(after, *fixed, [late], everything, sent, (0, chunks[-1][2]), chunks[-1])
    start = late_grad
    if early_back:
        start, rest = arrived(start, early_back[0][1:], [piece for pieces in late_back for piece in pieces[1:]])
        step = parts - 1
        late_back = [[pieces[0], *rest[g * step : (g + 1) * step]] for g, pieces in enumerate(late_back)]
    late_back = [swapped(pieces) for pieces in late_back]
    if early_back:
        start, _ = arrived(start, early_back[-1][1:])
    for group, back in zip(sent, late_back, strict=True):
        start = join(own, start, home, share, early_back, back, rows_of, chunks, group)
    gradient = jnp.where(
        own_place == 0, jnp.concatenate([late_grad, *grads], axis=0), jnp.concatenate([*grads, late_grad], axis=0)
    )
    return (start.reshape(comps, rows, cols), gradient.reshape(wind_speed.shape))


def solution(mesh):
    placed = (
        P("comp", "space", None),
        P(None, ("space", "comp"), None),
        P(("space", "comp"), None),
        P("comp", "space", None),
        P("comp", "space", None),
        P("space", None),
        P(),
        P(),
        P(),
        P(),
    )
    return jax.shard_map(
        shards,
        mesh=mesh,
        in_specs=placed,
        out_specs=(P("comp", "space", None), P(("space", "comp"), None)),
        check_vma=False,
    )
```

```python
import functools
import math

import jax
import jax.numpy as jnp
import numpy as np
from jax import lax
from jax.experimental import pallas as pl
from jax.experimental.pallas import tpu as pltpu
from jax.sharding import PartitionSpec as P

HALO = 2
TILE = 8
LANES = 128
MIB = 1 << 20
VMEM_LIMIT = 64 * MIB
COST = pl.CostEstimate(flops=1, bytes_accessed=1, transcendentals=0)
LONG = pl.CostEstimate(flops=10**11, bytes_accessed=100 * MIB, transcendentals=0)


def direction_factors(dirs):
    angle = (np.arange(dirs, dtype=np.float32) + np.float32(0.5)) * np.float32(2.0 * math.pi / dirs)
    return np.stack([np.float32(0.5) * np.abs(np.cos(angle)), np.float32(0.5) * np.abs(np.sin(angle))])


def chunk_row(owner, j, chunk):
    return jnp.where(owner == 0, chunk[0], chunk[1]) + j


UNREAD = pl.BlockSpec(memory_space=pl.ANY)


def lane_tiles(cols):
    return [pl.ds(c * LANES, LANES) for c in range(cols // LANES)]


def spreads(dirs):
    both = direction_factors(dirs).sum(axis=0)
    values = []
    for value in both:
        if not any(abs(value - other) < 1e-5 for other in values):
            values.append(value)
    return values, np.array([[int(np.argmin([abs(b - v) for v in values])) for b in both]], np.int32)


def coefficients(dirs, cel_ref, kept_ref, trn_ref, here, cg, turn, sea):
    sea = sea.astype(jnp.float32)
    celerity = 0.1 + 0.8 * cg.astype(jnp.float32) / 7.0
    turning = 0.3 * jnp.abs(turn.astype(jnp.float32) - 3.5) / 3.5
    cel_ref[here, :] = celerity * sea
    trn_ref[here, :] = turning * sea
    for n, both in enumerate(spreads(dirs)[0]):
        kept_ref[n, here, :] = (1.0 - float(both) * celerity - turning) * sea


def sweep(dirs, tiles, alone, lanes, sign_ref, along_ref, kind_ref, coefs, turns_up, load, store):
    cel_ref, kept_ref, trn_ref = coefs
    row = lax.broadcasted_iota(jnp.int32, (TILE, LANES), 0)
    lane = lax.broadcasted_iota(jnp.int32, (TILE, LANES), 1)
    nothing = jnp.zeros((TILE, LANES), jnp.float32)

    def span(t):
        return pl.ds(t * TILE, TILE)

    def one(d, carry):
        following = jnp.where(d == dirs - 1, 0, d + 1)
        previous = jnp.where(d == 0, dirs - 1, d - 1)
        ax = along_ref[0, d]
        ay = along_ref[1, d]
        kind = kind_ref[0, d]
        right = sign_ref[0, d] > 0
        high = sign_ref[1, d] > 0
        shift_x = jnp.where(right, LANES - 1, 1)
        shift_y = jnp.where(high, TILE - 1, 1)
        at_right = lane == jnp.where(right, LANES - 1, LANES)
        at_left = lane == jnp.where(right, LANES, 0)
        at_high = row == jnp.where(high, TILE - 1, TILE)
        at_low = row == jnp.where(high, TILE, 0)
        at_edge = row == jnp.where(high, TILE - 1, 0)

        def column(c):
            here = [load(t, d, lanes[c]) for t in range(tiles)]
            flow = [cel_ref[span(t), lanes[c]] * here[t] for t in range(tiles)]
            return here, flow, [pltpu.roll(f, shift_x, 1) for f in flow]

        before = [nothing] * tiles
        here, flow, moved = column(0)
        for c in range(len(lanes)):
            beyond = [nothing] * tiles
            if c + 1 < len(lanes):
                later = column(c + 1)
                beyond = later[2]
            lifted = [pltpu.roll(f, shift_y, 0) for f in flow]
            for t in range(tiles):
                flow_x = jnp.where(at_right, beyond[t], jnp.where(at_left, before[t], moved[t]))
                if alone:
                    flow_y = jnp.where(at_edge, nothing, lifted[t])
                else:
                    above = lifted[t + 1] if t + 1 < tiles else nothing
                    below = lifted[t - 1] if t > 0 else nothing
                    flow_y = jnp.where(at_high, above, jnp.where(at_low, below, lifted[t]))
                turned = jnp.where(turns_up(t, c), load(t, following, lanes[c]), load(t, previous, lanes[c]))
                total = kept_ref[kind, span(t), lanes[c]] * here[t] + ax * flow_x
                total = total + (ay * flow_y + trn_ref[span(t), lanes[c]] * turned)
                store(t, d, c, total)
            if c + 1 < len(lanes):
                before = moved
                here, flow, moved = later
        return carry

    lax.fori_loop(0, dirs, one, 0, unroll=6)


def emit(own, parts, local, chunk, dirs, lanes, swap_ref, send_refs):
    for k in range(parts):
        owner = own ^ k
        for j in range(chunk[2]):
            start = (owner * local + chunk_row(owner, j, chunk)) * (dirs + 1)
            for c, here in enumerate(lanes):
                send_refs[k][j, 0, :, here] = swap_ref[c, pl.ds(start, dirs), :].astype(jnp.bfloat16)


def inner_kernel(parts, local, chunk, into, own_ref, sign_ref, along_ref, kind_ref, _, forcing_ref, cg_ref, turn_ref, mask_ref, *refs):
    refs = refs[1:] if into else refs
    home_ref = refs[0]
    sends = parts if chunk else 0
    cel_ref, kept_ref, trn_ref, first_ref, swap_ref = refs[sends + 1 :]
    dirs, rows, cols = forcing_ref.shape[1:]
    pitch = dirs + 1
    lanes = lane_tiles(cols)
    tiles = rows // TILE

    def span(t):
        return pl.ds(t * TILE, TILE)

    for t in range(tiles):
        levels = (cg_ref[0, span(t), :], turn_ref[0, span(t), :], mask_ref[span(t), :])
        coefficients(dirs, cel_ref, kept_ref, trn_ref, span(t), *levels)

    def turns_up(t, c):
        return turn_ref[0, span(t), lanes[c]] >= 4

    def store_first(t, d, c, value):
        first_ref[d, span(t), lanes[c]] = value

    def store_last(t, d, c, value):
        home_ref[0, d, span(t), lanes[c]] = value
        if chunk:
            swap_ref[c, pl.ds(t * TILE * pitch + d, TILE, stride=pitch), :] = value

    coefs = (cel_ref, kept_ref, trn_ref)
    step = functools.partial(sweep, dirs, tiles, False, lanes, sign_ref, along_ref, kind_ref, coefs, turns_up)
    step(lambda t, d, here: forcing_ref[0, d, span(t), here], store_first)
    step(lambda t, d, here: first_ref[d, span(t), here], store_last)
    if chunk:
        emit(own_ref[0], parts, local, chunk, dirs, lanes, swap_ref, refs[1 : sends + 1])


def inner(own, signs, along, after, forcing, cg, turn, mask, into, parts, chunk, group):
    freqs, dirs, rows, cols = forcing.shape
    begin, many = group
    local = rows // parts
    smem = pl.BlockSpec(memory_space=pltpu.SMEM)
    levels = pl.BlockSpec((1, rows, cols), lambda f: (begin + f, 0, 0))
    block = pl.BlockSpec((1, dirs, rows, cols), lambda f: (begin + f, 0, 0, 0))
    coefs = pltpu.VMEM((rows, cols), jnp.float32)
    sends = parts if chunk else 0
    count = chunk[2] if chunk else 0
    outs = pl.pallas_call(
        functools.partial(inner_kernel, parts, local, chunk, into is not None),
        grid=(many,),
        in_specs=[smem, smem, smem, smem, UNREAD, block, levels, levels, pl.BlockSpec((rows, cols), lambda f: (0, 0))]
        + ([] if into is None else [UNREAD]),
        out_specs=[block] + [pl.BlockSpec((count, 1, dirs, cols), lambda f: (0, f, 0, 0))] * sends,
        out_shape=[jax.ShapeDtypeStruct(forcing.shape, jnp.float32)]
        + [jax.ShapeDtypeStruct((count, many, dirs, cols), jnp.bfloat16)] * sends,
        scratch_shapes=[
            coefs,
            pltpu.VMEM((len(spreads(dirs)[0]), rows, cols), jnp.float32),
            coefs,
            pltpu.VMEM((dirs, rows, cols), jnp.float32),
            pltpu.VMEM((cols // LANES, rows * (dirs + 1), LANES), jnp.float32),
        ],
        input_output_aliases={} if into is None else {9: 0},
        compiler_params=pltpu.CompilerParams(vmem_limit_bytes=VMEM_LIMIT),
        cost_estimate=COST,
    )(own, signs, *along, after, forcing, cg, turn, mask, *([] if into is None else [into]))
    return outs[0], list(outs[1:])


def edges_kernel(_, *refs):
    swap_ref, edge_ref = refs[-2:]
    dirs, _, cols = refs[0].shape[1:]
    pitch = dirs + 1
    lanes = lane_tiles(cols)
    edge_ref[...] = jnp.zeros_like(edge_ref)
    for side, low in ((0, 0), (1, TILE - HALO)):
        forcing_ref, cg_ref, turn_ref, mask_ref = refs[4 * side : 4 * side + 4]
        out_ref = refs[8 + side]

        def body(d, carry, forcing_ref=forcing_ref):
            for c, here in enumerate(lanes):
                swap_ref[c, pl.ds(d, TILE, stride=pitch), :] = forcing_ref[0, d, :, here]
            return carry

        lax.fori_loop(0, dirs, body, 0, unroll=12)
        for r in range(HALO):
            for c, here in enumerate(lanes):
                edge_ref[:dirs, here] = swap_ref[c, pl.ds((low + r) * pitch, dirs), :]
            for n, level in enumerate((cg_ref[0], turn_ref[0], mask_ref[...])):
                edge_ref[dirs + n : dirs + n + 1, :] = level[low + r : low + r + 1].astype(jnp.float32)
            out_ref[r, 0] = edge_ref[...].astype(jnp.bfloat16)


def edges(after, forcing, cg, turn, mask):
    freqs, dirs, rows, cols = forcing.shape
    out = pl.BlockSpec((HALO, 1, dirs + TILE, cols), lambda f: (0, f, 0, 0))
    shape = jax.ShapeDtypeStruct((HALO, freqs, dirs + TILE, cols), jnp.bfloat16)
    in_specs = [UNREAD]
    for t in (0, rows // TILE - 1):
        in_specs += [
            pl.BlockSpec((1, dirs, TILE, cols), lambda f, t=t: (f, 0, t, 0)),
            pl.BlockSpec((1, TILE, cols), lambda f, t=t: (f, t, 0)),
            pl.BlockSpec((1, TILE, cols), lambda f, t=t: (f, t, 0)),
            pl.BlockSpec((TILE, cols), lambda f, t=t: (t, 0)),
        ]
    return pl.pallas_call(
        edges_kernel,
        grid=(freqs,),
        in_specs=in_specs,
        out_specs=[out, out],
        out_shape=[shape, shape],
        scratch_shapes=[
            pltpu.VMEM((cols // LANES, TILE * (dirs + 1), LANES), jnp.float32),
            pltpu.VMEM((dirs + TILE, cols), jnp.float32),
        ],
        compiler_params=pltpu.CompilerParams(vmem_limit_bytes=VMEM_LIMIT),
        cost_estimate=COST,
    )(after, *(2 * [forcing, cg, turn, mask]))


def outer_kernel(parts, local, chunk, *refs):
    own_ref, sign_ref, along_ref, kind_ref, _, above_ref, below_ref = refs[:7]
    cg_ref, turn_ref, mask_ref, home_ref, share_ref = refs[7:12]
    send_refs = refs[12 : 12 + parts]
    cel_ref, kept_ref, trn_ref, up_ref, lev_ref, near_ref, first_ref, side_ref, edge_ref, swap_ref = refs[12 + parts :]
    dirs, rows, cols = home_ref.shape[1:]
    freqs = share_ref.shape[0]
    pitch = dirs + 1
    lanes = lane_tiles(cols)
    tiles = rows // TILE
    f = pl.program_id(0)

    def span(t):
        return pl.ds(t * TILE, TILE)

    @pl.when(f == 0)
    def _():
        edge_ref[...] = jnp.zeros_like(edge_ref)
        beyond = ((above_ref, 0, 0), (above_ref, 1, 1), (below_ref, 0, TILE - HALO), (below_ref, 1, TILE - 1))
        for n in range(freqs):
            for i, (ref, r, low) in enumerate(beyond):
                for c, here in enumerate(lanes):
                    piece = ref[r, n, :, here].astype(jnp.float32)
                    edge_ref[c, pl.ds(low * pitch, dirs), :] = piece[:dirs]
                    lev_ref[i * TILE : (i + 1) * TILE, here] = piece[dirs:]

            def gather(d, carry, n=n):
                for c, here in enumerate(lanes):
                    side_ref[d, span(n), here] = edge_ref[c, pl.ds(d, TILE, stride=pitch), :]
                return carry

            lax.fori_loop(0, dirs, gather, 0, unroll=12)
            for q, mine in enumerate((cg_ref[n], turn_ref[n], mask_ref[...])):
                for i, (_, _, low) in enumerate(beyond):
                    near_ref[q * TILE + low : q * TILE + low + 1, :] = lev_ref[i * TILE + q : i * TILE + q + 1, :]
                near_ref[q * TILE + HALO : q * TILE + 2 * HALO, :] = mine[:HALO].astype(jnp.float32)
                near_ref[q * TILE + 2 * HALO : q * TILE + 3 * HALO, :] = mine[rows - HALO :].astype(jnp.float32)
            coefficients(dirs, cel_ref, kept_ref, trn_ref, span(n), *[near_ref[span(q), :] for q in range(3)])
            up_ref[span(n), :] = near_ref[span(1), :]

        def turns_up(t, c):
            return up_ref[span(t), lanes[c]] >= 4.0

        def store_first(t, d, c, value):
            first_ref[d, span(t), lanes[c]] = value

        def store_last(t, d, c, value):
            share_ref[t, d, :, lanes[c]] = value

        coefs = (cel_ref, kept_ref, trn_ref)
        step = functools.partial(sweep, dirs, freqs, True, lanes, sign_ref, along_ref, kind_ref, coefs, turns_up)
        step(lambda t, d, here: side_ref[d, span(t), here], store_first)
        step(lambda t, d, here: first_ref[d, span(t), here], store_last)

    def whole(d, carry):
        for t in range(tiles):
            for c, here in enumerate(lanes):
                value = with_share(home_ref[0, d, span(t), here], share_ref, f, d, here, t, tiles)
                swap_ref[c, pl.ds(t * TILE * pitch + d, TILE, stride=pitch), :] = value
        return carry

    lax.fori_loop(0, dirs, whole, 0, unroll=4)
    emit(own_ref[0], parts, local, chunk, dirs, lanes, swap_ref, send_refs)


def with_share(value, share_ref, f, d, here, t, tiles):
    row = lax.broadcasted_iota(jnp.int32, value.shape, 0)
    if t == 0:
        value = value + jnp.where(row < HALO, pltpu.roll(share_ref[f, d, :, here], TILE - HALO, 0), 0.0)
    if t == tiles - 1:
        value = value + jnp.where(row >= TILE - HALO, pltpu.roll(share_ref[f, d, :, here], HALO, 0), 0.0)
    return value


def outer(own, signs, along, after, above, below, cg, turn, mask, home, parts, chunk):
    freqs, dirs, rows, cols = home.shape
    local = rows // parts
    smem = pl.BlockSpec(memory_space=pltpu.SMEM)
    edge = pl.BlockSpec((HALO, freqs, dirs + TILE, cols), lambda f: (0, 0, 0, 0))
    levels = pl.BlockSpec((freqs, rows, cols), lambda f: (0, 0, 0))
    tall = pltpu.VMEM((freqs * TILE, cols), jnp.float32)
    outs = pl.pallas_call(
        functools.partial(outer_kernel, parts, local, chunk),
        grid=(freqs,),
        in_specs=[smem, smem, smem, smem, UNREAD, edge, edge, levels, levels]
        + [pl.BlockSpec((rows, cols), lambda f: (0, 0)), pl.BlockSpec((1, dirs, rows, cols), lambda f: (f, 0, 0, 0))],
        out_specs=[pl.BlockSpec((freqs, dirs, TILE, cols), lambda f: (0, 0, 0, 0))]
        + [pl.BlockSpec((chunk[2], 1, dirs, cols), lambda f: (0, f, 0, 0))] * parts,
        out_shape=[jax.ShapeDtypeStruct((freqs, dirs, TILE, cols), jnp.float32)]
        + [jax.ShapeDtypeStruct((chunk[2], freqs, dirs, cols), jnp.bfloat16)] * parts,
        scratch_shapes=[
            tall,
            pltpu.VMEM((len(spreads(dirs)[0]), freqs * TILE, cols), jnp.float32),
            tall,
            tall,
            pltpu.VMEM((2 * HALO * TILE, cols), jnp.float32),
            pltpu.VMEM((3 * TILE, cols), jnp.float32),
            pltpu.VMEM((dirs, freqs * TILE, cols), jnp.float32),
            pltpu.VMEM((dirs, freqs * TILE, cols), jnp.float32),
            pltpu.VMEM((cols // LANES, TILE * (dirs + 1), LANES), jnp.float32),
            pltpu.VMEM((cols // LANES, rows * (dirs + 1), LANES), jnp.float32),
        ],
        compiler_params=pltpu.CompilerParams(vmem_limit_bytes=VMEM_LIMIT),
        cost_estimate=LONG,
    )(own, signs, *along, after, above, below, cg, turn, mask, home)
    return outs[0], list(outs[1:])


def by_row_kernel(*refs):
    state_ref, out_ref, swap_ref = refs[-3:]
    some, local, cols = state_ref.shape
    pitch = some + 1
    lanes = lane_tiles(cols)

    def body(d, carry):
        for c, here in enumerate(lanes):
            swap_ref[c, pl.ds(d, local, stride=pitch), :] = state_ref[d, :, here].astype(jnp.float32)
        return carry

    lax.fori_loop(0, some, body, 0, unroll=8)
    for r in range(local):
        for c, here in enumerate(lanes):
            out_ref[r, :, here] = swap_ref[c, pl.ds(r * pitch, some), :].astype(jnp.bfloat16)


def by_row(after, state):
    deep, local, cols = state.shape
    some = 48
    return pl.pallas_call(
        by_row_kernel,
        grid=(deep // some,),
        in_specs=[UNREAD] * len(after) + [pl.BlockSpec((some, local, cols), lambda d: (d, 0, 0))],
        out_specs=pl.BlockSpec((local, some, cols), lambda d: (0, d, 0)),
        out_shape=jax.ShapeDtypeStruct((local, deep, cols), jnp.bfloat16),
        scratch_shapes=[pltpu.VMEM((cols // LANES, local * (some + 1), LANES), jnp.float32)],
        compiler_params=pltpu.CompilerParams(vmem_limit_bytes=VMEM_LIMIT),
        cost_estimate=COST,
    )(*after, state)


def turned_kernel(_, w_in_ref, w_out_ref, weight_ref, in_t_ref, out_t_ref, column_ref):
    in_t_ref[...] = w_in_ref[...].T
    out_t_ref[...] = w_out_ref[...].T
    column_ref[...] = jnp.broadcast_to(weight_ref[...], (LANES, weight_ref.shape[1])).T


def turned(after, w_in, w_out, weight):
    hidden, total = w_in.shape
    step = 512
    tall = pl.BlockSpec((step, total), lambda h: (h, 0))
    wide = pl.BlockSpec((total, step), lambda h: (0, h))
    return pl.pallas_call(
        turned_kernel,
        grid=(hidden // step,),
        in_specs=[UNREAD, tall, wide, pl.BlockSpec((1, step), lambda h: (0, h))],
        out_specs=[wide, tall, pl.BlockSpec((step, LANES), lambda h: (h, 0))],
        out_shape=[
            jax.ShapeDtypeStruct((total, hidden), w_in.dtype),
            jax.ShapeDtypeStruct((hidden, total), w_in.dtype),
            jax.ShapeDtypeStruct((hidden, LANES), jnp.float32),
        ],
        compiler_params=pltpu.CompilerParams(vmem_limit_bytes=VMEM_LIMIT),
        cost_estimate=LONG,
    )(after, w_in, w_out, weight.reshape(1, hidden))


def source_kernel(parts, got, sent, dirs, step, first, chunk, own_ref, _, state_ref, wind_ref, w_in_ref, out_t_ref, in_t_ref, weight_ref, *refs):
    cell_refs = refs[: parts * len(got)]
    grad_ref = refs[parts * len(got)]
    back_refs = refs[parts * len(got) + 1 : -3]
    cell_ref, weighted_ref, grown_ref = refs[-3:]
    freqs = sum(many for _, many in got)
    hidden, width = weighted_ref.shape
    own = own_ref[0]

    def place(k, group):
        begin, many = group
        return pl.ds(pl.multiple_of(((own ^ k) * freqs + begin) * dirs, TILE), many * dirs)

    for g, group in enumerate(got):
        for k in range(parts):
            piece = cell_refs[g * parts + k][0].astype(jnp.float32)
            cell_ref[place(k, group), :] = piece.reshape(group[1] * dirs, width)
    cell = cell_ref[...].astype(jnp.bfloat16)
    state = state_ref[0]
    wind = wind_ref[pl.ds(chunk_row(own, first + pl.program_id(0), chunk), 1), :]
    grad = jnp.zeros((TILE, width), jnp.float32)
    for h in range(0, hidden, step):
        some = pl.ds(h, step)
        weight = weight_ref[some, :1]
        forward = jnp.dot(w_in_ref[some, :], state, preferred_element_type=jnp.float32) + weight * wind
        squash = jnp.tanh(forward)
        pulled = jnp.dot(out_t_ref[some, :], cell, preferred_element_type=jnp.float32)
        weighted = (1.0 - squash * squash) * pulled
        weighted_ref[some, :] = weighted.astype(jnp.bfloat16)
        grad = grad + jnp.sum((weight * weighted).reshape(step // TILE, TILE, width), axis=0)
    grad_ref[0] = jnp.sum(grad, axis=0, keepdims=True)
    grown_ref[...] = jnp.dot(in_t_ref[...], weighted_ref[...], preferred_element_type=jnp.float32)
    for g, group in enumerate(sent):
        for k in range(parts):
            grown = grown_ref[place(k, group), :].reshape(group[1], dirs, width)
            back_refs[g * parts + k][0] = grown.astype(jnp.bfloat16)


def source_term(own, after, state, wind, w_in, out_t, in_t, weight, cells, got, sent, rows, chunk):
    parts = len(cells[0])
    _, _, dirs, cols = cells[0][0].shape
    first, count = rows
    hidden, total = w_in.shape
    width = min(cols, 512)

    def row_of(j, own_ref):
        return chunk_row(own_ref[0], first + j, chunk)

    def whole(shape):
        return pl.BlockSpec(shape, lambda j, c, own_ref: (0, 0))

    cell_specs = [
        pl.BlockSpec((1, many, dirs, width), lambda j, c, own_ref: (first + j, 0, 0, c)) for _, many in got for _ in range(parts)
    ]
    back_specs = [pl.BlockSpec((1, many, dirs, width), lambda j, c, own_ref: (j, 0, 0, c)) for _, many in sent for _ in range(parts)]
    outs = pl.pallas_call(
        functools.partial(source_kernel, parts, got, sent, dirs, 256, first, chunk),
        grid_spec=pltpu.PrefetchScalarGridSpec(
            num_scalar_prefetch=1,
            grid=(count, cols // width),
            in_specs=[
                UNREAD,
                pl.BlockSpec((1, total, width), lambda j, c, own_ref: (row_of(j, own_ref), 0, c)),
                pl.BlockSpec((wind.shape[0], width), lambda j, c, own_ref: (0, c)),
                whole((hidden, total)),
                whole((hidden, total)),
                whole((total, hidden)),
                whole((hidden, LANES)),
            ]
            + cell_specs,
            out_specs=[pl.BlockSpec((1, 1, width), lambda j, c, own_ref: (j, 0, c))] + back_specs,
            scratch_shapes=[
                pltpu.VMEM((total, width), jnp.float32),
                pltpu.VMEM((hidden, width), jnp.bfloat16),
                pltpu.VMEM((total, width), jnp.float32),
            ],
        ),
        out_shape=[jax.ShapeDtypeStruct((count, 1, cols), jnp.float32)]
        + [jax.ShapeDtypeStruct((count, many, dirs, cols), jnp.bfloat16) for _, many in sent for _ in range(parts)],
        compiler_params=pltpu.CompilerParams(vmem_limit_bytes=VMEM_LIMIT),
        cost_estimate=COST,
    )(own, after, state, wind, w_in, out_t, in_t, weight, *[cell for group in cells for cell in group])
    return outs[0], [list(outs[1 + g * parts : 1 + (g + 1) * parts]) for g in range(len(sent))]


def join_kernel(parts, spans, own_ref, _, home_ref, share_ref, *refs):
    out_ref, swap_ref = refs[-2:]
    dirs, rows, cols = home_ref.shape[1:]
    pitch = dirs + 1
    local = rows // parts
    own = own_ref[0]
    lanes = lane_tiles(cols)
    tiles = rows // TILE
    for i, (first, count, chunk) in enumerate(spans):
        for k in range(parts):
            owner = own ^ k
            for j in range(count):
                start = (owner * local + chunk_row(owner, first + j, chunk)) * pitch
                for c, here in enumerate(lanes):
                    swap_ref[c, pl.ds(start, dirs), :] = refs[i * parts + k][j, 0, :, here].astype(jnp.float32)

    def body(d, carry):
        for t in range(tiles):
            for c, here in enumerate(lanes):
                grown = swap_ref[c, pl.ds(t * TILE * pitch + d, TILE, stride=pitch), :]
                value = with_share(home_ref[0, d, pl.ds(t * TILE, TILE), here], share_ref, 0, d, here, t, tiles)
                out_ref[0, d, pl.ds(t * TILE, TILE), here] = value + grown
        return carry

    lax.fori_loop(0, dirs, body, 0, unroll=4)


def join(own, into, home, share, early, late, rows_of, chunks, group):
    begin, many = group
    parts = len(late)
    _, dirs, rows, cols = home.shape
    last = late[0].shape[0]
    spans = [(*span, chunks[0]) for span in rows_of] + [(0, last, chunks[-1])]
    width = cols // 2 if cols % (2 * LANES) == 0 else cols
    block = pl.BlockSpec((1, dirs, rows, width), lambda f, c: (begin + f, 0, 0, c))
    specs = [
        pl.BlockSpec((count, 1, dirs, width), lambda f, c: (0, begin + f, 0, c)) for _, count in rows_of for _ in range(parts)
    ] + [pl.BlockSpec((last, 1, dirs, width), lambda f, c: (0, f, 0, c))] * parts
    return pl.pallas_call(
        functools.partial(join_kernel, parts, spans),
        grid=(many, cols // width),
        in_specs=[pl.BlockSpec(memory_space=pltpu.SMEM), UNREAD, block]
        + [pl.BlockSpec((1, dirs, TILE, width), lambda f, c: (begin + f, 0, 0, c))]
        + specs,
        out_specs=block,
        out_shape=jax.ShapeDtypeStruct(home.shape, jnp.float32),
        scratch_shapes=[pltpu.VMEM((width // LANES, rows * (dirs + 1), LANES), jnp.float32)],
        input_output_aliases={} if begin == 0 else {1: 0},
        compiler_params=pltpu.CompilerParams(vmem_limit_bytes=VMEM_LIMIT),
        cost_estimate=COST,
    )(own, into, home, share, *[piece for pieces in early for piece in pieces], *late)


def arrived_kernel(held, *refs):
    refs[-1][...] = jnp.zeros_like(refs[-1])


def arrived(after, pieces, held=()):
    outs = pl.pallas_call(
        functools.partial(arrived_kernel, len(held)),
        in_specs=[UNREAD] * (1 + len(pieces) + len(held)),
        out_specs=[UNREAD] * len(held) + [pl.BlockSpec(memory_space=pltpu.VMEM)],
        out_shape=[jax.ShapeDtypeStruct(h.shape, h.dtype) for h in held] + [jax.ShapeDtypeStruct((TILE, LANES), jnp.float32)],
        input_output_aliases={1 + len(pieces) + i: i for i in range(len(held))},
        cost_estimate=COST,
    )(after, *pieces, *held)
    return outs[-1], list(outs[:-1])


def swapped(pieces):
    parts = len(pieces)
    moved = {k: lax.ppermute(pieces[k], "comp", [(i, i ^ k) for i in range(parts)]) for k in range(parts - 1, 0, -1)}
    return [pieces[0]] + [moved[k] for k in range(1, parts)]


def across(low, high):
    count = lax.axis_size("space")
    up = [(i, i + 1) for i in range(count - 1)]
    down = [(i + 1, i) for i in range(count - 1)]
    return lax.ppermute(high, "space", up), lax.ppermute(low, "space", down)


def shards(
    adjoint_forcing,
    forward_state,
    wind_speed,
    cg_index,
    turn_index,
    sea_mask,
    dir_sign,
    w_in,
    w_out,
    wind_weight,
):
    parts = lax.axis_size("comp")
    own_place = lax.axis_index("comp")
    own = own_place.astype(jnp.int32).reshape(1)
    dirs = dir_sign.shape[1]
    comps, rows, cols = adjoint_forcing.shape
    freqs = comps // dirs
    local = rows // parts
    along = (jnp.asarray(direction_factors(dirs)), jnp.asarray(spreads(dirs)[1]))
    forcing = adjoint_forcing.reshape(freqs, dirs, rows, cols)
    everything = [(0, freqs)]
    many = freqs // 2 if freqs % 2 == 0 else freqs
    groups = [(begin, many) for begin in range(0, freqs, many)]
    sent = groups
    levels = (cg_index, turn_index, sea_mask)
    if local > HALO:
        chunks = [(HALO, 0, local - HALO), (0, local - HALO, HALO)]
    else:
        chunks = [(0, 0, local)]
    ahead = chunks[0] if len(chunks) > 1 else None

    early, home, after = [], None, sea_mask
    for g, group in enumerate(groups):
        home, pieces = inner(own, dir_sign, along, after, forcing, *levels, home, parts, ahead, group)
        if ahead:
            early.append(swapped(pieces))
        if g == 0:
            low, high = edges(pieces[-1] if ahead else home, forcing, *levels)
            after = high
    above, below = across(low, high)
    after = home
    for pieces in early[:-1]:
        after, _ = arrived(after, pieces[1:])
    state = by_row((after,), forward_state)
    share, pieces = outer(own, dir_sign, along, state, above, below, *levels, home, parts, chunks[-1])
    late = swapped(pieces)
    in_t, out_t, weight = turned(share, w_in, w_out, wind_weight)
    term = functools.partial(source_term, own)
    fixed = (state, wind_speed, w_in, out_t, in_t, weight)
    after, grads, early_back, rows_of = in_t, [], [], []
    if ahead:
        count = ahead[2]
        some = 2 if count % 2 == 0 else 1
        rows_of = [(first, some) for first in range(0, count, some)]
    for n, span in enumerate(rows_of):
        if n == 1:
            after, _ = arrived(after, late[-1:])
        if n > 1:
            after, _ = arrived(after, early_back[n - 2][1:2])
        grad, [back] = term(after, *fixed, early, groups, everything, span, ahead)
        after = grad
        if not grads:
            after, rest = arrived(grad, late[1:-1] if len(rows_of) > 1 else late[1:], back[1:])
            back = [back[0], *rest]
        grads.append(grad)
        early_back.append(swapped(back))
    late_grad, late_back = term(after, *fixed, [late], everything, sent, (0, chunks[-1][2]), chunks[-1])
    start = late_grad
    if early_back:
        start, rest = arrived(start, early_back[0][1:], [piece for pieces in late_back for piece in pieces[1:]])
        step = parts - 1
        late_back = [[pieces[0], *rest[g * step : (g + 1) * step]] for g, pieces in enumerate(late_back)]
    late_back = [swapped(pieces) for pieces in late_back]
    if early_back:
        start, _ = arrived(start, early_back[-1][1:])
    for group, back in zip(sent, late_back, strict=True):
        start = join(own, start, home, share, early_back, back, rows_of, chunks, group)
    gradient = jnp.where(
        own_place == 0, jnp.concatenate([late_grad, *grads], axis=0), jnp.concatenate([*grads, late_grad], axis=0)
    )
    return (start.reshape(comps, rows, cols), gradient.reshape(wind_speed.shape))


def solution(mesh):
    placed = (
        P("comp", "space", None),
        P(None, ("space", "comp"), None),
        P(("space", "comp"), None),
        P("comp", "space", None),
        P("comp", "space", None),
        P("space", None),
        P(),
        P(),
        P(),
        P(),
    )
    return jax.shard_map(
        shards,
        mesh=mesh,
        in_specs=placed,
        out_specs=(P("comp", "space", None), P(("space", "comp"), None)),
        check_vma=False,
    )
```

```python
import functools
import math

import jax
import jax.numpy as jnp
import numpy as np
from jax import lax
from jax.experimental import pallas as pl
from jax.experimental.pallas import tpu as pltpu
from jax.sharding import PartitionSpec as P

HALO = 2
TILE = 8
LANES = 128
MIB = 1 << 20
VMEM_LIMIT = 64 * MIB
COST = pl.CostEstimate(flops=1, bytes_accessed=1, transcendentals=0)
LONG = pl.CostEstimate(flops=10**11, bytes_accessed=100 * MIB, transcendentals=0)


def direction_factors(dirs):
    angle = (np.arange(dirs, dtype=np.float32) + np.float32(0.5)) * np.float32(2.0 * math.pi / dirs)
    return np.stack([np.float32(0.5) * np.abs(np.cos(angle)), np.float32(0.5) * np.abs(np.sin(angle))])


def chunk_row(owner, j, chunk):
    return jnp.where(owner == 0, chunk[0], chunk[1]) + j


UNREAD = pl.BlockSpec(memory_space=pl.ANY)


def lane_tiles(cols):
    return [pl.ds(c * LANES, LANES) for c in range(cols // LANES)]


def spreads(dirs):
    both = direction_factors(dirs).sum(axis=0)
    values = []
    for value in both:
        if not any(abs(value - other) < 1e-5 for other in values):
            values.append(value)
    return values, np.array([[int(np.argmin([abs(b - v) for v in values])) for b in both]], np.int32)


def coefficients(dirs, cel_ref, kept_ref, trn_ref, here, cg, turn, sea):
    sea = sea.astype(jnp.float32)
    celerity = 0.1 + 0.8 * cg.astype(jnp.float32) / 7.0
    turning = 0.3 * jnp.abs(turn.astype(jnp.float32) - 3.5) / 3.5
    cel_ref[here, :] = celerity * sea
    trn_ref[here, :] = turning * sea
    for n, both in enumerate(spreads(dirs)[0]):
        kept_ref[n, here, :] = (1.0 - float(both) * celerity - turning) * sea


def sweep(dirs, tiles, alone, lanes, sign_ref, along_ref, kind_ref, coefs, turns_up, load, store):
    cel_ref, kept_ref, trn_ref = coefs
    row = lax.broadcasted_iota(jnp.int32, (TILE, LANES), 0)
    lane = lax.broadcasted_iota(jnp.int32, (TILE, LANES), 1)
    nothing = jnp.zeros((TILE, LANES), jnp.float32)

    def span(t):
        return pl.ds(t * TILE, TILE)

    def one(d, carry):
        following = jnp.where(d == dirs - 1, 0, d + 1)
        previous = jnp.where(d == 0, dirs - 1, d - 1)
        ax = along_ref[0, d]
        ay = along_ref[1, d]
        kind = kind_ref[0, d]
        right = sign_ref[0, d] > 0
        high = sign_ref[1, d] > 0
        shift_x = jnp.where(right, LANES - 1, 1)
        shift_y = jnp.where(high, TILE - 1, 1)
        at_right = lane == jnp.where(right, LANES - 1, LANES)
        at_left = lane == jnp.where(right, LANES, 0)
        at_high = row == jnp.where(high, TILE - 1, TILE)
        at_low = row == jnp.where(high, TILE, 0)
        at_edge = row == jnp.where(high, TILE - 1, 0)

        def column(c):
            here = [load(t, d, lanes[c]) for t in range(tiles)]
            flow = [cel_ref[span(t), lanes[c]] * here[t] for t in range(tiles)]
            return here, flow, [pltpu.roll(f, shift_x, 1) for f in flow]

        before = [nothing] * tiles
        here, flow, moved = column(0)
        for c in range(len(lanes)):
            beyond = [nothing] * tiles
            if c + 1 < len(lanes):
                later = column(c + 1)
                beyond = later[2]
            lifted = [pltpu.roll(f, shift_y, 0) for f in flow]
            for t in range(tiles):
                flow_x = jnp.where(at_right, beyond[t], jnp.where(at_left, before[t], moved[t]))
                if alone:
                    flow_y = jnp.where(at_edge, nothing, lifted[t])
                else:
                    above = lifted[t + 1] if t + 1 < tiles else nothing
                    below = lifted[t - 1] if t > 0 else nothing
                    flow_y = jnp.where(at_high, above, jnp.where(at_low, below, lifted[t]))
                turned = jnp.where(turns_up(t, c), load(t, following, lanes[c]), load(t, previous, lanes[c]))
                total = kept_ref[kind, span(t), lanes[c]] * here[t] + ax * flow_x
                total = total + (ay * flow_y + trn_ref[span(t), lanes[c]] * turned)
                store(t, d, c, total)
            if c + 1 < len(lanes):
                before = moved
                here, flow, moved = later
        return carry

    lax.fori_loop(0, dirs, one, 0, unroll=6)


def emit(own, parts, local, chunk, dirs, lanes, swap_ref, send_refs):
    for k in range(parts):
        owner = own ^ k
        for j in range(chunk[2]):
            start = (owner * local + chunk_row(owner, j, chunk)) * (dirs + 1)
            for c, here in enumerate(lanes):
                send_refs[k][j, 0, :, here] = swap_ref[c, pl.ds(start, dirs), :].astype(jnp.bfloat16)


def inner_kernel(parts, local, chunk, into, own_ref, sign_ref, along_ref, kind_ref, _, forcing_ref, cg_ref, turn_ref, mask_ref, *refs):
    refs = refs[1:] if into else refs
    home_ref = refs[0]
    sends = parts if chunk else 0
    cel_ref, kept_ref, trn_ref, first_ref, swap_ref = refs[sends + 1 :]
    dirs, rows, cols = forcing_ref.shape[1:]
    pitch = dirs + 1
    lanes = lane_tiles(cols)
    tiles = rows // TILE

    def span(t):
        return pl.ds(t * TILE, TILE)

    for t in range(tiles):
        levels = (cg_ref[0, span(t), :], turn_ref[0, span(t), :], mask_ref[span(t), :])
        coefficients(dirs, cel_ref, kept_ref, trn_ref, span(t), *levels)

    def turns_up(t, c):
        return turn_ref[0, span(t), lanes[c]] >= 4

    def store_first(t, d, c, value):
        first_ref[d, span(t), lanes[c]] = value

    def store_last(t, d, c, value):
        home_ref[0, d, span(t), lanes[c]] = value
        if chunk:
            swap_ref[c, pl.ds(t * TILE * pitch + d, TILE, stride=pitch), :] = value

    coefs = (cel_ref, kept_ref, trn_ref)
    step = functools.partial(sweep, dirs, tiles, False, lanes, sign_ref, along_ref, kind_ref, coefs, turns_up)
    step(lambda t, d, here: forcing_ref[0, d, span(t), here], store_first)
    step(lambda t, d, here: first_ref[d, span(t), here], store_last)
    if chunk:
        emit(own_ref[0], parts, local, chunk, dirs, lanes, swap_ref, refs[1 : sends + 1])


def inner(own, signs, along, after, forcing, cg, turn, mask, into, parts, chunk, group):
    freqs, dirs, rows, cols = forcing.shape
    begin, many = group
    local = rows // parts
    smem = pl.BlockSpec(memory_space=pltpu.SMEM)
    levels = pl.BlockSpec((1, rows, cols), lambda f: (begin + f, 0, 0))
    block = pl.BlockSpec((1, dirs, rows, cols), lambda f: (begin + f, 0, 0, 0))
    coefs = pltpu.VMEM((rows, cols), jnp.float32)
    sends = parts if chunk else 0
    count = chunk[2] if chunk else 0
    outs = pl.pallas_call(
        functools.partial(inner_kernel, parts, local, chunk, into is not None),
        grid=(many,),
        in_specs=[smem, smem, smem, smem, UNREAD, block, levels, levels, pl.BlockSpec((rows, cols), lambda f: (0, 0))]
        + ([] if into is None else [UNREAD]),
        out_specs=[block] + [pl.BlockSpec((count, 1, dirs, cols), lambda f: (0, f, 0, 0))] * sends,
        out_shape=[jax.ShapeDtypeStruct(forcing.shape, jnp.float32)]
        + [jax.ShapeDtypeStruct((count, many, dirs, cols), jnp.bfloat16)] * sends,
        scratch_shapes=[
            coefs,
            pltpu.VMEM((len(spreads(dirs)[0]), rows, cols), jnp.float32),
            coefs,
            pltpu.VMEM((dirs, rows, cols), jnp.float32),
            pltpu.VMEM((cols // LANES, rows * (dirs + 1), LANES), jnp.float32),
        ],
        input_output_aliases={} if into is None else {9: 0},
        compiler_params=pltpu.CompilerParams(vmem_limit_bytes=VMEM_LIMIT),
        cost_estimate=COST,
    )(own, signs, *along, after, forcing, cg, turn, mask, *([] if into is None else [into]))
    return outs[0], list(outs[1:])


def edges_kernel(_, *refs):
    swap_ref, edge_ref = refs[-2:]
    dirs, _, cols = refs[0].shape[1:]
    pitch = dirs + 1
    lanes = lane_tiles(cols)
    edge_ref[...] = jnp.zeros_like(edge_ref)
    for side, low in ((0, 0), (1, TILE - HALO)):
        forcing_ref, cg_ref, turn_ref, mask_ref = refs[4 * side : 4 * side + 4]
        out_ref = refs[8 + side]

        def body(d, carry, forcing_ref=forcing_ref):
            for c, here in enumerate(lanes):
                swap_ref[c, pl.ds(d, TILE, stride=pitch), :] = forcing_ref[0, d, :, here]
            return carry

        lax.fori_loop(0, dirs, body, 0, unroll=12)
        for r in range(HALO):
            for c, here in enumerate(lanes):
                edge_ref[:dirs, here] = swap_ref[c, pl.ds((low + r) * pitch, dirs), :]
            for n, level in enumerate((cg_ref[0], turn_ref[0], mask_ref[...])):
                edge_ref[dirs + n : dirs + n + 1, :] = level[low + r : low + r + 1].astype(jnp.float32)
            out_ref[r, 0] = edge_ref[...].astype(jnp.bfloat16)


def edges(after, forcing, cg, turn, mask):
    freqs, dirs, rows, cols = forcing.shape
    out = pl.BlockSpec((HALO, 1, dirs + TILE, cols), lambda f: (0, f, 0, 0))
    shape = jax.ShapeDtypeStruct((HALO, freqs, dirs + TILE, cols), jnp.bfloat16)
    in_specs = [UNREAD]
    for t in (0, rows // TILE - 1):
        in_specs += [
            pl.BlockSpec((1, dirs, TILE, cols), lambda f, t=t: (f, 0, t, 0)),
            pl.BlockSpec((1, TILE, cols), lambda f, t=t: (f, t, 0)),
            pl.BlockSpec((1, TILE, cols), lambda f, t=t: (f, t, 0)),
            pl.BlockSpec((TILE, cols), lambda f, t=t: (t, 0)),
        ]
    return pl.pallas_call(
        edges_kernel,
        grid=(freqs,),
        in_specs=in_specs,
        out_specs=[out, out],
        out_shape=[shape, shape],
        scratch_shapes=[
            pltpu.VMEM((cols // LANES, TILE * (dirs + 1), LANES), jnp.float32),
            pltpu.VMEM((dirs + TILE, cols), jnp.float32),
        ],
        compiler_params=pltpu.CompilerParams(vmem_limit_bytes=VMEM_LIMIT),
        cost_estimate=COST,
    )(after, *(2 * [forcing, cg, turn, mask]))


def outer_kernel(parts, local, chunk, *refs):
    own_ref, sign_ref, along_ref, kind_ref, _, above_ref, below_ref = refs[:7]
    cg_ref, turn_ref, mask_ref, home_ref, share_ref = refs[7:12]
    send_refs = refs[12 : 12 + parts]
    cel_ref, kept_ref, trn_ref, up_ref, lev_ref, near_ref, first_ref, side_ref, edge_ref, swap_ref = refs[12 + parts :]
    dirs, rows, cols = home_ref.shape[1:]
    freqs = share_ref.shape[0]
    pitch = dirs + 1
    lanes = lane_tiles(cols)
    tiles = rows // TILE
    f = pl.program_id(0)

    def span(t):
        return pl.ds(t * TILE, TILE)

    @pl.when(f == 0)
    def _():
        edge_ref[...] = jnp.zeros_like(edge_ref)
        beyond = ((above_ref, 0, 0), (above_ref, 1, 1), (below_ref, 0, TILE - HALO), (below_ref, 1, TILE - 1))
        for n in range(freqs):
            for i, (ref, r, low) in enumerate(beyond):
                for c, here in enumerate(lanes):
                    piece = ref[r, n, :, here].astype(jnp.float32)
                    edge_ref[c, pl.ds(low * pitch, dirs), :] = piece[:dirs]
                    lev_ref[i * TILE : (i + 1) * TILE, here] = piece[dirs:]

            def gather(d, carry, n=n):
                for c, here in enumerate(lanes):
                    side_ref[d, span(n), here] = edge_ref[c, pl.ds(d, TILE, stride=pitch), :]
                return carry

            lax.fori_loop(0, dirs, gather, 0, unroll=12)
            for q, mine in enumerate((cg_ref[n], turn_ref[n], mask_ref[...])):
                for i, (_, _, low) in enumerate(beyond):
                    near_ref[q * TILE + low : q * TILE + low + 1, :] = lev_ref[i * TILE + q : i * TILE + q + 1, :]
                near_ref[q * TILE + HALO : q * TILE + 2 * HALO, :] = mine[:HALO].astype(jnp.float32)
                near_ref[q * TILE + 2 * HALO : q * TILE + 3 * HALO, :] = mine[rows - HALO :].astype(jnp.float32)
            coefficients(dirs, cel_ref, kept_ref, trn_ref, span(n), *[near_ref[span(q), :] for q in range(3)])
            up_ref[span(n), :] = near_ref[span(1), :]

        def turns_up(t, c):
            return up_ref[span(t), lanes[c]] >= 4.0

        def store_first(t, d, c, value):
            first_ref[d, span(t), lanes[c]] = value

        def store_last(t, d, c, value):
            share_ref[t, d, :, lanes[c]] = value

        coefs = (cel_ref, kept_ref, trn_ref)
        step = functools.partial(sweep, dirs, freqs, True, lanes, sign_ref, along_ref, kind_ref, coefs, turns_up)
        step(lambda t, d, here: side_ref[d, span(t), here], store_first)
        step(lambda t, d, here: first_ref[d, span(t), here], store_last)

    def whole(d, carry):
        for t in range(tiles):
            for c, here in enumerate(lanes):
                value = with_share(home_ref[0, d, span(t), here], share_ref, f, d, here, t, tiles)
                swap_ref[c, pl.ds(t * TILE * pitch + d, TILE, stride=pitch), :] = value
        return carry

    lax.fori_loop(0, dirs, whole, 0, unroll=4)
    emit(own_ref[0], parts, local, chunk, dirs, lanes, swap_ref, send_refs)


def with_share(value, share_ref, f, d, here, t, tiles):
    row = lax.broadcasted_iota(jnp.int32, value.shape, 0)
    if t == 0:
        value = value + jnp.where(row < HALO, pltpu.roll(share_ref[f, d, :, here], TILE - HALO, 0), 0.0)
    if t == tiles - 1:
        value = value + jnp.where(row >= TILE - HALO, pltpu.roll(share_ref[f, d, :, here], HALO, 0), 0.0)
    return value


def outer(own, signs, along, after, above, below, cg, turn, mask, home, parts, chunk):
    freqs, dirs, rows, cols = home.shape
    local = rows // parts
    smem = pl.BlockSpec(memory_space=pltpu.SMEM)
    edge = pl.BlockSpec((HALO, freqs, dirs + TILE, cols), lambda f: (0, 0, 0, 0))
    levels = pl.BlockSpec((freqs, rows, cols), lambda f: (0, 0, 0))
    tall = pltpu.VMEM((freqs * TILE, cols), jnp.float32)
    outs = pl.pallas_call(
        functools.partial(outer_kernel, parts, local, chunk),
        grid=(freqs,),
        in_specs=[smem, smem, smem, smem, UNREAD, edge, edge, levels, levels]
        + [pl.BlockSpec((rows, cols), lambda f: (0, 0)), pl.BlockSpec((1, dirs, rows, cols), lambda f: (f, 0, 0, 0))],
        out_specs=[pl.BlockSpec((freqs, dirs, TILE, cols), lambda f: (0, 0, 0, 0))]
        + [pl.BlockSpec((chunk[2], 1, dirs, cols), lambda f: (0, f, 0, 0))] * parts,
        out_shape=[jax.ShapeDtypeStruct((freqs, dirs, TILE, cols), jnp.float32)]
        + [jax.ShapeDtypeStruct((chunk[2], freqs, dirs, cols), jnp.bfloat16)] * parts,
        scratch_shapes=[
            tall,
            pltpu.VMEM((len(spreads(dirs)[0]), freqs * TILE, cols), jnp.float32),
            tall,
            tall,
            pltpu.VMEM((2 * HALO * TILE, cols), jnp.float32),
            pltpu.VMEM((3 * TILE, cols), jnp.float32),
            pltpu.VMEM((dirs, freqs * TILE, cols), jnp.float32),
            pltpu.VMEM((dirs, freqs * TILE, cols), jnp.float32),
            pltpu.VMEM((cols // LANES, TILE * (dirs + 1), LANES), jnp.float32),
            pltpu.VMEM((cols // LANES, rows * (dirs + 1), LANES), jnp.float32),
        ],
        compiler_params=pltpu.CompilerParams(vmem_limit_bytes=VMEM_LIMIT),
        cost_estimate=LONG,
    )(own, signs, *along, after, above, below, cg, turn, mask, home)
    return outs[0], list(outs[1:])


def by_row_kernel(*refs):
    state_ref, out_ref, swap_ref = refs[-3:]
    some, local, cols = state_ref.shape
    pitch = some + 1
    lanes = lane_tiles(cols)

    def body(d, carry):
        for c, here in enumerate(lanes):
            swap_ref[c, pl.ds(d, local, stride=pitch), :] = state_ref[d, :, here].astype(jnp.float32)
        return carry

    lax.fori_loop(0, some, body, 0, unroll=8)
    for r in range(local):
        for c, here in enumerate(lanes):
            out_ref[r, :, here] = swap_ref[c, pl.ds(r * pitch, some), :].astype(jnp.bfloat16)


def by_row(after, state):
    deep, local, cols = state.shape
    some = 48
    return pl.pallas_call(
        by_row_kernel,
        grid=(deep // some,),
        in_specs=[UNREAD] * len(after) + [pl.BlockSpec((some, local, cols), lambda d: (d, 0, 0))],
        out_specs=pl.BlockSpec((local, some, cols), lambda d: (0, d, 0)),
        out_shape=jax.ShapeDtypeStruct((local, deep, cols), jnp.bfloat16),
        scratch_shapes=[pltpu.VMEM((cols // LANES, local * (some + 1), LANES), jnp.float32)],
        compiler_params=pltpu.CompilerParams(vmem_limit_bytes=VMEM_LIMIT),
        cost_estimate=COST,
    )(*after, state)


def turned_kernel(_, w_in_ref, w_out_ref, weight_ref, in_t_ref, out_t_ref, column_ref):
    in_t_ref[...] = w_in_ref[...].T
    out_t_ref[...] = w_out_ref[...].T

    @pl.when(pl.program_id(0) == 0)
    def _():
        column_ref[...] = jnp.broadcast_to(weight_ref[...][None, :], (LANES, weight_ref.shape[0])).T


def turned(after, w_in, w_out, weight):
    hidden, total = w_in.shape
    step = 512
    tall = pl.BlockSpec((step, total), lambda h: (h, 0))
    wide = pl.BlockSpec((total, step), lambda h: (0, h))
    return pl.pallas_call(
        turned_kernel,
        grid=(hidden // step,),
        in_specs=[UNREAD, tall, wide, pl.BlockSpec(memory_space=pltpu.VMEM)],
        out_specs=[wide, tall, pl.BlockSpec((hidden, LANES), lambda h: (0, 0))],
        out_shape=[
            jax.ShapeDtypeStruct((total, hidden), w_in.dtype),
            jax.ShapeDtypeStruct((hidden, total), w_in.dtype),
            jax.ShapeDtypeStruct((hidden, LANES), jnp.float32),
        ],
        compiler_params=pltpu.CompilerParams(vmem_limit_bytes=VMEM_LIMIT),
        cost_estimate=LONG,
    )(after, w_in, w_out, weight)


def source_kernel(parts, got, sent, dirs, step, first, chunk, own_ref, _, state_ref, wind_ref, w_in_ref, out_t_ref, in_t_ref, weight_ref, *refs):
    cell_refs = refs[: parts * len(got)]
    grad_ref = refs[parts * len(got)]
    back_refs = refs[parts * len(got) + 1 : -3]
    cell_ref, weighted_ref, grown_ref = refs[-3:]
    freqs = sum(many for _, many in got)
    hidden, width = weighted_ref.shape
    own = own_ref[0]

    def place(k, group):
        begin, many = group
        return pl.ds(pl.multiple_of(((own ^ k) * freqs + begin) * dirs, TILE), many * dirs)

    for g, group in enumerate(got):
        for k in range(parts):
            piece = cell_refs[g * parts + k][0].astype(jnp.float32)
            cell_ref[place(k, group), :] = piece.reshape(group[1] * dirs, width)
    cell = cell_ref[...].astype(jnp.bfloat16)
    state = state_ref[0]
    wind = wind_ref[pl.ds(chunk_row(own, first + pl.program_id(0), chunk), 1), :]
    grad = jnp.zeros((TILE, width), jnp.float32)
    for h in range(0, hidden, step):
        some = pl.ds(h, step)
        weight = weight_ref[some, :1]
        forward = jnp.dot(w_in_ref[some, :], state, preferred_element_type=jnp.float32) + weight * wind
        squash = jnp.tanh(forward)
        pulled = jnp.dot(out_t_ref[some, :], cell, preferred_element_type=jnp.float32)
        weighted = (1.0 - squash * squash) * pulled
        weighted_ref[some, :] = weighted.astype(jnp.bfloat16)
        grad = grad + jnp.sum((weight * weighted).reshape(step // TILE, TILE, width), axis=0)
    grad_ref[0] = jnp.sum(grad, axis=0, keepdims=True)
    grown_ref[...] = jnp.dot(in_t_ref[...], weighted_ref[...], preferred_element_type=jnp.float32)
    for g, group in enumerate(sent):
        for k in range(parts):
            grown = grown_ref[place(k, group), :].reshape(group[1], dirs, width)
            back_refs[g * parts + k][0] = grown.astype(jnp.bfloat16)


def source_term(own, after, state, wind, w_in, out_t, in_t, weight, cells, got, sent, rows, chunk):
    parts = len(cells[0])
    _, _, dirs, cols = cells[0][0].shape
    first, count = rows
    hidden, total = w_in.shape
    width = min(cols, 512)

    def row_of(j, own_ref):
        return chunk_row(own_ref[0], first + j, chunk)

    def whole(shape):
        return pl.BlockSpec(shape, lambda j, c, own_ref: (0, 0))

    cell_specs = [
        pl.BlockSpec((1, many, dirs, width), lambda j, c, own_ref: (first + j, 0, 0, c)) for _, many in got for _ in range(parts)
    ]
    back_specs = [pl.BlockSpec((1, many, dirs, width), lambda j, c, own_ref: (j, 0, 0, c)) for _, many in sent for _ in range(parts)]
    outs = pl.pallas_call(
        functools.partial(source_kernel, parts, got, sent, dirs, 256, first, chunk),
        grid_spec=pltpu.PrefetchScalarGridSpec(
            num_scalar_prefetch=1,
            grid=(count, cols // width),
            in_specs=[
                UNREAD,
                pl.BlockSpec((1, total, width), lambda j, c, own_ref: (row_of(j, own_ref), 0, c)),
                pl.BlockSpec((wind.shape[0], width), lambda j, c, own_ref: (0, c)),
                whole((hidden, total)),
                whole((hidden, total)),
                whole((total, hidden)),
                whole((hidden, LANES)),
            ]
            + cell_specs,
            out_specs=[pl.BlockSpec((1, 1, width), lambda j, c, own_ref: (j, 0, c))] + back_specs,
            scratch_shapes=[
                pltpu.VMEM((total, width), jnp.float32),
                pltpu.VMEM((hidden, width), jnp.bfloat16),
                pltpu.VMEM((total, width), jnp.float32),
            ],
        ),
        out_shape=[jax.ShapeDtypeStruct((count, 1, cols), jnp.float32)]
        + [jax.ShapeDtypeStruct((count, many, dirs, cols), jnp.bfloat16) for _, many in sent for _ in range(parts)],
        compiler_params=pltpu.CompilerParams(vmem_limit_bytes=VMEM_LIMIT),
        cost_estimate=COST,
    )(own, after, state, wind, w_in, out_t, in_t, weight, *[cell for group in cells for cell in group])
    return outs[0], [list(outs[1 + g * parts : 1 + (g + 1) * parts]) for g in range(len(sent))]


def join_kernel(parts, spans, own_ref, _, home_ref, share_ref, *refs):
    out_ref, swap_ref = refs[-2:]
    dirs, rows, cols = home_ref.shape[1:]
    pitch = dirs + 1
    local = rows // parts
    own = own_ref[0]
    lanes = lane_tiles(cols)
    tiles = rows // TILE
    for i, (first, count, chunk) in enumerate(spans):
        for k in range(parts):
            owner = own ^ k
            for j in range(count):
                start = (owner * local + chunk_row(owner, first + j, chunk)) * pitch
                for c, here in enumerate(lanes):
                    swap_ref[c, pl.ds(start, dirs), :] = refs[i * parts + k][j, 0, :, here].astype(jnp.float32)

    def body(d, carry):
        for t in range(tiles):
            for c, here in enumerate(lanes):
                grown = swap_ref[c, pl.ds(t * TILE * pitch + d, TILE, stride=pitch), :]
                value = with_share(home_ref[0, d, pl.ds(t * TILE, TILE), here], share_ref, 0, d, here, t, tiles)
                out_ref[0, d, pl.ds(t * TILE, TILE), here] = value + grown
        return carry

    lax.fori_loop(0, dirs, body, 0, unroll=2)


def join(own, into, home, share, early, late, rows_of, chunks, group):
    begin, many = group
    parts = len(late)
    _, dirs, rows, cols = home.shape
    last = late[0].shape[0]
    spans = [(*span, chunks[0]) for span in rows_of] + [(0, last, chunks[-1])]
    block = pl.BlockSpec((1, dirs, rows, cols), lambda f: (begin + f, 0, 0, 0))
    specs = [
        pl.BlockSpec((count, 1, dirs, cols), lambda f: (0, begin + f, 0, 0)) for _, count in rows_of for _ in range(parts)
    ] + [pl.BlockSpec((last, 1, dirs, cols), lambda f: (0, f, 0, 0))] * parts
    return pl.pallas_call(
        functools.partial(join_kernel, parts, spans),
        grid=(many,),
        in_specs=[pl.BlockSpec(memory_space=pltpu.SMEM), UNREAD, block]
        + [pl.BlockSpec((1, dirs, TILE, cols), lambda f: (begin + f, 0, 0, 0))]
        + specs,
        out_specs=block,
        out_shape=jax.ShapeDtypeStruct(home.shape, jnp.float32),
        scratch_shapes=[pltpu.VMEM((cols // LANES, rows * (dirs + 1), LANES), jnp.float32)],
        input_output_aliases={} if begin == 0 else {1: 0},
        compiler_params=pltpu.CompilerParams(vmem_limit_bytes=VMEM_LIMIT),
        cost_estimate=COST,
    )(own, into, home, share, *[piece for pieces in early for piece in pieces], *late)


def arrived_kernel(held, *refs):
    refs[-1][...] = jnp.zeros_like(refs[-1])


def arrived(after, pieces, held=()):
    outs = pl.pallas_call(
        functools.partial(arrived_kernel, len(held)),
        in_specs=[UNREAD] * (1 + len(pieces) + len(held)),
        out_specs=[UNREAD] * len(held) + [pl.BlockSpec(memory_space=pltpu.VMEM)],
        out_shape=[jax.ShapeDtypeStruct(h.shape, h.dtype) for h in held] + [jax.ShapeDtypeStruct((TILE, LANES), jnp.float32)],
        input_output_aliases={1 + len(pieces) + i: i for i in range(len(held))},
        cost_estimate=COST,
    )(after, *pieces, *held)
    return outs[-1], list(outs[:-1])


def swapped(pieces):
    parts = len(pieces)
    moved = {k: lax.ppermute(pieces[k], "comp", [(i, i ^ k) for i in range(parts)]) for k in range(parts - 1, 0, -1)}
    return [pieces[0]] + [moved[k] for k in range(1, parts)]


def across(low, high):
    count = lax.axis_size("space")
    up = [(i, i + 1) for i in range(count - 1)]
    down = [(i + 1, i) for i in range(count - 1)]
    return lax.ppermute(high, "space", up), lax.ppermute(low, "space", down)


def shards(
    adjoint_forcing,
    forward_state,
    wind_speed,
    cg_index,
    turn_index,
    sea_mask,
    dir_sign,
    w_in,
    w_out,
    wind_weight,
):
    parts = lax.axis_size("comp")
    own_place = lax.axis_index("comp")
    own = own_place.astype(jnp.int32).reshape(1)
    dirs = dir_sign.shape[1]
    comps, rows, cols = adjoint_forcing.shape
    freqs = comps // dirs
    local = rows // parts
    along = (jnp.asarray(direction_factors(dirs)), jnp.asarray(spreads(dirs)[1]))
    forcing = adjoint_forcing.reshape(freqs, dirs, rows, cols)
    everything = [(0, freqs)]
    many = freqs // 2 if freqs % 2 == 0 else freqs
    groups = [(begin, many) for begin in range(0, freqs, many)]
    sent = groups
    levels = (cg_index, turn_index, sea_mask)
    if local > HALO:
        chunks = [(HALO, 0, local - HALO), (0, local - HALO, HALO)]
    else:
        chunks = [(0, 0, local)]
    ahead = chunks[0] if len(chunks) > 1 else None

    early, home, after = [], None, sea_mask
    for g, group in enumerate(groups):
        home, pieces = inner(own, dir_sign, along, after, forcing, *levels, home, parts, ahead, group)
        if ahead:
            early.append(swapped(pieces))
        if g == 0:
            low, high = edges(pieces[-1] if ahead else home, forcing, *levels)
            after = high
    above, below = across(low, high)
    after = home
    for pieces in early[:-1]:
        after, _ = arrived(after, pieces[1:])
    state = by_row((after,), forward_state)
    share, pieces = outer(own, dir_sign, along, state, above, below, *levels, home, parts, chunks[-1])
    late = swapped(pieces)
    in_t, out_t, weight = turned(share, w_in, w_out, wind_weight)
    term = functools.partial(source_term, own)
    fixed = (state, wind_speed, w_in, out_t, in_t, weight)
    after, grads, early_back, rows_of = in_t, [], [], []
    if ahead:
        count = ahead[2]
        some = 2 if count % 2 == 0 else 1
        rows_of = [(first, some) for first in range(0, count, some)]
    for n, span in enumerate(rows_of):
        if n == 1:
            after, _ = arrived(after, late[-1:])
        if n > 1:
            after, _ = arrived(after, early_back[n - 2][1:2])
        grad, [back] = term(after, *fixed, early, groups, everything, span, ahead)
        after = grad
        if not grads:
            after, rest = arrived(grad, late[1:-1] if len(rows_of) > 1 else late[1:], back[1:])
            back = [back[0], *rest]
        grads.append(grad)
        early_back.append(swapped(back))
    late_grad, late_back = term(after, *fixed, [late], everything, sent, (0, chunks[-1][2]), chunks[-1])
    start = late_grad
    if early_back:
        start, rest = arrived(start, early_back[0][1:], [piece for pieces in late_back for piece in pieces[1:]])
        step = parts - 1
        late_back = [[pieces[0], *rest[g * step : (g + 1) * step]] for g, pieces in enumerate(late_back)]
    late_back = [swapped(pieces) for pieces in late_back]
    if early_back:
        start, _ = arrived(start, early_back[-1][1:])
    for group, back in zip(sent, late_back, strict=True):
        start = join(own, start, home, share, early_back, back, rows_of, chunks, group)
    gradient = jnp.where(
        own_place == 0, jnp.concatenate([late_grad, *grads], axis=0), jnp.concatenate([*grads, late_grad], axis=0)
    )
    return (start.reshape(comps, rows, cols), gradient.reshape(wind_speed.shape))


def solution(mesh):
    placed = (
        P("comp", "space", None),
        P(None, ("space", "comp"), None),
        P(("space", "comp"), None),
        P("comp", "space", None),
        P("comp", "space", None),
        P("space", None),
        P(),
        P(),
        P(),
        P(),
    )
    return jax.shard_map(
        shards,
        mesh=mesh,
        in_specs=placed,
        out_specs=(P("comp", "space", None), P(("space", "comp"), None)),
        check_vma=False,
    )
```

```python
import functools
import math

import jax
import jax.numpy as jnp
import numpy as np
from jax import lax
from jax.experimental import pallas as pl
from jax.experimental.pallas import tpu as pltpu
from jax.sharding import PartitionSpec as P

HALO = 2
TILE = 8
LANES = 128
MIB = 1 << 20
VMEM_LIMIT = 64 * MIB
COST = pl.CostEstimate(flops=1, bytes_accessed=1, transcendentals=0)
LONG = pl.CostEstimate(flops=10**11, bytes_accessed=100 * MIB, transcendentals=0)


def direction_factors(dirs):
    angle = (np.arange(dirs, dtype=np.float32) + np.float32(0.5)) * np.float32(2.0 * math.pi / dirs)
    return np.stack([np.float32(0.5) * np.abs(np.cos(angle)), np.float32(0.5) * np.abs(np.sin(angle))])


def chunk_row(owner, j, chunk):
    return jnp.where(owner == 0, chunk[0], chunk[1]) + j


UNREAD = pl.BlockSpec(memory_space=pl.ANY)


def lane_tiles(cols):
    return [pl.ds(c * LANES, LANES) for c in range(cols // LANES)]


def spreads(dirs):
    both = direction_factors(dirs).sum(axis=0)
    values = []
    for value in both:
        if not any(abs(value - other) < 1e-5 for other in values):
            values.append(value)
    return values, np.array([[int(np.argmin([abs(b - v) for v in values])) for b in both]], np.int32)


def coefficients(dirs, cel_ref, kept_ref, trn_ref, here, cg, turn, sea):
    sea = sea.astype(jnp.float32)
    celerity = 0.1 + 0.8 * cg.astype(jnp.float32) / 7.0
    turning = 0.3 * jnp.abs(turn.astype(jnp.float32) - 3.5) / 3.5
    cel_ref[here, :] = celerity * sea
    trn_ref[here, :] = turning * sea
    for n, both in enumerate(spreads(dirs)[0]):
        kept_ref[n, here, :] = (1.0 - float(both) * celerity - turning) * sea


def sweep(dirs, tiles, alone, lanes, sign_ref, along_ref, kind_ref, coefs, turns_up, load, store):
    cel_ref, kept_ref, trn_ref = coefs
    row = lax.broadcasted_iota(jnp.int32, (TILE, LANES), 0)
    lane = lax.broadcasted_iota(jnp.int32, (TILE, LANES), 1)
    nothing = jnp.zeros((TILE, LANES), jnp.float32)

    def span(t):
        return pl.ds(t * TILE, TILE)

    def one(d, carry):
        following = jnp.where(d == dirs - 1, 0, d + 1)
        previous = jnp.where(d == 0, dirs - 1, d - 1)
        ax = along_ref[0, d]
        ay = along_ref[1, d]
        kind = kind_ref[0, d]
        right = sign_ref[0, d] > 0
        high = sign_ref[1, d] > 0
        shift_x = jnp.where(right, LANES - 1, 1)
        shift_y = jnp.where(high, TILE - 1, 1)
        at_right = lane == jnp.where(right, LANES - 1, LANES)
        at_left = lane == jnp.where(right, LANES, 0)
        at_high = row == jnp.where(high, TILE - 1, TILE)
        at_low = row == jnp.where(high, TILE, 0)
        at_edge = row == jnp.where(high, TILE - 1, 0)

        def column(c):
            here = [load(t, d, lanes[c]) for t in range(tiles)]
            flow = [cel_ref[span(t), lanes[c]] * here[t] for t in range(tiles)]
            return here, flow, [pltpu.roll(f, shift_x, 1) for f in flow]

        before = [nothing] * tiles
        here, flow, moved = column(0)
        for c in range(len(lanes)):
            beyond = [nothing] * tiles
            if c + 1 < len(lanes):
                later = column(c + 1)
                beyond = later[2]
            lifted = [pltpu.roll(f, shift_y, 0) for f in flow]
            for t in range(tiles):
                flow_x = jnp.where(at_right, beyond[t], jnp.where(at_left, before[t], moved[t]))
                if alone:
                    flow_y = jnp.where(at_edge, nothing, lifted[t])
                else:
                    above = lifted[t + 1] if t + 1 < tiles else nothing
                    below = lifted[t - 1] if t > 0 else nothing
                    flow_y = jnp.where(at_high, above, jnp.where(at_low, below, lifted[t]))
                turned = jnp.where(turns_up(t, c), load(t, following, lanes[c]), load(t, previous, lanes[c]))
                total = kept_ref[kind, span(t), lanes[c]] * here[t] + ax * flow_x
                total = total + (ay * flow_y + trn_ref[span(t), lanes[c]] * turned)
                store(t, d, c, total)
            if c + 1 < len(lanes):
                before = moved
                here, flow, moved = later
        return carry

    lax.fori_loop(0, dirs, one, 0, unroll=12)


def emit(own, parts, local, chunk, dirs, lanes, swap_ref, send_refs):
    for k in range(parts):
        owner = own ^ k
        for j in range(chunk[2]):
            start = (owner * local + chunk_row(owner, j, chunk)) * (dirs + 1)
            for c, here in enumerate(lanes):
                send_refs[k][j, 0, :, here] = swap_ref[c, pl.ds(start, dirs), :].astype(jnp.bfloat16)


def inner_kernel(parts, local, chunk, into, own_ref, sign_ref, along_ref, kind_ref, _, forcing_ref, cg_ref, turn_ref, mask_ref, *refs):
    refs = refs[1:] if into else refs
    home_ref = refs[0]
    sends = parts if chunk else 0
    cel_ref, kept_ref, trn_ref, first_ref, swap_ref = refs[sends + 1 :]
    dirs, rows, cols = forcing_ref.shape[1:]
    pitch = dirs + 1
    lanes = lane_tiles(cols)
    tiles = rows // TILE

    def span(t):
        return pl.ds(t * TILE, TILE)

    for t in range(tiles):
        levels = (cg_ref[0, span(t), :], turn_ref[0, span(t), :], mask_ref[span(t), :])
        coefficients(dirs, cel_ref, kept_ref, trn_ref, span(t), *levels)

    def turns_up(t, c):
        return turn_ref[0, span(t), lanes[c]] >= 4

    def store_first(t, d, c, value):
        first_ref[d, span(t), lanes[c]] = value

    def store_last(t, d, c, value):
        home_ref[0, d, span(t), lanes[c]] = value
        if chunk:
            swap_ref[c, pl.ds(t * TILE * pitch + d, TILE, stride=pitch), :] = value

    coefs = (cel_ref, kept_ref, trn_ref)
    step = functools.partial(sweep, dirs, tiles, False, lanes, sign_ref, along_ref, kind_ref, coefs, turns_up)
    step(lambda t, d, here: forcing_ref[0, d, span(t), here], store_first)
    step(lambda t, d, here: first_ref[d, span(t), here], store_last)
    if chunk:
        emit(own_ref[0], parts, local, chunk, dirs, lanes, swap_ref, refs[1 : sends + 1])


def inner(own, signs, along, after, forcing, cg, turn, mask, into, parts, chunk, group):
    freqs, dirs, rows, cols = forcing.shape
    begin, many = group
    local = rows // parts
    smem = pl.BlockSpec(memory_space=pltpu.SMEM)
    levels = pl.BlockSpec((1, rows, cols), lambda f: (begin + f, 0, 0))
    block = pl.BlockSpec((1, dirs, rows, cols), lambda f: (begin + f, 0, 0, 0))
    coefs = pltpu.VMEM((rows, cols), jnp.float32)
    sends = parts if chunk else 0
    count = chunk[2] if chunk else 0
    outs = pl.pallas_call(
        functools.partial(inner_kernel, parts, local, chunk, into is not None),
        grid=(many,),
        in_specs=[smem, smem, smem, smem, UNREAD, block, levels, levels, pl.BlockSpec((rows, cols), lambda f: (0, 0))]
        + ([] if into is None else [UNREAD]),
        out_specs=[block] + [pl.BlockSpec((count, 1, dirs, cols), lambda f: (0, f, 0, 0))] * sends,
        out_shape=[jax.ShapeDtypeStruct(forcing.shape, jnp.float32)]
        + [jax.ShapeDtypeStruct((count, many, dirs, cols), jnp.bfloat16)] * sends,
        scratch_shapes=[
            coefs,
            pltpu.VMEM((len(spreads(dirs)[0]), rows, cols), jnp.float32),
            coefs,
            pltpu.VMEM((dirs, rows, cols), jnp.float32),
            pltpu.VMEM((cols // LANES, rows * (dirs + 1), LANES), jnp.float32),
        ],
        input_output_aliases={} if into is None else {9: 0},
        compiler_params=pltpu.CompilerParams(vmem_limit_bytes=VMEM_LIMIT),
        cost_estimate=COST,
    )(own, signs, *along, after, forcing, cg, turn, mask, *([] if into is None else [into]))
    return outs[0], list(outs[1:])


def edges_kernel(_, *refs):
    swap_ref, edge_ref = refs[-2:]
    dirs, _, cols = refs[0].shape[1:]
    pitch = dirs + 1
    lanes = lane_tiles(cols)
    edge_ref[...] = jnp.zeros_like(edge_ref)
    for side, low in ((0, 0), (1, TILE - HALO)):
        forcing_ref, cg_ref, turn_ref, mask_ref = refs[4 * side : 4 * side + 4]
        out_ref = refs[8 + side]

        def body(d, carry, forcing_ref=forcing_ref):
            for c, here in enumerate(lanes):
                swap_ref[c, pl.ds(d, TILE, stride=pitch), :] = forcing_ref[0, d, :, here]
            return carry

        lax.fori_loop(0, dirs, body, 0, unroll=12)
        for r in range(HALO):
            for c, here in enumerate(lanes):
                edge_ref[:dirs, here] = swap_ref[c, pl.ds((low + r) * pitch, dirs), :]
            for n, level in enumerate((cg_ref[0], turn_ref[0], mask_ref[...])):
                edge_ref[dirs + n : dirs + n + 1, :] = level[low + r : low + r + 1].astype(jnp.float32)
            out_ref[r, 0] = edge_ref[...].astype(jnp.bfloat16)


def edges(after, forcing, cg, turn, mask):
    freqs, dirs, rows, cols = forcing.shape
    out = pl.BlockSpec((HALO, 1, dirs + TILE, cols), lambda f: (0, f, 0, 0))
    shape = jax.ShapeDtypeStruct((HALO, freqs, dirs + TILE, cols), jnp.bfloat16)
    in_specs = [UNREAD]
    for t in (0, rows // TILE - 1):
        in_specs += [
            pl.BlockSpec((1, dirs, TILE, cols), lambda f, t=t: (f, 0, t, 0)),
            pl.BlockSpec((1, TILE, cols), lambda f, t=t: (f, t, 0)),
            pl.BlockSpec((1, TILE, cols), lambda f, t=t: (f, t, 0)),
            pl.BlockSpec((TILE, cols), lambda f, t=t: (t, 0)),
        ]
    return pl.pallas_call(
        edges_kernel,
        grid=(freqs,),
        in_specs=in_specs,
        out_specs=[out, out],
        out_shape=[shape, shape],
        scratch_shapes=[
            pltpu.VMEM((cols // LANES, TILE * (dirs + 1), LANES), jnp.float32),
            pltpu.VMEM((dirs + TILE, cols), jnp.float32),
        ],
        compiler_params=pltpu.CompilerParams(vmem_limit_bytes=VMEM_LIMIT),
        cost_estimate=COST,
    )(after, *(2 * [forcing, cg, turn, mask]))


def outer_kernel(parts, local, chunk, *refs):
    own_ref, sign_ref, along_ref, kind_ref, _, above_ref, below_ref = refs[:7]
    cg_ref, turn_ref, mask_ref, home_ref, share_ref = refs[7:12]
    send_refs = refs[12 : 12 + parts]
    cel_ref, kept_ref, trn_ref, up_ref, lev_ref, near_ref, first_ref, side_ref, edge_ref, swap_ref = refs[12 + parts :]
    dirs, rows, cols = home_ref.shape[1:]
    freqs = share_ref.shape[0]
    pitch = dirs + 1
    lanes = lane_tiles(cols)
    tiles = rows // TILE
    f = pl.program_id(0)

    def span(t):
        return pl.ds(t * TILE, TILE)

    @pl.when(f == 0)
    def _():
        edge_ref[...] = jnp.zeros_like(edge_ref)
        beyond = ((above_ref, 0, 0), (above_ref, 1, 1), (below_ref, 0, TILE - HALO), (below_ref, 1, TILE - 1))
        for n in range(freqs):
            for i, (ref, r, low) in enumerate(beyond):
                for c, here in enumerate(lanes):
                    piece = ref[r, n, :, here].astype(jnp.float32)
                    edge_ref[c, pl.ds(low * pitch, dirs), :] = piece[:dirs]
                    lev_ref[i * TILE : (i + 1) * TILE, here] = piece[dirs:]

            def gather(d, carry, n=n):
                for c, here in enumerate(lanes):
                    side_ref[d, span(n), here] = edge_ref[c, pl.ds(d, TILE, stride=pitch), :]
                return carry

            lax.fori_loop(0, dirs, gather, 0, unroll=12)
            for q, mine in enumerate((cg_ref[n], turn_ref[n], mask_ref[...])):
                for i, (_, _, low) in enumerate(beyond):
                    near_ref[q * TILE + low : q * TILE + low + 1, :] = lev_ref[i * TILE + q : i * TILE + q + 1, :]
                near_ref[q * TILE + HALO : q * TILE + 2 * HALO, :] = mine[:HALO].astype(jnp.float32)
                near_ref[q * TILE + 2 * HALO : q * TILE + 3 * HALO, :] = mine[rows - HALO :].astype(jnp.float32)
            coefficients(dirs, cel_ref, kept_ref, trn_ref, span(n), *[near_ref[span(q), :] for q in range(3)])
            up_ref[span(n), :] = near_ref[span(1), :]

        def turns_up(t, c):
            return up_ref[span(t), lanes[c]] >= 4.0

        def store_first(t, d, c, value):
            first_ref[d, span(t), lanes[c]] = value

        def store_last(t, d, c, value):
            share_ref[t, d, :, lanes[c]] = value

        coefs = (cel_ref, kept_ref, trn_ref)
        step = functools.partial(sweep, dirs, freqs, True, lanes, sign_ref, along_ref, kind_ref, coefs, turns_up)
        step(lambda t, d, here: side_ref[d, span(t), here], store_first)
        step(lambda t, d, here: first_ref[d, span(t), here], store_last)

    def whole(d, carry):
        for t in range(tiles):
            for c, here in enumerate(lanes):
                value = with_share(home_ref[0, d, span(t), here], share_ref, f, d, here, t, tiles)
                swap_ref[c, pl.ds(t * TILE * pitch + d, TILE, stride=pitch), :] = value
        return carry

    lax.fori_loop(0, dirs, whole, 0, unroll=4)
    emit(own_ref[0], parts, local, chunk, dirs, lanes, swap_ref, send_refs)


def with_share(value, share_ref, f, d, here, t, tiles):
    row = lax.broadcasted_iota(jnp.int32, value.shape, 0)
    if t == 0:
        value = value + jnp.where(row < HALO, pltpu.roll(share_ref[f, d, :, here], TILE - HALO, 0), 0.0)
    if t == tiles - 1:
        value = value + jnp.where(row >= TILE - HALO, pltpu.roll(share_ref[f, d, :, here], HALO, 0), 0.0)
    return value


def outer(own, signs, along, after, above, below, cg, turn, mask, home, parts, chunk):
    freqs, dirs, rows, cols = home.shape
    local = rows // parts
    smem = pl.BlockSpec(memory_space=pltpu.SMEM)
    edge = pl.BlockSpec((HALO, freqs, dirs + TILE, cols), lambda f: (0, 0, 0, 0))
    levels = pl.BlockSpec((freqs, rows, cols), lambda f: (0, 0, 0))
    tall = pltpu.VMEM((freqs * TILE, cols), jnp.float32)
    outs = pl.pallas_call(
        functools.partial(outer_kernel, parts, local, chunk),
        grid=(freqs,),
        in_specs=[smem, smem, smem, smem, UNREAD, edge, edge, levels, levels]
        + [pl.BlockSpec((rows, cols), lambda f: (0, 0)), pl.BlockSpec((1, dirs, rows, cols), lambda f: (f, 0, 0, 0))],
        out_specs=[pl.BlockSpec((freqs, dirs, TILE, cols), lambda f: (0, 0, 0, 0))]
        + [pl.BlockSpec((chunk[2], 1, dirs, cols), lambda f: (0, f, 0, 0))] * parts,
        out_shape=[jax.ShapeDtypeStruct((freqs, dirs, TILE, cols), jnp.float32)]
        + [jax.ShapeDtypeStruct((chunk[2], freqs, dirs, cols), jnp.bfloat16)] * parts,
        scratch_shapes=[
            tall,
            pltpu.VMEM((len(spreads(dirs)[0]), freqs * TILE, cols), jnp.float32),
            tall,
            tall,
            pltpu.VMEM((2 * HALO * TILE, cols), jnp.float32),
            pltpu.VMEM((3 * TILE, cols), jnp.float32),
            pltpu.VMEM((dirs, freqs * TILE, cols), jnp.float32),
            pltpu.VMEM((dirs, freqs * TILE, cols), jnp.float32),
            pltpu.VMEM((cols // LANES, TILE * (dirs + 1), LANES), jnp.float32),
            pltpu.VMEM((cols // LANES, rows * (dirs + 1), LANES), jnp.float32),
        ],
        compiler_params=pltpu.CompilerParams(vmem_limit_bytes=VMEM_LIMIT),
        cost_estimate=LONG,
    )(own, signs, *along, after, above, below, cg, turn, mask, home)
    return outs[0], list(outs[1:])


def by_row_kernel(*refs):
    state_ref, out_ref, swap_ref = refs[-3:]
    some, local, cols = state_ref.shape
    pitch = some + 1
    lanes = lane_tiles(cols)

    def body(d, carry):
        for c, here in enumerate(lanes):
            swap_ref[c, pl.ds(d, local, stride=pitch), :] = state_ref[d, :, here].astype(jnp.float32)
        return carry

    lax.fori_loop(0, some, body, 0, unroll=8)
    for r in range(local):
        for c, here in enumerate(lanes):
            out_ref[r, :, here] = swap_ref[c, pl.ds(r * pitch, some), :].astype(jnp.bfloat16)


def by_row(after, state):
    deep, local, cols = state.shape
    some = 48
    return pl.pallas_call(
        by_row_kernel,
        grid=(deep // some,),
        in_specs=[UNREAD] * len(after) + [pl.BlockSpec((some, local, cols), lambda d: (d, 0, 0))],
        out_specs=pl.BlockSpec((local, some, cols), lambda d: (0, d, 0)),
        out_shape=jax.ShapeDtypeStruct((local, deep, cols), jnp.bfloat16),
        scratch_shapes=[pltpu.VMEM((cols // LANES, local * (some + 1), LANES), jnp.float32)],
        compiler_params=pltpu.CompilerParams(vmem_limit_bytes=VMEM_LIMIT),
        cost_estimate=COST,
    )(*after, state)


def turned_kernel(_, w_in_ref, w_out_ref, weight_ref, in_t_ref, out_t_ref, column_ref):
    in_t_ref[...] = w_in_ref[...].T
    out_t_ref[...] = w_out_ref[...].T

    @pl.when(pl.program_id(0) == 0)
    def _():
        column_ref[...] = jnp.broadcast_to(weight_ref[...][None, :], (LANES, weight_ref.shape[0])).T


def turned(after, w_in, w_out, weight):
    hidden, total = w_in.shape
    step = 512
    tall = pl.BlockSpec((step, total), lambda h: (h, 0))
    wide = pl.BlockSpec((total, step), lambda h: (0, h))
    return pl.pallas_call(
        turned_kernel,
        grid=(hidden // step,),
        in_specs=[UNREAD, tall, wide, pl.BlockSpec(memory_space=pltpu.VMEM)],
        out_specs=[wide, tall, pl.BlockSpec((hidden, LANES), lambda h: (0, 0))],
        out_shape=[
            jax.ShapeDtypeStruct((total, hidden), w_in.dtype),
            jax.ShapeDtypeStruct((hidden, total), w_in.dtype),
            jax.ShapeDtypeStruct((hidden, LANES), jnp.float32),
        ],
        compiler_params=pltpu.CompilerParams(vmem_limit_bytes=VMEM_LIMIT),
        cost_estimate=LONG,
    )(after, w_in, w_out, weight)


def source_kernel(parts, got, sent, dirs, step, first, chunk, own_ref, _, state_ref, wind_ref, w_in_ref, out_t_ref, in_t_ref, weight_ref, *refs):
    cell_refs = refs[: parts * len(got)]
    grad_ref = refs[parts * len(got)]
    back_refs = refs[parts * len(got) + 1 : -3]
    cell_ref, weighted_ref, grown_ref = refs[-3:]
    freqs = sum(many for _, many in got)
    hidden, width = weighted_ref.shape
    own = own_ref[0]

    def place(k, group):
        begin, many = group
        return pl.ds(pl.multiple_of(((own ^ k) * freqs + begin) * dirs, TILE), many * dirs)

    for g, group in enumerate(got):
        for k in range(parts):
            piece = cell_refs[g * parts + k][0].astype(jnp.float32)
            cell_ref[place(k, group), :] = piece.reshape(group[1] * dirs, width)
    cell = cell_ref[...].astype(jnp.bfloat16)
    state = state_ref[0]
    wind = wind_ref[pl.ds(chunk_row(own, first + pl.program_id(0), chunk), 1), :]
    grad = jnp.zeros((TILE, width), jnp.float32)
    for h in range(0, hidden, step):
        some = pl.ds(h, step)
        weight = weight_ref[some, :1]
        forward = jnp.dot(w_in_ref[some, :], state, preferred_element_type=jnp.float32) + weight * wind
        squash = jnp.tanh(forward)
        pulled = jnp.dot(out_t_ref[some, :], cell, preferred_element_type=jnp.float32)
        weighted = (1.0 - squash * squash) * pulled
        weighted_ref[some, :] = weighted.astype(jnp.bfloat16)
        grad = grad + jnp.sum((weight * weighted).reshape(step // TILE, TILE, width), axis=0)
    grad_ref[0] = jnp.sum(grad, axis=0, keepdims=True)
    grown_ref[...] = jnp.dot(in_t_ref[...], weighted_ref[...], preferred_element_type=jnp.float32)
    for g, group in enumerate(sent):
        for k in range(parts):
            grown = grown_ref[place(k, group), :].reshape(group[1], dirs, width)
            back_refs[g * parts + k][0] = grown.astype(jnp.bfloat16)


def source_term(own, after, state, wind, w_in, out_t, in_t, weight, cells, got, sent, rows, chunk):
    parts = len(cells[0])
    _, _, dirs, cols = cells[0][0].shape
    first, count = rows
    hidden, total = w_in.shape
    width = min(cols, 512)

    def row_of(j, own_ref):
        return chunk_row(own_ref[0], first + j, chunk)

    def whole(shape):
        return pl.BlockSpec(shape, lambda j, c, own_ref: (0, 0))

    cell_specs = [
        pl.BlockSpec((1, many, dirs, width), lambda j, c, own_ref: (first + j, 0, 0, c)) for _, many in got for _ in range(parts)
    ]
    back_specs = [pl.BlockSpec((1, many, dirs, width), lambda j, c, own_ref: (j, 0, 0, c)) for _, many in sent for _ in range(parts)]
    outs = pl.pallas_call(
        functools.partial(source_kernel, parts, got, sent, dirs, 256, first, chunk),
        grid_spec=pltpu.PrefetchScalarGridSpec(
            num_scalar_prefetch=1,
            grid=(count, cols // width),
            in_specs=[
                UNREAD,
                pl.BlockSpec((1, total, width), lambda j, c, own_ref: (row_of(j, own_ref), 0, c)),
                pl.BlockSpec((wind.shape[0], width), lambda j, c, own_ref: (0, c)),
                whole((hidden, total)),
                whole((hidden, total)),
                whole((total, hidden)),
                whole((hidden, LANES)),
            ]
            + cell_specs,
            out_specs=[pl.BlockSpec((1, 1, width), lambda j, c, own_ref: (j, 0, c))] + back_specs,
            scratch_shapes=[
                pltpu.VMEM((total, width), jnp.float32),
                pltpu.VMEM((hidden, width), jnp.bfloat16),
                pltpu.VMEM((total, width), jnp.float32),
            ],
        ),
        out_shape=[jax.ShapeDtypeStruct((count, 1, cols), jnp.float32)]
        + [jax.ShapeDtypeStruct((count, many, dirs, cols), jnp.bfloat16) for _, many in sent for _ in range(parts)],
        compiler_params=pltpu.CompilerParams(vmem_limit_bytes=VMEM_LIMIT),
        cost_estimate=COST,
    )(own, after, state, wind, w_in, out_t, in_t, weight, *[cell for group in cells for cell in group])
    return outs[0], [list(outs[1 + g * parts : 1 + (g + 1) * parts]) for g in range(len(sent))]


def join_kernel(parts, spans, own_ref, _, home_ref, share_ref, *refs):
    out_ref, swap_ref = refs[-2:]
    dirs, rows, cols = home_ref.shape[1:]
    pitch = dirs + 1
    local = rows // parts
    own = own_ref[0]
    lanes = lane_tiles(cols)
    tiles = rows // TILE
    for i, (first, count, chunk) in enumerate(spans):
        for k in range(parts):
            owner = own ^ k
            for j in range(count):
                start = (owner * local + chunk_row(owner, first + j, chunk)) * pitch
                for c, here in enumerate(lanes):
                    swap_ref[c, pl.ds(start, dirs), :] = refs[i * parts + k][j, 0, :, here].astype(jnp.float32)

    def body(d, carry):
        for t in range(tiles):
            for c, here in enumerate(lanes):
                grown = swap_ref[c, pl.ds(t * TILE * pitch + d, TILE, stride=pitch), :]
                value = with_share(home_ref[0, d, pl.ds(t * TILE, TILE), here], share_ref, 0, d, here, t, tiles)
                out_ref[0, d, pl.ds(t * TILE, TILE), here] = value + grown
        return carry

    lax.fori_loop(0, dirs, body, 0, unroll=2)


def join(own, into, home, share, early, late, rows_of, chunks, group):
    begin, many = group
    parts = len(late)
    _, dirs, rows, cols = home.shape
    last = late[0].shape[0]
    spans = [(*span, chunks[0]) for span in rows_of] + [(0, last, chunks[-1])]
    block = pl.BlockSpec((1, dirs, rows, cols), lambda f: (begin + f, 0, 0, 0))
    specs = [
        pl.BlockSpec((count, 1, dirs, cols), lambda f: (0, begin + f, 0, 0)) for _, count in rows_of for _ in range(parts)
    ] + [pl.BlockSpec((last, 1, dirs, cols), lambda f: (0, f, 0, 0))] * parts
    return pl.pallas_call(
        functools.partial(join_kernel, parts, spans),
        grid=(many,),
        in_specs=[pl.BlockSpec(memory_space=pltpu.SMEM), UNREAD, block]
        + [pl.BlockSpec((1, dirs, TILE, cols), lambda f: (begin + f, 0, 0, 0))]
        + specs,
        out_specs=block,
        out_shape=jax.ShapeDtypeStruct(home.shape, jnp.float32),
        scratch_shapes=[pltpu.VMEM((cols // LANES, rows * (dirs + 1), LANES), jnp.float32)],
        input_output_aliases={} if begin == 0 else {1: 0},
        compiler_params=pltpu.CompilerParams(vmem_limit_bytes=VMEM_LIMIT),
        cost_estimate=COST,
    )(own, into, home, share, *[piece for pieces in early for piece in pieces], *late)


def arrived_kernel(held, *refs):
    refs[-1][...] = jnp.zeros_like(refs[-1])


def arrived(after, pieces, held=()):
    outs = pl.pallas_call(
        functools.partial(arrived_kernel, len(held)),
        in_specs=[UNREAD] * (1 + len(pieces) + len(held)),
        out_specs=[UNREAD] * len(held) + [pl.BlockSpec(memory_space=pltpu.VMEM)],
        out_shape=[jax.ShapeDtypeStruct(h.shape, h.dtype) for h in held] + [jax.ShapeDtypeStruct((TILE, LANES), jnp.float32)],
        input_output_aliases={1 + len(pieces) + i: i for i in range(len(held))},
        cost_estimate=COST,
    )(after, *pieces, *held)
    return outs[-1], list(outs[:-1])


def swapped(pieces):
    parts = len(pieces)
    moved = {k: lax.ppermute(pieces[k], "comp", [(i, i ^ k) for i in range(parts)]) for k in range(parts - 1, 0, -1)}
    return [pieces[0]] + [moved[k] for k in range(1, parts)]


def across(low, high):
    count = lax.axis_size("space")
    up = [(i, i + 1) for i in range(count - 1)]
    down = [(i + 1, i) for i in range(count - 1)]
    return lax.ppermute(high, "space", up), lax.ppermute(low, "space", down)


def shards(
    adjoint_forcing,
    forward_state,
    wind_speed,
    cg_index,
    turn_index,
    sea_mask,
    dir_sign,
    w_in,
    w_out,
    wind_weight,
):
    parts = lax.axis_size("comp")
    own_place = lax.axis_index("comp")
    own = own_place.astype(jnp.int32).reshape(1)
    dirs = dir_sign.shape[1]
    comps, rows, cols = adjoint_forcing.shape
    freqs = comps // dirs
    local = rows // parts
    along = (jnp.asarray(direction_factors(dirs)), jnp.asarray(spreads(dirs)[1]))
    forcing = adjoint_forcing.reshape(freqs, dirs, rows, cols)
    everything = [(0, freqs)]
    many = freqs // 2 if freqs % 2 == 0 else freqs
    groups = [(begin, many) for begin in range(0, freqs, many)]
    sent = groups
    levels = (cg_index, turn_index, sea_mask)
    if local > HALO:
        chunks = [(HALO, 0, local - HALO), (0, local - HALO, HALO)]
    else:
        chunks = [(0, 0, local)]
    ahead = chunks[0] if len(chunks) > 1 else None

    early, home, after = [], None, sea_mask
    for g, group in enumerate(groups):
        home, pieces = inner(own, dir_sign, along, after, forcing, *levels, home, parts, ahead, group)
        if ahead:
            early.append(swapped(pieces))
        if g == 0:
            low, high = edges(pieces[-1] if ahead else home, forcing, *levels)
            after = high
    above, below = across(low, high)
    after = home
    for pieces in early[:-1]:
        after, _ = arrived(after, pieces[:0:-1])
    state = by_row((after,), forward_state)
    share, pieces = outer(own, dir_sign, along, state, above, below, *levels, home, parts, chunks[-1])
    late = swapped(pieces)
    in_t, out_t, weight = turned(share, w_in, w_out, wind_weight)
    term = functools.partial(source_term, own)
    fixed = (state, wind_speed, w_in, out_t, in_t, weight)
    after, grads, early_back, rows_of = in_t, [], [], []
    if ahead:
        count = ahead[2]
        some = 2 if count % 2 == 0 else 1
        rows_of = [(first, some) for first in range(0, count, some)]
    for n, span in enumerate(rows_of):
        if n == 1:
            after, _ = arrived(after, late[-1:])
        if n > 1:
            after, _ = arrived(after, early_back[n - 2][1:2])
        grad, [back] = term(after, *fixed, early, groups, everything, span, ahead)
        after = grad
        if not grads:
            after, rest = arrived(grad, late[1:-1] if len(rows_of) > 1 else late[1:], back[1:])
            back = [back[0], *rest]
        grads.append(grad)
        early_back.append(swapped(back))
    late_grad, late_back = term(after, *fixed, [late], everything, sent, (0, chunks[-1][2]), chunks[-1])
    start = late_grad
    if early_back:
        start, rest = arrived(start, early_back[0][1:], [piece for pieces in late_back for piece in pieces[1:]])
        step = parts - 1
        late_back = [[pieces[0], *rest[g * step : (g + 1) * step]] for g, pieces in enumerate(late_back)]
    late_back = [swapped(pieces) for pieces in late_back]
    if early_back:
        start, _ = arrived(start, early_back[-1][1:])
    for group, back in zip(sent, late_back, strict=True):
        start = join(own, start, home, share, early_back, back, rows_of, chunks, group)
    gradient = jnp.where(
        own_place == 0, jnp.concatenate([late_grad, *grads], axis=0), jnp.concatenate([*grads, late_grad], axis=0)
    )
    return (start.reshape(comps, rows, cols), gradient.reshape(wind_speed.shape))


def solution(mesh):
    placed = (
        P("comp", "space", None),
        P(None, ("space", "comp"), None),
        P(("space", "comp"), None),
        P("comp", "space", None),
        P("comp", "space", None),
        P("space", None),
        P(),
        P(),
        P(),
        P(),
    )
    return jax.shard_map(
        shards,
        mesh=mesh,
        in_specs=placed,
        out_specs=(P("comp", "space", None), P(("space", "comp"), None)),
        check_vma=False,
    )
```
